512 devices in a mesh: dp: 4 (over x), width: 16 (over z, core), mlp: 8 (over y).
Axes of the slice: x: 4, y: 8, z: 8, core: 2. Of those that a mesh axis runs over, the one named last changes fastest.
Arguments:
- tokens: bfloat16 [512, 6144], P('dp', 'width'), may hold values from -34 to 34
- gain: float32 [6144], P('width'), may hold values from 0.5 to 1.5
- up_weight: bfloat16 [6144, 12288], P('width', 'mlp'), may hold values from -0.078125 to 0.078125
- down_weight: bfloat16 [12288, 6144], P('mlp', 'width'), may hold values from -0.0546875 to 0.0546875
- cotangent: bfloat16 [512, 6144], P('dp', 'width'), may hold values from -6 to 6
Outputs:
- output: bfloat16 [512, 6144], P('dp', 'width')
- grad_tokens: bfloat16 [512, 6144], P('dp', 'width')
- grad_gain: float32 [6144], P('width')
- grad_up: float32 [6144, 8, 1536], P('width', 'mlp', 'dp')
- grad_down: float32 [8, 1536, 6144], P('mlp', 'dp', 'width')
The draws below stay inside these ranges and needn't reach their ends.
All inputs are finite; a program needn't handle non-finite values.
Results may differ from the reference program's by a relative error of at most 0.025.
Values may be sent and summed in bfloat16 or wider, within the bound.
A program may use at most 64 MiB of HBM per device.

```python
import math
import jax
import jax.numpy as jnp
from jax import lax

D = 6144
FF = 12288
TOK_DEV = 128
TOKENS = 512
N_DP = 4
N_WIDTH = 16
N_MLP = 8


def draw_tokens(key, part):
    key = jax.random.fold_in(key, 11)
    keys = jax.random.split(key, 4)
    position = jnp.arange(D, dtype=jnp.float32) / (D - 1)
    column_scale = jnp.exp(math.log(3.0) * position) * jax.random.uniform(keys[0], (D,), jnp.float32, 1.0, 3.0)
    row_scale = jnp.exp(jax.random.uniform(keys[1], (TOKENS, 1), jnp.float32, math.log(0.3), math.log(3.0)))
    offset = jax.random.uniform(keys[2], (D,), jnp.float32, -1.0, 1.0)
    base = jnp.clip(jax.random.normal(keys[3], (TOKENS, D), jnp.float32), -4.0, 4.0)
    values = 0.25 * (base + offset[None, :]) * column_scale[None, :] * row_scale
    return values.astype(jnp.bfloat16)


def block_scale(stream_key, shape, cuts, smallest, largest):
    factor_of, own = 1.0, jax.random.fold_in(stream_key, 6)
    for dim, parts in cuts:
        steps = jnp.exp(jax.random.uniform(jax.random.fold_in(own, dim), (parts,), jnp.float32, smallest / len(cuts), largest / len(cuts)))
        factor_of = factor_of * jnp.repeat(steps, shape[dim] // parts).reshape([-1 if axis == dim else 1 for axis in range(len(shape))])
    return factor_of


def noise(key, dims, spread, most, cuts=(), held_as=jnp.bfloat16):
    drawn = jax.random.normal(key, dims, jnp.float32) * spread
    if len(cuts) > 0:
        drawn = block_scale(key, dims, cuts, -0.22, 0.18) * drawn
    return jnp.clip(drawn, min=-most, max=most).astype(held_as)


def setup_inputs(seed: int = 0) -> dict:
    key_of = jax.random.split(jax.random.key(seed), 6)
    tokens = draw_tokens(jax.random.fold_in(key_of[5], 71), 0)
    gain = jnp.clip(0.5 + 1.0 * jax.random.uniform(key_of[1], (D,), jnp.float32) ** block_scale(key_of[1], (D,), ((0, 16),), -0.2, 0.2), 0.5, 1.5)
    up_weight = noise(key_of[2], (D, FF), D ** -0.5, 0.078125, ((0, 16), (1, 8)))
    down_weight = noise(key_of[3], (FF, D), FF ** -0.5, 0.0546875, ((0, 8), (1, 16)))
    cotangent = noise(key_of[4], (TOKENS, D), 1.0, 6.0, ((0, 4), (1, 16)))
    return {"tokens": tokens, "gain": gain, "up_weight": up_weight, "down_weight": down_weight, "cotangent": cotangent}


inv_root_two = 0.7071067811865476
inv_root_two_pi = 0.3989422804014327

def gelu_value(values):
    return 0.5 * values * (1.0 + lax.erf(values * inv_root_two))

def gelu_slope(values):
    return 0.5 * (1.0 + lax.erf(values * inv_root_two)) + values * jnp.exp(-0.5 * values * values) * inv_root_two_pi

def blocked_sum(left, right, contract_right):
    block = D // N_WIDTH

    def one_block(total, shard):
        first = shard * block
        left_block = lax.dynamic_slice_in_dim(left, first, block, 1)
        right_block = lax.dynamic_slice_in_dim(right, first, block, contract_right)
        term = lax.dot_general(left_block, right_block, (((1,), (contract_right,)), ((), ())), preferred_element_type=jnp.float32)
        rounded = lax.optimization_barrier(term.astype(jnp.bfloat16))
        return (total + rounded.astype(jnp.float32), None)
    other = right.shape[1 - contract_right]
    start = jnp.zeros((left.shape[0], other), jnp.float32)
    total, _ = lax.scan(one_block, start, jnp.arange(N_WIDTH, dtype=jnp.int32))
    return total

def reference(tokens, gain, up_weight, down_weight, cotangent):
    inputs = tokens.astype(jnp.float32)
    mean = lax.optimization_barrier(jnp.mean(inputs, axis=1, keepdims=True))
    centered = inputs - mean
    inv_std = lax.rsqrt(lax.optimization_barrier(jnp.mean(centered * centered, axis=1, keepdims=True)) + 1e-06)
    normed = centered * inv_std
    scaled = (normed * gain[None, :]).astype(jnp.bfloat16)
    pre_act = blocked_sum(scaled, up_weight, 0)
    hidden = gelu_value(pre_act).astype(jnp.bfloat16)
    output = jnp.dot(hidden, down_weight, preferred_element_type=jnp.float32).astype(jnp.bfloat16)
    grad_hidden = blocked_sum(cotangent, down_weight, 1)
    grad_pre = (grad_hidden * gelu_slope(pre_act)).astype(jnp.bfloat16)
    grad_scaled = lax.dot_general(grad_pre, up_weight, (((1,), (1,)), ((), ())), preferred_element_type=jnp.float32)
    grad_normed = grad_scaled * gain[None, :]
    first_mean = lax.optimization_barrier(jnp.mean(grad_normed, axis=1, keepdims=True))
    second_mean = lax.optimization_barrier(jnp.mean(grad_normed * normed, axis=1, keepdims=True))
    grad_tokens = (inv_std * (grad_normed - first_mean - normed * second_mean)).astype(jnp.bfloat16)
    grad_gain = lax.optimization_barrier(jnp.sum(grad_scaled * normed, axis=0))
    up_total = jnp.zeros((D, FF), jnp.float32)
    down_total = jnp.zeros((FF, D), jnp.float32)
    for group in range(N_DP):
        rows = slice(group * TOK_DEV, (group + 1) * TOK_DEV)
        up_term = lax.dot_general(scaled[rows], grad_pre[rows], (((0,), (0,)), ((), ())), preferred_element_type=jnp.float32)
        down_term = lax.dot_general(hidden[rows], cotangent[rows], (((0,), (0,)), ((), ())), preferred_element_type=jnp.float32)
        up_total = up_total + lax.optimization_barrier(up_term.astype(jnp.bfloat16)).astype(jnp.float32)
        down_total = down_total + lax.optimization_barrier(down_term.astype(jnp.bfloat16)).astype(jnp.float32)
    grad_up = up_total.reshape(D, N_MLP, FF // N_MLP)
    grad_down = down_total.reshape(N_MLP, FF // N_MLP, D)
    return (output, grad_tokens, grad_gain, grad_up, grad_down)
```

```python
import functools

import jax
import jax.numpy as jnp
from jax import lax
from jax.experimental import pallas as pl
from jax.experimental.pallas import tpu as pltpu
from jax.sharding import PartitionSpec as P

MESH = pl.DeviceIdType.MESH
F32, BF16 = jnp.float32, jnp.bfloat16
TB = 16
EXTRA = 128

inv_root_two = 0.7071067811865476
inv_root_two_pi = 0.3989422804014327


def dot(left, right, left_dim, right_dim):
    return lax.dot_general(
        left, right, (((left_dim,), (right_dim,)), ((), ())), preferred_element_type=F32
    )


def pack(first, second):
    lane = lax.broadcasted_iota(jnp.int32, (first.shape[0], EXTRA), 1)
    high_one, high_two = first.astype(BF16).astype(F32), second.astype(BF16).astype(F32)
    held = jnp.where(lane == 0, high_one, 0.0)
    held = jnp.where(lane == 1, high_two, held)
    held = jnp.where(lane == 2, first - high_one, held)
    held = jnp.where(lane == 3, second - high_two, held)
    return held.astype(BF16)


def unpack(held):
    return held[:, 0:1] + held[:, 2:3], held[:, 1:2] + held[:, 3:4]


def send(src, dst, ss, rs, **where):
    pltpu.make_async_remote_copy(
        src_ref=src, dst_ref=dst, send_sem=ss, recv_sem=rs, device_id=where, device_id_type=MESH
    ).start()


def arrived(ref, sem):
    pltpu.make_async_copy(ref, ref, sem).wait()


def ring(axis, me, device=lambda position: position):
    def at(o):
        return lax.rem(me + o % 8, 8)
    return at, lambda o: {axis: device(at(o))}


def lanes_of(block, side):
    cut = block.shape[-1] // 256 * 128
    return block.at[:, pl.ds(0, cut) if side == 0 else pl.ds(cut, block.shape[-1] - cut)]


def scatter(to_whom, terms, got, halves, ss, rs):
    at, to = to_whom
    for side, o in ((0, 1), (1, -1)):
        send(terms.at[at(3 * o)], got.at[4 + side], ss, rs.at[4 + side], **to(o))
    for side, o in ((0, 2), (1, -2)):
        send(lanes_of(terms.at[at(4)], side), halves[side], ss, rs.at[6 + side], **to(o))
    for side, o in ((0, 1), (1, -1)):
        send(terms.at[at(o)], got.at[side], ss, rs.at[side], **to(o))


def scatter_pass(to_whom, own, got, halves, sums, ss, rs):
    at, to = to_whom
    for side, o in ((0, 2), (1, -2)):
        arrived(got.at[4 + side], rs.at[4 + side])
        arrived(halves[side], rs.at[6 + side])
        term = own[at(o)] + got[4 + side].astype(F32)
        half = halves[side][...].astype(F32)
        cut = term.shape[-1] // 256 * 128
        low, high = term[:, 0:cut], term[:, cut:]
        sums[side, :, 0:cut] = (low + half if side == 0 else low).astype(BF16)
        sums[side, :, cut:] = (high if side == 0 else high + half).astype(BF16)
        send(sums.at[side], got.at[2 + side], ss, rs.at[2 + side], **to(o))


def scatter_sum(to_whom, own, got, rs):
    at, _ = to_whom
    for slot in range(4):
        arrived(got.at[slot], rs.at[slot])
    return own[at(0)] + jnp.sum(got[0:4].astype(F32), axis=0)


def gather(to_whom, buf, ss, rs):
    at, to = to_whom
    block = buf.at[at(0)]
    for o, slot in ((2, 2), (-2, 3), (1, 0), (-1, 1)):
        send(block, block, ss, rs.at[slot], **to(o))


def gather_pass(here, there, buf, ss, rs, far_rs, use):
    at, _ = here
    for side, o in ((0, 1), (1, -1)):
        block = buf.at[at(-2 * o)]
        arrived(block, rs.at[2 + side])
        half = lanes_of(block, side)
        for (_, to), sems, first in ((here, rs, 4), (there, far_rs, 0)):
            send(block, block, ss, sems.at[first + side], **to(o))
            send(half, half, ss, sems.at[first + 2 + side], **to(2 * o))
        use(block)


def gather_near(here, buf, rs, use):
    at, _ = here
    for side, o in ((0, -1), (1, 1)):
        arrived(buf.at[at(o)], rs.at[side])
        use(buf.at[at(o)])


def gather_far(here, buf, sems, first):
    at, _ = here
    for side, o in ((0, -3), (1, 3)):
        arrived(buf.at[at(o)], sems.at[first + side])
        arrived(lanes_of(buf.at[at(4)], side), sems.at[first + 2 + side])


def around(i, n):
    half = lax.div(n - 2 - i, 2) + 1
    return jnp.where(lax.rem(n - 2 - i, 2) == 0, half, n - half)


def direct_scatter(axis, me, n, terms, got, ss, rs):
    def one(i, carry):
        o = around(i, n)
        peer = lax.rem(me + o, n)
        send(terms.at[peer], got.at[o - 1], ss, rs, **{axis: peer})
        return carry
    lax.fori_loop(0, n - 1, one, 0)


def direct_gather(axis, me, n, buf, ss, rs):
    def one(i, carry):
        send(buf.at[me], buf.at[me], ss, rs, **{axis: lax.rem(me + around(i, n), n)})
        return carry
    lax.fori_loop(0, n - 1, one, 0)


def kernel(
    sizes, tok_h, gain_h, wup_h, wdn_h, cot_h, out, gt, gg, gup, gdn,
    tok, gain_v, wup, wdn, cotx, scx, normed, inv_col,
    stat_s, stat_r,
    sib_s, sib_r, own, zs, zr, zh, zc, leaning, away_col,
    hid, gp, hx, gpx,
    ys0, yr0, part0, ys1, yr1, part1,
    outv, gtv,
    gg_s, ggx_r, ggy_s, ggy_r,
    ld, sib_ss, sib_rs, stat_ss, stat_rs, z_ss, z_rs, ag_ss, ag_rs, far_rs, rel_ss, rel_rs,
    x_ss, x_rs, q_ss, q_rs, join_ss, join_rs, y_ss, y_rs, yag_ss, yag_rs, ggx_ss, ggx_rs, ggy_ss, ggy_rs,
):
    NX, NZ, NY, D = sizes
    T, DS = tok.shape
    TY = T // NY
    FS = wup.shape[1]
    FH, FQ = FS // 2, FS // NX
    NW = 2 * NZ
    x, w, y = lax.axis_index("dp"), lax.axis_index("width"), lax.axis_index("mlp")
    z = lax.div(w, 2)
    c = w - 2 * z
    sibling = 2 * z + 1 - c

    over_z = ring("width", z, lambda position: 2 * position + c)
    across_z = ring("width", z, lambda position: 2 * position + 1 - c)

    def quarter(q):
        first = q * FQ
        h = lax.div(first, FH)
        return h, pl.ds(pl.multiple_of(first - h * FH, FQ), FQ)

    loads = [
        pltpu.make_async_copy(tok_h, tok, ld.at[0]),
        pltpu.make_async_copy(gain_h, gain_v, ld.at[1]),
        pltpu.make_async_copy(wup_h, wup, ld.at[2]),
        pltpu.make_async_copy(cot_h, cotx.at[0], ld.at[3]),
        pltpu.make_async_copy(wdn_h, wdn, ld.at[4]),
    ]
    for load in loads:
        load.start()

    barrier = pltpu.get_barrier_semaphore()

    def greet(axis, me, n):
        def one(k, carry):
            pl.semaphore_signal(barrier, inc=1, device_id={axis: lax.rem(me + k, n)}, device_id_type=MESH)
            return carry
        lax.fori_loop(1, n, one, 0)

    greet("width", w, NW)
    greet("mlp", y, NY)
    greet("dp", x, NX)

    mine = pl.ds(pl.multiple_of(c * FH, FH), FH)
    other = pl.ds(pl.multiple_of(FH - c * FH, FH), FH)

    loads[0].wait()
    loads[1].wait()
    values = tok[...].astype(F32)
    total = jnp.sum(values, axis=1, keepdims=True)
    shifted = values - total * (1.0 / DS)
    spread = jnp.sum(shifted * shifted, axis=1, keepdims=True)
    g_all = gain_v[...].reshape(1, DS)
    leaning[0:T] = (shifted * g_all).astype(BF16)
    row = lax.broadcasted_iota(jnp.int32, (TB, DS), 0)
    g_one = g_all.astype(BF16).astype(F32)
    g_two = (g_all - g_one).astype(BF16).astype(F32)
    g_rows = jnp.where(row == 0, g_one, jnp.where(row == 1, g_two, jnp.where(row == 2, g_all - g_one - g_two, 0.0)))
    leaning[T:] = g_rows.astype(BF16)
    loads[2].wait()
    its_half = dot(leaning[...], wup[:, other], 1, 0)
    sib_s[0] = its_half[0:T].astype(BF16)
    pl.semaphore_wait(barrier, NW - 1 + NY - 1 + NX - 1)
    send(sib_s.at[0], sib_r.at[0], sib_ss.at[0], sib_rs.at[0], width=sibling)

    loads[3].wait()
    loads[4].wait()
    sib_s[1] = dot(cotx[0], wdn[other, :], 1, 1).astype(BF16)
    send(sib_s.at[1], sib_r.at[1], sib_ss.at[1], sib_rs.at[1], width=sibling)

    def merge(k, mine_half):
        arrived(sib_r.at[k], sib_rs.at[k])
        both = (mine_half + sib_r[k].astype(F32)).reshape(NZ, TB, FH)
        own[k] = both
        zs[k] = both.astype(BF16)
        scatter(over_z, zs.at[k], zr.at[k], [zh.at[k, 0], zh.at[k, 1]], z_ss.at[k], z_rs.at[k])

    def merge_pass(k):
        scatter_pass(
            over_z, own.at[k], zr.at[k], [zh.at[k, 0], zh.at[k, 1]], zc.at[k], z_ss.at[k], z_rs.at[k]
        )

    my_half = dot(leaning[...], wup[:, mine], 1, 0)
    merge(0, my_half[0:T])
    merge(1, dot(cotx[0], wdn[mine, :], 1, 1))

    total_row = jnp.transpose(jnp.broadcast_to(total, (T, EXTRA)))[0:1]
    spread_row = jnp.transpose(jnp.broadcast_to(spread, (T, EXTRA)))[0:1]
    for h, half in ((c, my_half), (1 - c, its_half)):
        lean = jnp.sum(half[T:], axis=0, keepdims=True)
        stat_s[h, 0:1, 0:T] = total_row
        stat_s[h, 1:2, 0:T] = spread_row
        for j in range(FH // 128):
            stat_s[h, 2 + j : 3 + j, :] = lean[:, j * 128 : (j + 1) * 128]

    def tell(k, carry):
        peer = lax.rem(w + k, NW)
        send(stat_s.at[lax.rem(peer, 2)], stat_r.at[k - 1], stat_ss, stat_rs, width=peer)
        return carry
    lax.fori_loop(1, NW, tell, 0)

    right, left = lax.rem(x + 1, NX), lax.rem(x + NX - 1, NX)
    first_rows, last_rows = pl.ds(0, T // 2), pl.ds(T // 2, T // 2)

    def spread_x(k, buf):
        send(buf.at[0], buf.at[1], x_ss.at[k], x_rs.at[k, 0], dp=right)
        send(buf.at[0], buf.at[NX - 1], x_ss.at[k], x_rs.at[k, 1], dp=left)

    def pass_x(k, buf):
        arrived(buf.at[1], x_rs.at[k, 0])
        send(buf.at[1, first_rows], buf.at[2, first_rows], x_ss.at[k], x_rs.at[k, 2], dp=right)
        arrived(buf.at[NX - 1], x_rs.at[k, 1])
        send(buf.at[NX - 1, last_rows], buf.at[2, last_rows], x_ss.at[k], x_rs.at[k, 3], dp=left)

    def end_x(k, buf):
        arrived(buf.at[2, first_rows], x_rs.at[k, 2])
        arrived(buf.at[2, last_rows], x_rs.at[k, 3])

    merge_pass(0)
    merge_pass(1)
    spread_x(0, cotx)

    arrived(stat_r, stat_rs)
    its = stat_r[...]
    my_stat = stat_s[c]
    sums, spreads = its[:, 0, :], its[:, 1, :]
    mean = (jnp.sum(sums, axis=0, keepdims=True) + my_stat[0:1]) * (1.0 / D)
    away, my_away = sums * (1.0 / DS) - mean, my_stat[0:1] * (1.0 / DS) - mean
    variance = (
        jnp.sum(spreads + DS * away * away, axis=0, keepdims=True) + my_stat[1:2] + DS * my_away * my_away
    ) * (1.0 / D)
    inv_std = lax.rsqrt(variance + 1e-06)
    mean_col = jnp.transpose(jnp.broadcast_to(mean[:, 0:T], (EXTRA, T)))
    std_col = jnp.transpose(jnp.broadcast_to(inv_std[:, 0:T], (EXTRA, T)))
    inv_col[...] = std_col
    aways = jnp.concatenate([away[:, 0:T], my_away[:, 0:T], jnp.zeros((EXTRA - NW, T), F32)], axis=0)
    away_col[...] = jnp.transpose(aways)
    token_rows = pl.ds(pl.multiple_of(z * TB, TB), TB)
    my_aways = away_col[token_rows, :]
    leans, shift = [], []
    for j in range(FH // 128):
        piece = [its[s, 2 + j : 3 + j, :] for s in range(NW - 1)] + [my_stat[2 + j : 3 + j, :]]
        leans.append(functools.reduce(jnp.add, piece))
        shift.append(functools.reduce(jnp.add, [my_aways[:, s : s + 1] * piece[s] for s in range(NW)]))
    lean_row = jnp.concatenate(leans, axis=1)
    shift = jnp.concatenate(shift, axis=1)
    def hand_over(k):
        return lambda block: send(block, block, rel_ss.at[k], rel_rs.at[k], width=sibling)

    pre_act = (scatter_sum(over_z, own.at[0], zr.at[0], z_rs.at[0]) + shift) * inv_col[token_rows, 0:1]
    below = 0.5 * (1.0 + lax.erf(pre_act * inv_root_two))
    hid[c, z] = (pre_act * below).astype(BF16)
    units, grads = hid.at[c], gp.at[c]
    gather(over_z, units, ag_ss.at[0], ag_rs.at[0])
    hand_over(0)(hid.at[c, z])
    slope = below + pre_act * jnp.exp(-0.5 * pre_act * pre_act) * inv_root_two_pi
    grad_hidden = scatter_sum(over_z, own.at[1], zr.at[1], z_rs.at[1])
    grad_pre = (grad_hidden * slope).astype(BF16)
    wide = grad_pre.astype(F32)
    gp[c, z, :, 0:FH] = grad_pre
    gp[c, z, :, FH:] = pack(
        jnp.sum(wide * lean_row, axis=1, keepdims=True), jnp.sum(wide * pre_act, axis=1, keepdims=True)
    )
    gather(over_z, grads, ag_ss.at[1], ag_rs.at[1])
    hand_over(1)(gp.at[c, z])

    gather_pass(over_z, across_z, units, ag_ss.at[0], ag_rs.at[0], far_rs.at[0], hand_over(0))
    gather_near(over_z, units, ag_rs.at[0], hand_over(0))
    gather_pass(over_z, across_z, grads, ag_ss.at[1], ag_rs.at[1], far_rs.at[1], hand_over(1))
    gather_near(over_z, grads, ag_rs.at[1], hand_over(1))
    pass_x(0, cotx)
    for j in range(DS // 128):
        cols = slice(j * 128, (j + 1) * 128)
        normal = (tok[:, cols].astype(F32) - mean_col) * std_col
        normed[:, cols] = normal
        scx[0, :, cols] = (normal * g_all[:, cols]).astype(BF16)
    spread_x(1, scx)

    def gathered(k, buf):
        gather_far(over_z, buf.at[c], ag_rs.at[k], 4)
        gather_far(over_z, buf.at[1 - c], far_rs.at[k], 0)
        arrived(buf.at[1 - c, pl.ds(0, 5)], rel_rs.at[k])

    gathered(0, hid)

    term = dot(hid[0].reshape(T, FH), wdn[0:FH, :], 1, 0) + dot(hid[1].reshape(T, FH), wdn[FH:, :], 1, 0)
    term = term.reshape(NY, TY, DS)
    part0[...] = term
    ys0[...] = term.astype(BF16)
    direct_scatter("mlp", y, NY, ys0, yr0, y_ss.at[0], y_rs.at[0])

    my_blocks = pl.ds(pl.multiple_of(c * (NZ // 2), NZ // 2), NZ // 2)
    its_blocks = pl.ds(pl.multiple_of((1 - c) * (NZ // 2), NZ // 2), NZ // 2)

    def share(k, buf, dst):
        def one(o, carry):
            peer = lax.rem(x + o, NX)
            h, lanes = quarter(peer)
            send(buf.at[h, my_blocks, :, lanes], dst.at[o, my_blocks], q_ss.at[k], q_rs.at[k], dp=peer)
            return carry
        lax.fori_loop(1, NX, one, 0)
        h, lanes = quarter(x)
        dst[0] = buf[h, :, :, lanes]

    def join(k, dst):
        halves = dst.at[pl.ds(1, NX - 1), my_blocks]
        arrived(halves, q_rs.at[k])
        send(halves, halves, join_ss.at[k], join_rs.at[k], width=sibling)

    share(0, hid, hx)

    gathered(1, gp)
    term = dot(gp[0, :, :, 0:FH].reshape(T, FH), wup[:, 0:FH], 1, 1) + dot(
        gp[1, :, :, 0:FH].reshape(T, FH), wup[:, FH:], 1, 1
    )
    side = (gp[0, :, :, FH:].astype(F32) + gp[1, :, :, FH:].astype(F32)).reshape(T, EXTRA)
    part1[:, :, 0:DS] = term.reshape(NY, TY, DS)
    ys1[:, :, 0:DS] = term.reshape(NY, TY, DS).astype(BF16)
    part1[:, :, DS:] = side.reshape(NY, TY, EXTRA)
    ys1[:, :, DS:] = pack(*unpack(side)).reshape(NY, TY, EXTRA)
    direct_scatter("mlp", y, NY, ys1, yr1, y_ss.at[1], y_rs.at[1])
    share(1, gp, gpx)
    pass_x(1, scx)
    join(0, hx)

    arrived(yr0, y_rs.at[0])
    outv[y] = (part0[y] + jnp.sum(yr0[...].astype(F32), axis=0)).astype(BF16)
    direct_gather("mlp", y, NY, outv, yag_ss.at[0], yag_rs.at[0])

    end_x(0, cotx)
    arrived(hx.at[pl.ds(1, NX - 1), its_blocks], join_rs.at[0])
    gdn[...] = dot(hx[...].reshape(NX * T, FQ), cotx[...].reshape(NX * T, DS), 0, 0)
    arrived(yr1, y_rs.at[1])
    whole = part1[y] + jnp.sum(yr1[...].astype(F32), axis=0)
    grad_scaled = whole[:, 0:DS]
    first, second = unpack(whole[:, DS:])
    block = pl.ds(pl.multiple_of(y * TY, TY), TY)
    normal = normed[block, :]
    gtv[y] = (
        inv_col[block, 0:1] * (grad_scaled * gain_v[...].reshape(1, DS) - first * (1.0 / D) - normal * (second * (1.0 / D)))
    ).astype(BF16)
    direct_gather("mlp", y, NY, gtv, yag_ss.at[1], yag_rs.at[1])
    product = grad_scaled * normal
    gg_s[...] = jnp.sum(product.reshape(TY // 8, 8, DS), axis=0)

    def gain_x(o, carry):
        send(gg_s, ggx_r.at[o - 1], ggx_ss, ggx_rs, dp=lax.rem(x + o, NX))
        return carry
    lax.fori_loop(1, NX, gain_x, 0)
    join(1, gpx)

    arrived(ggx_r, ggx_rs)
    ggy_s[...] = gg_s[...] + jnp.sum(ggx_r[...], axis=0)

    def gain_y(o, carry):
        send(ggy_s, ggy_r.at[o - 1], ggy_ss, ggy_rs, mlp=lax.rem(y + o, NY))
        return carry
    lax.fori_loop(1, NY, gain_y, 0)

    end_x(1, scx)
    arrived(gpx.at[pl.ds(1, NX - 1), its_blocks], join_rs.at[1])
    product = dot(scx[...].reshape(NX * T, DS), gpx[...].reshape(NX * T, FQ), 0, 0)
    pieces = FQ // 128
    for j in range(pieces):
        gup[pl.ds(j, DS, stride=pieces), :] = product[:, j * 128 : (j + 1) * 128]
    arrived(outv.at[pl.ds(0, NY - 1)], yag_rs.at[0])
    out[...] = outv[...].reshape(T, DS)
    arrived(gtv.at[pl.ds(0, NY - 1)], yag_rs.at[1])
    gt[...] = gtv[...].reshape(T, DS)
    arrived(ggy_r, ggy_rs)
    gg[...] = jnp.sum(ggy_s[...] + jnp.sum(ggy_r[...], axis=0), axis=0)

    for k in range(2):
        arrived(sib_s.at[k], sib_ss.at[k])
        arrived(zs.at[k, pl.ds(0, NZ - 1)], z_ss.at[k])
    arrived(stat_r, stat_ss)
    for k, buf in enumerate((hid, gp)):
        arrived(buf.at[:, pl.ds(0, 5)], ag_ss.at[k])
        arrived(buf.at[0, pl.ds(0, 5)], rel_ss.at[k])
    for k, buf in enumerate((cotx, scx)):
        arrived(buf.at[pl.ds(0, NX - 1)], x_ss.at[k])
    for k, buf in enumerate((hx, gpx)):
        arrived(buf.at[pl.ds(1, NX - 1), my_blocks], q_ss.at[k])
        arrived(buf.at[pl.ds(1, NX - 1), my_blocks], join_ss.at[k])
    arrived(ys0.at[pl.ds(0, NY - 1)], y_ss.at[0])
    arrived(ys1.at[pl.ds(0, NY - 1)], y_ss.at[1])
    arrived(outv.at[pl.ds(0, NY - 1)], yag_ss.at[0])
    arrived(gtv.at[pl.ds(0, NY - 1)], yag_ss.at[1])
    arrived(ggx_r, ggx_ss)
    arrived(ggy_r, ggy_ss)


def place(*refs):
    made, given, sems = refs[0:5], refs[5:10], refs[10]
    copies = [pltpu.make_async_copy(src, dst, sems.at[k]) for k, (src, dst) in enumerate(zip(made, given))]
    for copy in copies:
        copy.start()
    for copy in copies:
        copy.wait()


def solution(mesh):
    NX, NZ, NY = mesh.shape["dp"], mesh.shape["width"] // 2, mesh.shape["mlp"]

    def shards(tokens, gain, up_weight, down_weight, cotangent):
        T, DS = tokens.shape
        FS = up_weight.shape[1]
        FH, FQ = FS // 2, FS // NX
        vmem, dma = pltpu.VMEM, pltpu.SemaphoreType.DMA
        results = (
            jax.ShapeDtypeStruct((T, DS), BF16),
            jax.ShapeDtypeStruct((T, DS), BF16),
            jax.ShapeDtypeStruct((DS,), F32),
            jax.ShapeDtypeStruct((DS * FQ // 128, 128), F32),
            jax.ShapeDtypeStruct((FQ, DS), F32),
        )
        call = pl.pallas_call(
            functools.partial(kernel, (NX, NZ, NY, DS * 2 * NZ)),
            out_shape=results,
            in_specs=[pl.BlockSpec(memory_space=pltpu.HBM)] * 5,
            out_specs=[pl.BlockSpec(memory_space=pltpu.VMEM)] * 5,
            scratch_shapes=[
                vmem((T, DS), BF16), vmem((DS,), F32), vmem((DS, FS), BF16), vmem((FS, DS), BF16),
                vmem((NX, T, DS), BF16), vmem((NX, T, DS), BF16), vmem((T, DS), F32), vmem((T, EXTRA), F32),
                vmem((2, 8, 128), F32), vmem((2 * NZ - 1, 8, 128), F32),
                vmem((2, T, FH), BF16), vmem((2, T, FH), BF16), vmem((2, NZ, TB, FH), F32),
                vmem((2, NZ, TB, FH), BF16), vmem((2, 6, TB, FH), BF16),
                vmem((2, 2, TB, FH // 2), BF16), vmem((2, 2, TB, FH), BF16),
                vmem((T + TB, DS), BF16), vmem((T, EXTRA), F32),
                vmem((2, NZ, TB, FH), BF16), vmem((2, NZ, TB, FH + EXTRA), BF16),
                vmem((NX, NZ, TB, FQ), BF16), vmem((NX, NZ, TB, FQ), BF16),
                *(
                    shape
                    for wide in (DS, DS + EXTRA)
                    for shape in (
                        vmem((NY, TB, wide), BF16), vmem((NY - 1, TB, wide), BF16), vmem((NY, TB, wide), F32),
                    )
                ),
                vmem((NY, TB, DS), BF16), vmem((NY, TB, DS), BF16),
                vmem((8, DS), F32), vmem((NX - 1, 8, DS), F32), vmem((8, DS), F32), vmem((NY - 1, 8, DS), F32),
                dma((5,)), dma((2,)), dma((2,)), dma, dma, dma((2,)), dma((2, 8)),
                dma((2,)), dma((2, 8)), dma((2, 4)), dma((2,)), dma((2,)),
                dma((2,)), dma((2, 4)), dma((2,)), dma((2,)), dma((2,)), dma((2,)),
                dma((2,)), dma((2,)), dma((2,)), dma((2,)), dma, dma, dma, dma,
            ],
            compiler_params=pltpu.CompilerParams(
                collective_id=0, has_side_effects=True, vmem_limit_bytes=48 * 1024 * 1024
            ),
            cost_estimate=pl.CostEstimate(
                flops=12 * T * DS * FS, bytes_accessed=4 * DS * FS + 8 * DS * FQ, transcendentals=2 * TB * FH
            ),
        )
        put = pl.pallas_call(
            place,
            out_shape=results,
            in_specs=[pl.BlockSpec(memory_space=pltpu.VMEM)] * 5,
            out_specs=[pl.BlockSpec(memory_space=pltpu.HBM)] * 5,
            scratch_shapes=[dma((5,))],
            compiler_params=pltpu.CompilerParams(vmem_limit_bytes=4 * 1024 * 1024),
        )
        output, grad_tokens, grad_gain, grad_up, grad_down = put(
            *call(*(pltpu.with_memory_space_constraint(a, pltpu.HBM) for a in (tokens, gain, up_weight, down_weight, cotangent)))
        )
        return output, grad_tokens, grad_gain, grad_up.reshape(DS, 1, FQ), grad_down[None, :, :]

    placed = (P("dp", "width"), P("width"), P("width", "mlp"), P("mlp", "width"), P("dp", "width"))
    return jax.shard_map(
        shards,
        mesh=mesh,
        in_specs=placed,
        out_specs=(
            P("dp", "width"),
            P("dp", "width"),
            P("width"),
            P("width", "mlp", "dp"),
            P("mlp", "dp", "width"),
        ),
        check_vma=False,
    )
```

```python
import functools

import jax
import jax.numpy as jnp
from jax import lax
from jax.experimental import pallas as pl
from jax.experimental.pallas import tpu as pltpu
from jax.sharding import PartitionSpec as P

MESH = pl.DeviceIdType.MESH
F32, BF16 = jnp.float32, jnp.bfloat16
TB = 16
EXTRA = 128

inv_root_two = 0.7071067811865476
inv_root_two_pi = 0.3989422804014327


def dot(left, right, left_dim, right_dim):
    return lax.dot_general(
        left, right, (((left_dim,), (right_dim,)), ((), ())), preferred_element_type=F32
    )


def pack(first, second):
    lane = lax.broadcasted_iota(jnp.int32, (first.shape[0], EXTRA), 1)
    high_one, high_two = first.astype(BF16).astype(F32), second.astype(BF16).astype(F32)
    held = jnp.where(lane == 0, high_one, 0.0)
    held = jnp.where(lane == 1, high_two, held)
    held = jnp.where(lane == 2, first - high_one, held)
    held = jnp.where(lane == 3, second - high_two, held)
    return held.astype(BF16)


def unpack(held):
    return held[:, 0:1] + held[:, 2:3], held[:, 1:2] + held[:, 3:4]


def send(src, dst, ss, rs, **where):
    pltpu.make_async_remote_copy(
        src_ref=src, dst_ref=dst, send_sem=ss, recv_sem=rs, device_id=where, device_id_type=MESH
    ).start()


def arrived(ref, sem):
    pltpu.make_async_copy(ref, ref, sem).wait()


def ring(axis, me, device=lambda position: position):
    def at(o):
        return lax.rem(me + o % 8, 8)
    return at, lambda o: {axis: device(at(o))}


def lanes_of(block, side):
    cut = block.shape[-1] // 256 * 128
    return block.at[:, pl.ds(0, cut) if side == 0 else pl.ds(cut, block.shape[-1] - cut)]


def scatter(to_whom, terms, got, halves, ss, rs):
    at, to = to_whom
    for side, o in ((0, 1), (1, -1)):
        send(terms.at[at(3 * o)], got.at[4 + side], ss, rs.at[4 + side], **to(o))
    for side, o in ((0, 2), (1, -2)):
        send(lanes_of(terms.at[at(4)], side), halves[side], ss, rs.at[6 + side], **to(o))
    for side, o in ((0, 1), (1, -1)):
        send(terms.at[at(o)], got.at[side], ss, rs.at[side], **to(o))


def scatter_pass(to_whom, own, got, halves, sums, ss, rs):
    at, to = to_whom
    for side, o in ((0, 2), (1, -2)):
        arrived(got.at[4 + side], rs.at[4 + side])
        arrived(halves[side], rs.at[6 + side])
        term = own[at(o)] + got[4 + side].astype(F32)
        half = halves[side][...].astype(F32)
        cut = term.shape[-1] // 256 * 128
        low, high = term[:, 0:cut], term[:, cut:]
        sums[side, :, 0:cut] = (low + half if side == 0 else low).astype(BF16)
        sums[side, :, cut:] = (high if side == 0 else high + half).astype(BF16)
        send(sums.at[side], got.at[2 + side], ss, rs.at[2 + side], **to(o))


def scatter_sum(to_whom, own, got, rs):
    at, _ = to_whom
    for slot in range(4):
        arrived(got.at[slot], rs.at[slot])
    return own[at(0)] + jnp.sum(got[0:4].astype(F32), axis=0)


def gather(to_whom, buf, ss, rs):
    at, to = to_whom
    block = buf.at[at(0)]
    for o, slot in ((2, 2), (-2, 3), (1, 0), (-1, 1)):
        send(block, block, ss, rs.at[slot], **to(o))


def gather_pass(here, there, buf, ss, rs, far_rs, use):
    at, _ = here
    for side, o in ((0, 1), (1, -1)):
        block = buf.at[at(-2 * o)]
        arrived(block, rs.at[2 + side])
        half = lanes_of(block, side)
        for (_, to), sems, first in ((here, rs, 4), (there, far_rs, 0)):
            send(block, block, ss, sems.at[first + side], **to(o))
            send(half, half, ss, sems.at[first + 2 + side], **to(2 * o))
        use(block)


def gather_near(here, buf, rs, use):
    at, _ = here
    for side, o in ((0, -1), (1, 1)):
        arrived(buf.at[at(o)], rs.at[side])
        use(buf.at[at(o)])


def gather_far(here, buf, sems, first):
    at, _ = here
    for side, o in ((0, -3), (1, 3)):
        arrived(buf.at[at(o)], sems.at[first + side])
        arrived(lanes_of(buf.at[at(4)], side), sems.at[first + 2 + side])


def around(i, n):
    half = lax.div(n - 2 - i, 2) + 1
    return jnp.where(lax.rem(n - 2 - i, 2) == 0, half, n - half)


def direct_scatter(axis, me, n, terms, got, ss, rs):
    def one(i, carry):
        o = around(i, n)
        peer = lax.rem(me + o, n)
        send(terms.at[peer], got.at[o - 1], ss, rs, **{axis: peer})
        return carry
    lax.fori_loop(0, n - 1, one, 0)


def direct_gather(axis, me, n, buf, ss, rs):
    def one(i, carry):
        send(buf.at[me], buf.at[me], ss, rs, **{axis: lax.rem(me + around(i, n), n)})
        return carry
    lax.fori_loop(0, n - 1, one, 0)


def kernel(
    sizes, tok_h, gain_h, wup_h, wdn_h, cot_h, out, gt, gg, gup, gdn,
    tok, gain_v, wup, wdn, cotx, scx, normed, inv_col,
    stat_s, stat_r,
    sib_s, sib_r, own, zs, zr, zh, zc, leaning, away_col,
    hid, gp, hx, gpx,
    ys0, yr0, part0, ys1, yr1, part1,
    outv, gtv,
    gg_s, ggx_r, ggy_s, ggy_r,
    ld, sib_ss, sib_rs, stat_ss, stat_rs, z_ss, z_rs, ag_ss, ag_rs, far_rs, rel_ss, rel_rs,
    x_ss, x_rs, q_ss, q_rs, join_ss, join_rs, y_ss, y_rs, yag_ss, yag_rs, ggx_ss, ggx_rs, ggy_ss, ggy_rs,
):
    NX, NZ, NY, D = sizes
    T, DS = tok.shape
    TY = T // NY
    FS = wup.shape[1]
    FH, FQ = FS // 2, FS // NX
    NW = 2 * NZ
    x, w, y = lax.axis_index("dp"), lax.axis_index("width"), lax.axis_index("mlp")
    z = lax.div(w, 2)
    c = w - 2 * z
    sibling = 2 * z + 1 - c

    over_z = ring("width", z, lambda position: 2 * position + c)
    across_z = ring("width", z, lambda position: 2 * position + 1 - c)

    def quarter(q):
        first = q * FQ
        h = lax.div(first, FH)
        return h, pl.ds(pl.multiple_of(first - h * FH, FQ), FQ)

    loads = [
        pltpu.make_async_copy(tok_h, tok, ld.at[0]),
        pltpu.make_async_copy(gain_h, gain_v, ld.at[1]),
        pltpu.make_async_copy(wup_h, wup, ld.at[2]),
        pltpu.make_async_copy(cot_h, cotx.at[0], ld.at[3]),
        pltpu.make_async_copy(wdn_h, wdn, ld.at[4]),
    ]
    for load in loads:
        load.start()

    barrier = pltpu.get_barrier_semaphore()

    def greet(axis, me, n):
        def one(k, carry):
            pl.semaphore_signal(barrier, inc=1, device_id={axis: lax.rem(me + k, n)}, device_id_type=MESH)
            return carry
        lax.fori_loop(1, n, one, 0)

    greet("width", w, NW)
    greet("mlp", y, NY)
    greet("dp", x, NX)

    mine = pl.ds(pl.multiple_of(c * FH, FH), FH)
    other = pl.ds(pl.multiple_of(FH - c * FH, FH), FH)

    loads[0].wait()
    loads[1].wait()
    values = tok[...].astype(F32)
    total = jnp.sum(values, axis=1, keepdims=True)
    shifted = values - total * (1.0 / DS)
    spread = jnp.sum(shifted * shifted, axis=1, keepdims=True)
    g_all = gain_v[...].reshape(1, DS)
    leaning[0:T] = (shifted * g_all).astype(BF16)
    row = lax.broadcasted_iota(jnp.int32, (TB, DS), 0)
    g_one = g_all.astype(BF16).astype(F32)
    g_two = (g_all - g_one).astype(BF16).astype(F32)
    g_rows = jnp.where(row == 0, g_one, jnp.where(row == 1, g_two, jnp.where(row == 2, g_all - g_one - g_two, 0.0)))
    leaning[T:] = g_rows.astype(BF16)
    loads[2].wait()
    its_half = dot(leaning[...], wup[:, other], 1, 0)
    sib_s[0] = its_half[0:T].astype(BF16)
    pl.semaphore_wait(barrier, NW - 1 + NY - 1 + NX - 1)
    send(sib_s.at[0], sib_r.at[0], sib_ss.at[0], sib_rs.at[0], width=sibling)

    loads[3].wait()
    loads[4].wait()
    sib_s[1] = dot(cotx[0], wdn[other, :], 1, 1).astype(BF16)
    send(sib_s.at[1], sib_r.at[1], sib_ss.at[1], sib_rs.at[1], width=sibling)

    def merge(k, mine_half):
        arrived(sib_r.at[k], sib_rs.at[k])
        both = (mine_half + sib_r[k].astype(F32)).reshape(NZ, TB, FH)
        own[k] = both
        zs[k] = both.astype(BF16)
        scatter(over_z, zs.at[k], zr.at[k], [zh.at[k, 0], zh.at[k, 1]], z_ss.at[k], z_rs.at[k])

    def merge_pass(k):
        scatter_pass(
            over_z, own.at[k], zr.at[k], [zh.at[k, 0], zh.at[k, 1]], zc.at[k], z_ss.at[k], z_rs.at[k]
        )

    my_half = dot(leaning[...], wup[:, mine], 1, 0)
    merge(0, my_half[0:T])
    merge(1, dot(cotx[0], wdn[mine, :], 1, 1))

    total_row = jnp.transpose(jnp.broadcast_to(total, (T, EXTRA)))[0:1]
    spread_row = jnp.transpose(jnp.broadcast_to(spread, (T, EXTRA)))[0:1]
    for h, half in ((c, my_half), (1 - c, its_half)):
        lean = jnp.sum(half[T:], axis=0, keepdims=True)
        stat_s[h, 0:1, 0:T] = total_row
        stat_s[h, 1:2, 0:T] = spread_row
        for j in range(FH // 128):
            stat_s[h, 2 + j : 3 + j, :] = lean[:, j * 128 : (j + 1) * 128]

    def tell(k, carry):
        peer = lax.rem(w + k, NW)
        send(stat_s.at[lax.rem(peer, 2)], stat_r.at[k - 1], stat_ss, stat_rs, width=peer)
        return carry
    lax.fori_loop(1, NW, tell, 0)

    right, left = lax.rem(x + 1, NX), lax.rem(x + NX - 1, NX)
    first_rows, last_rows = pl.ds(0, T // 2), pl.ds(T // 2, T // 2)

    def spread_x(k, buf):
        send(buf.at[0], buf.at[1], x_ss.at[k], x_rs.at[k, 0], dp=right)
        send(buf.at[0], buf.at[NX - 1], x_ss.at[k], x_rs.at[k, 1], dp=left)

    def pass_x(k, buf):
        arrived(buf.at[1], x_rs.at[k, 0])
        send(buf.at[1, first_rows], buf.at[2, first_rows], x_ss.at[k], x_rs.at[k, 2], dp=right)
        arrived(buf.at[NX - 1], x_rs.at[k, 1])
        send(buf.at[NX - 1, last_rows], buf.at[2, last_rows], x_ss.at[k], x_rs.at[k, 3], dp=left)

    def end_x(k, buf):
        arrived(buf.at[2, first_rows], x_rs.at[k, 2])
        arrived(buf.at[2, last_rows], x_rs.at[k, 3])

    merge_pass(0)
    merge_pass(1)
    spread_x(0, cotx)

    arrived(stat_r, stat_rs)
    its = stat_r[...]
    my_stat = stat_s[c]
    sums, spreads = its[:, 0, :], its[:, 1, :]
    mean = (jnp.sum(sums, axis=0, keepdims=True) + my_stat[0:1]) * (1.0 / D)
    away, my_away = sums * (1.0 / DS) - mean, my_stat[0:1] * (1.0 / DS) - mean
    variance = (
        jnp.sum(spreads + DS * away * away, axis=0, keepdims=True) + my_stat[1:2] + DS * my_away * my_away
    ) * (1.0 / D)
    inv_std = lax.rsqrt(variance + 1e-06)
    mean_col = jnp.transpose(jnp.broadcast_to(mean[:, 0:T], (EXTRA, T)))
    std_col = jnp.transpose(jnp.broadcast_to(inv_std[:, 0:T], (EXTRA, T)))
    inv_col[...] = std_col
    aways = jnp.concatenate([away[:, 0:T], my_away[:, 0:T], jnp.zeros((EXTRA - NW, T), F32)], axis=0)
    away_col[...] = jnp.transpose(aways)
    token_rows = pl.ds(pl.multiple_of(z * TB, TB), TB)
    my_aways = away_col[token_rows, :]
    leans, shift = [], []
    for j in range(FH // 128):
        piece = [its[s, 2 + j : 3 + j, :] for s in range(NW - 1)] + [my_stat[2 + j : 3 + j, :]]
        leans.append(functools.reduce(jnp.add, piece))
        shift.append(functools.reduce(jnp.add, [my_aways[:, s : s + 1] * piece[s] for s in range(NW)]))
    lean_row = jnp.concatenate(leans, axis=1)
    shift = jnp.concatenate(shift, axis=1)
    def hand_over(k):
        return lambda block: send(block, block, rel_ss.at[k], rel_rs.at[k], width=sibling)

    pre_act = (scatter_sum(over_z, own.at[0], zr.at[0], z_rs.at[0]) + shift) * inv_col[token_rows, 0:1]
    below = 0.5 * (1.0 + lax.erf(pre_act * inv_root_two))
    hid[c, z] = (pre_act * below).astype(BF16)
    units, grads = hid.at[c], gp.at[c]
    gather(over_z, units, ag_ss.at[0], ag_rs.at[0])
    hand_over(0)(hid.at[c, z])
    slope = below + pre_act * jnp.exp(-0.5 * pre_act * pre_act) * inv_root_two_pi
    grad_hidden = scatter_sum(over_z, own.at[1], zr.at[1], z_rs.at[1])
    grad_pre = (grad_hidden * slope).astype(BF16)
    wide = grad_pre.astype(F32)
    gp[c, z, :, 0:FH] = grad_pre
    gp[c, z, :, FH:] = pack(
        jnp.sum(wide * lean_row, axis=1, keepdims=True), jnp.sum(wide * pre_act, axis=1, keepdims=True)
    )
    gather(over_z, grads, ag_ss.at[1], ag_rs.at[1])
    hand_over(1)(gp.at[c, z])

    gather_pass(over_z, across_z, units, ag_ss.at[0], ag_rs.at[0], far_rs.at[0], hand_over(0))
    gather_near(over_z, units, ag_rs.at[0], hand_over(0))
    gather_pass(over_z, across_z, grads, ag_ss.at[1], ag_rs.at[1], far_rs.at[1], hand_over(1))
    gather_near(over_z, grads, ag_rs.at[1], hand_over(1))
    pass_x(0, cotx)
    for j in range(DS // 128):
        cols = slice(j * 128, (j + 1) * 128)
        normal = (tok[:, cols].astype(F32) - mean_col) * std_col
        normed[:, cols] = normal
        scx[0, :, cols] = (normal * g_all[:, cols]).astype(BF16)
    spread_x(1, scx)

    def gathered(k, buf):
        gather_far(over_z, buf.at[c], ag_rs.at[k], 4)
        gather_far(over_z, buf.at[1 - c], far_rs.at[k], 0)
        arrived(buf.at[1 - c, pl.ds(0, 5)], rel_rs.at[k])

    gathered(0, hid)

    term = dot(hid[0].reshape(T, FH), wdn[0:FH, :], 1, 0) + dot(hid[1].reshape(T, FH), wdn[FH:, :], 1, 0)
    term = term.reshape(NY, TY, DS)
    part0[...] = term
    ys0[...] = term.astype(BF16)
    direct_scatter("mlp", y, NY, ys0, yr0, y_ss.at[0], y_rs.at[0])

    my_blocks = pl.ds(pl.multiple_of(c * (NZ // 2), NZ // 2), NZ // 2)
    its_blocks = pl.ds(pl.multiple_of((1 - c) * (NZ // 2), NZ // 2), NZ // 2)

    def share(k, buf, dst):
        def one(o, carry):
            peer = lax.rem(x + o, NX)
            h, lanes = quarter(peer)
            send(buf.at[h, my_blocks, :, lanes], dst.at[o, my_blocks], q_ss.at[k], q_rs.at[k], dp=peer)
            return carry
        lax.fori_loop(1, NX, one, 0)
        h, lanes = quarter(x)
        dst[0] = buf[h, :, :, lanes]

    def join(k, dst):
        halves = dst.at[pl.ds(1, NX - 1), my_blocks]
        arrived(halves, q_rs.at[k])
        send(halves, halves, join_ss.at[k], join_rs.at[k], width=sibling)

    share(0, hid, hx)

    gathered(1, gp)
    term = dot(gp[0, :, :, 0:FH].reshape(T, FH), wup[:, 0:FH], 1, 1) + dot(
        gp[1, :, :, 0:FH].reshape(T, FH), wup[:, FH:], 1, 1
    )
    side = (gp[0, :, :, FH:].astype(F32) + gp[1, :, :, FH:].astype(F32)).reshape(T, EXTRA)
    first, second = unpack(side)
    normal = normed[...]
    corrected = inv_col[:, 0:1] * (
        term * gain_v[...].reshape(1, DS) - first * (1.0 / D) - normal * (second * (1.0 / D))
    )
    corrected = corrected.reshape(NY, TY, DS)
    part1[...] = corrected
    ys1[...] = corrected.astype(BF16)
    direct_scatter("mlp", y, NY, ys1, yr1, y_ss.at[1], y_rs.at[1])
    share(1, gp, gpx)
    gg_s[...] = jnp.sum((term * normal).reshape(T // 8, 8, DS), axis=0)

    def gain_x(o, carry):
        send(gg_s, ggx_r.at[o - 1], ggx_ss, ggx_rs, dp=lax.rem(x + o, NX))
        return carry
    lax.fori_loop(1, NX, gain_x, 0)
    pass_x(1, scx)
    join(0, hx)

    arrived(yr0, y_rs.at[0])
    outv[y] = (part0[y] + jnp.sum(yr0[...].astype(F32), axis=0)).astype(BF16)
    direct_gather("mlp", y, NY, outv, yag_ss.at[0], yag_rs.at[0])

    arrived(ggx_r, ggx_rs)
    ggy_s[...] = gg_s[...] + jnp.sum(ggx_r[...], axis=0)

    def gain_y(o, carry):
        send(ggy_s, ggy_r.at[o - 1], ggy_ss, ggy_rs, mlp=lax.rem(y + o, NY))
        return carry
    lax.fori_loop(1, NY, gain_y, 0)

    end_x(0, cotx)
    arrived(hx.at[pl.ds(1, NX - 1), its_blocks], join_rs.at[0])
    gdn[...] = dot(hx[...].reshape(NX * T, FQ), cotx[...].reshape(NX * T, DS), 0, 0)
    arrived(yr1, y_rs.at[1])
    gtv[y] = (part1[y] + jnp.sum(yr1[...].astype(F32), axis=0)).astype(BF16)
    direct_gather("mlp", y, NY, gtv, yag_ss.at[1], yag_rs.at[1])
    join(1, gpx)

    end_x(1, scx)
    arrived(gpx.at[pl.ds(1, NX - 1), its_blocks], join_rs.at[1])
    product = dot(scx[...].reshape(NX * T, DS), gpx[...].reshape(NX * T, FQ), 0, 0)
    pieces = FQ // 128
    for j in range(pieces):
        gup[pl.ds(j, DS, stride=pieces), :] = product[:, j * 128 : (j + 1) * 128]
    arrived(outv.at[pl.ds(0, NY - 1)], yag_rs.at[0])
    out[...] = outv[...].reshape(T, DS)
    arrived(gtv.at[pl.ds(0, NY - 1)], yag_rs.at[1])
    gt[...] = gtv[...].reshape(T, DS)
    arrived(ggy_r, ggy_rs)
    gg[...] = jnp.sum(ggy_s[...] + jnp.sum(ggy_r[...], axis=0), axis=0)

    for k in range(2):
        arrived(sib_s.at[k], sib_ss.at[k])
        arrived(zs.at[k, pl.ds(0, NZ - 1)], z_ss.at[k])
    arrived(stat_r, stat_ss)
    for k, buf in enumerate((hid, gp)):
        arrived(buf.at[:, pl.ds(0, 5)], ag_ss.at[k])
        arrived(buf.at[0, pl.ds(0, 5)], rel_ss.at[k])
    for k, buf in enumerate((cotx, scx)):
        arrived(buf.at[pl.ds(0, NX - 1)], x_ss.at[k])
    for k, buf in enumerate((hx, gpx)):
        arrived(buf.at[pl.ds(1, NX - 1), my_blocks], q_ss.at[k])
        arrived(buf.at[pl.ds(1, NX - 1), my_blocks], join_ss.at[k])
    arrived(ys0.at[pl.ds(0, NY - 1)], y_ss.at[0])
    arrived(ys1.at[pl.ds(0, NY - 1)], y_ss.at[1])
    arrived(outv.at[pl.ds(0, NY - 1)], yag_ss.at[0])
    arrived(gtv.at[pl.ds(0, NY - 1)], yag_ss.at[1])
    arrived(ggx_r, ggx_ss)
    arrived(ggy_r, ggy_ss)


def place(*refs):
    made, given, sems = refs[0:5], refs[5:10], refs[10]
    copies = [pltpu.make_async_copy(src, dst, sems.at[k]) for k, (src, dst) in enumerate(zip(made, given))]
    for copy in copies:
        copy.start()
    for copy in copies:
        copy.wait()


def solution(mesh):
    NX, NZ, NY = mesh.shape["dp"], mesh.shape["width"] // 2, mesh.shape["mlp"]

    def shards(tokens, gain, up_weight, down_weight, cotangent):
        T, DS = tokens.shape
        FS = up_weight.shape[1]
        FH, FQ = FS // 2, FS // NX
        vmem, dma = pltpu.VMEM, pltpu.SemaphoreType.DMA
        results = (
            jax.ShapeDtypeStruct((T, DS), BF16),
            jax.ShapeDtypeStruct((T, DS), BF16),
            jax.ShapeDtypeStruct((DS,), F32),
            jax.ShapeDtypeStruct((DS * FQ // 128, 128), F32),
            jax.ShapeDtypeStruct((FQ, DS), F32),
        )
        call = pl.pallas_call(
            functools.partial(kernel, (NX, NZ, NY, DS * 2 * NZ)),
            out_shape=results,
            in_specs=[pl.BlockSpec(memory_space=pltpu.HBM)] * 5,
            out_specs=[pl.BlockSpec(memory_space=pltpu.VMEM)] * 5,
            scratch_shapes=[
                vmem((T, DS), BF16), vmem((DS,), F32), vmem((DS, FS), BF16), vmem((FS, DS), BF16),
                vmem((NX, T, DS), BF16), vmem((NX, T, DS), BF16), vmem((T, DS), F32), vmem((T, EXTRA), F32),
                vmem((2, 8, 128), F32), vmem((2 * NZ - 1, 8, 128), F32),
                vmem((2, T, FH), BF16), vmem((2, T, FH), BF16), vmem((2, NZ, TB, FH), F32),
                vmem((2, NZ, TB, FH), BF16), vmem((2, 6, TB, FH), BF16),
                vmem((2, 2, TB, FH // 2), BF16), vmem((2, 2, TB, FH), BF16),
                vmem((T + TB, DS), BF16), vmem((T, EXTRA), F32),
                vmem((2, NZ, TB, FH), BF16), vmem((2, NZ, TB, FH + EXTRA), BF16),
                vmem((NX, NZ, TB, FQ), BF16), vmem((NX, NZ, TB, FQ), BF16),
                *(
                    shape
                    for _ in range(2)
                    for shape in (
                        vmem((NY, TB, DS), BF16), vmem((NY - 1, TB, DS), BF16), vmem((NY, TB, DS), F32),
                    )
                ),
                vmem((NY, TB, DS), BF16), vmem((NY, TB, DS), BF16),
                vmem((8, DS), F32), vmem((NX - 1, 8, DS), F32), vmem((8, DS), F32), vmem((NY - 1, 8, DS), F32),
                dma((5,)), dma((2,)), dma((2,)), dma, dma, dma((2,)), dma((2, 8)),
                dma((2,)), dma((2, 8)), dma((2, 4)), dma((2,)), dma((2,)),
                dma((2,)), dma((2, 4)), dma((2,)), dma((2,)), dma((2,)), dma((2,)),
                dma((2,)), dma((2,)), dma((2,)), dma((2,)), dma, dma, dma, dma,
            ],
            compiler_params=pltpu.CompilerParams(
                collective_id=0, has_side_effects=True, vmem_limit_bytes=48 * 1024 * 1024
            ),
            cost_estimate=pl.CostEstimate(
                flops=12 * T * DS * FS, bytes_accessed=4 * DS * FS + 8 * DS * FQ, transcendentals=2 * TB * FH
            ),
        )
        put = pl.pallas_call(
            place,
            out_shape=results,
            in_specs=[pl.BlockSpec(memory_space=pltpu.VMEM)] * 5,
            out_specs=[pl.BlockSpec(memory_space=pltpu.HBM)] * 5,
            scratch_shapes=[dma((5,))],
            compiler_params=pltpu.CompilerParams(vmem_limit_bytes=4 * 1024 * 1024),
        )
        output, grad_tokens, grad_gain, grad_up, grad_down = put(
            *call(*(pltpu.with_memory_space_constraint(a, pltpu.HBM) for a in (tokens, gain, up_weight, down_weight, cotangent)))
        )
        return output, grad_tokens, grad_gain, grad_up.reshape(DS, 1, FQ), grad_down[None, :, :]

    placed = (P("dp", "width"), P("width"), P("width", "mlp"), P("mlp", "width"), P("dp", "width"))
    return jax.shard_map(
        shards,
        mesh=mesh,
        in_specs=placed,
        out_specs=(
            P("dp", "width"),
            P("dp", "width"),
            P("width"),
            P("width", "mlp", "dp"),
            P("mlp", "dp", "width"),
        ),
        check_vma=False,
    )
```

```python
import functools

import jax
import jax.numpy as jnp
from jax import lax
from jax.experimental import pallas as pl
from jax.experimental.pallas import tpu as pltpu
from jax.sharding import PartitionSpec as P

MESH = pl.DeviceIdType.MESH
F32, BF16 = jnp.float32, jnp.bfloat16
TB = 16
EXTRA = 128

inv_root_two = 0.7071067811865476
inv_root_two_pi = 0.3989422804014327


def dot(left, right, left_dim, right_dim):
    return lax.dot_general(
        left, right, (((left_dim,), (right_dim,)), ((), ())), preferred_element_type=F32
    )


def pack(first, second):
    lane = lax.broadcasted_iota(jnp.int32, (first.shape[0], EXTRA), 1)
    high_one, high_two = first.astype(BF16).astype(F32), second.astype(BF16).astype(F32)
    held = jnp.where(lane == 0, high_one, 0.0)
    held = jnp.where(lane == 1, high_two, held)
    held = jnp.where(lane == 2, first - high_one, held)
    held = jnp.where(lane == 3, second - high_two, held)
    return held.astype(BF16)


def unpack(held):
    return held[:, 0:1] + held[:, 2:3], held[:, 1:2] + held[:, 3:4]


def send(src, dst, ss, rs, **where):
    pltpu.make_async_remote_copy(
        src_ref=src, dst_ref=dst, send_sem=ss, recv_sem=rs, device_id=where, device_id_type=MESH
    ).start()


def arrived(ref, sem):
    pltpu.make_async_copy(ref, ref, sem).wait()


def ring(axis, me, device=lambda position: position):
    def at(o):
        return lax.rem(me + o % 8, 8)
    return at, lambda o: {axis: device(at(o))}


def lanes_of(block, side):
    cut = block.shape[-1] // 256 * 128
    return block.at[:, pl.ds(0, cut) if side == 0 else pl.ds(cut, block.shape[-1] - cut)]


def scatter(to_whom, terms, got, halves, ss, rs):
    at, to = to_whom
    for side, o in ((0, 1), (1, -1)):
        send(terms.at[at(3 * o)], got.at[4 + side], ss, rs.at[4 + side], **to(o))
    for side, o in ((0, 2), (1, -2)):
        send(lanes_of(terms.at[at(4)], side), halves[side], ss, rs.at[6 + side], **to(o))
    for side, o in ((0, 1), (1, -1)):
        send(terms.at[at(o)], got.at[side], ss, rs.at[side], **to(o))


def scatter_pass(to_whom, own, got, halves, sums, ss, rs):
    at, to = to_whom
    for side, o in ((0, 2), (1, -2)):
        arrived(got.at[4 + side], rs.at[4 + side])
        arrived(halves[side], rs.at[6 + side])
        term = own[at(o)] + got[4 + side].astype(F32)
        half = halves[side][...].astype(F32)
        cut = term.shape[-1] // 256 * 128
        low, high = term[:, 0:cut], term[:, cut:]
        sums[side, :, 0:cut] = (low + half if side == 0 else low).astype(BF16)
        sums[side, :, cut:] = (high if side == 0 else high + half).astype(BF16)
        send(sums.at[side], got.at[2 + side], ss, rs.at[2 + side], **to(o))


def scatter_sum(to_whom, own, got, rs):
    at, _ = to_whom
    for slot in range(4):
        arrived(got.at[slot], rs.at[slot])
    return own[at(0)] + jnp.sum(got[0:4].astype(F32), axis=0)


def gather(to_whom, buf, ss, rs):
    at, to = to_whom
    block = buf.at[at(0)]
    for o, slot in ((2, 2), (-2, 3), (1, 0), (-1, 1)):
        send(block, block, ss, rs.at[slot], **to(o))


def gather_pass(here, there, buf, ss, rs, far_rs, use):
    at, _ = here
    for side, o in ((0, 1), (1, -1)):
        block = buf.at[at(-2 * o)]
        arrived(block, rs.at[2 + side])
        half = lanes_of(block, side)
        for (_, to), sems, first in ((here, rs, 4), (there, far_rs, 0)):
            send(block, block, ss, sems.at[first + side], **to(o))
            send(half, half, ss, sems.at[first + 2 + side], **to(2 * o))
        use(block)


def gather_near(here, buf, rs, use):
    at, _ = here
    for side, o in ((0, -1), (1, 1)):
        arrived(buf.at[at(o)], rs.at[side])
        use(buf.at[at(o)])


def gather_far(here, buf, sems, first):
    at, _ = here
    for side, o in ((0, -3), (1, 3)):
        arrived(buf.at[at(o)], sems.at[first + side])
        arrived(lanes_of(buf.at[at(4)], side), sems.at[first + 2 + side])


def kernel(
    sizes, tok_h, gain_h, wup_h, wdn_h, cot_h, out, gt, gg, gup, gdn,
    tok, gain_v, wup, wdn, cotx, scx, normed, inv_col,
    stat_s, stat_r,
    sib_s, sib_r, own, zs, zr, zh, zc, leaning, away_col,
    hid, gp, hx, gpx,
    ys0, yr0, part0, ys1, yr1, part1,
    outv, gtv,
    gg_sum, gg_s, ggx_r, ggy_s, ggy_r,
    ld, sib_ss, sib_rs, stat_ss, stat_rs, z_ss, z_rs, ag_ss, ag_rs, far_rs, rel_ss, rel_rs,
    x_ss, x_rs, q_ss, q_rs, join_ss, join_rs, y_ss, y_rs, yag_ss, yag_rs, ggx_ss, ggx_rs, ggy_ss, ggy_rs,
):
    NX, NZ, NY, D = sizes
    T, DS = tok.shape
    TY = T // NY
    FS = wup.shape[1]
    FH, FQ = FS // 2, FS // NX
    NW = 2 * NZ
    x, w, y = lax.axis_index("dp"), lax.axis_index("width"), lax.axis_index("mlp")
    z = lax.div(w, 2)
    c = w - 2 * z
    sibling = 2 * z + 1 - c

    over_z = ring("width", z, lambda position: 2 * position + c)
    across_z = ring("width", z, lambda position: 2 * position + 1 - c)

    def quarter(q):
        first = q * FQ
        h = lax.div(first, FH)
        return h, pl.ds(pl.multiple_of(first - h * FH, FQ), FQ)

    loads = [
        pltpu.make_async_copy(tok_h, tok, ld.at[0]),
        pltpu.make_async_copy(gain_h, gain_v, ld.at[1]),
        pltpu.make_async_copy(wup_h, wup, ld.at[2]),
        pltpu.make_async_copy(cot_h, cotx.at[0], ld.at[3]),
        pltpu.make_async_copy(wdn_h, wdn, ld.at[4]),
    ]
    for load in loads:
        load.start()

    barrier = pltpu.get_barrier_semaphore()

    def greet(axis, me, n):
        def one(k, carry):
            pl.semaphore_signal(barrier, inc=1, device_id={axis: lax.rem(me + k, n)}, device_id_type=MESH)
            return carry
        lax.fori_loop(1, n, one, 0)

    greet("width", w, NW)
    greet("mlp", y, NY)
    greet("dp", x, NX)

    mine = pl.ds(pl.multiple_of(c * FH, FH), FH)
    other = pl.ds(pl.multiple_of(FH - c * FH, FH), FH)

    loads[0].wait()
    loads[1].wait()
    values = tok[...].astype(F32)
    total = jnp.sum(values, axis=1, keepdims=True)
    shifted = values - total * (1.0 / DS)
    spread = jnp.sum(shifted * shifted, axis=1, keepdims=True)
    g_all = gain_v[...].reshape(1, DS)
    leaning[0:T] = (shifted * g_all).astype(BF16)
    row = lax.broadcasted_iota(jnp.int32, (TB, DS), 0)
    g_one = g_all.astype(BF16).astype(F32)
    g_two = (g_all - g_one).astype(BF16).astype(F32)
    g_rows = jnp.where(row == 0, g_one, jnp.where(row == 1, g_two, jnp.where(row == 2, g_all - g_one - g_two, 0.0)))
    leaning[T:] = g_rows.astype(BF16)
    loads[2].wait()
    its_half = dot(leaning[...], wup[:, other], 1, 0)
    sib_s[0] = its_half[0:T].astype(BF16)
    pl.semaphore_wait(barrier, NW - 1 + NY - 1 + NX - 1)
    send(sib_s.at[0], sib_r.at[0], sib_ss.at[0], sib_rs.at[0], width=sibling)

    loads[3].wait()
    loads[4].wait()
    sib_s[1] = dot(cotx[0], wdn[other, :], 1, 1).astype(BF16)
    send(sib_s.at[1], sib_r.at[1], sib_ss.at[1], sib_rs.at[1], width=sibling)

    def merge(k, mine_half):
        arrived(sib_r.at[k], sib_rs.at[k])
        both = (mine_half + sib_r[k].astype(F32)).reshape(NZ, TB, FH)
        own[k] = both
        zs[k] = both.astype(BF16)
        scatter(over_z, zs.at[k], zr.at[k], [zh.at[k, 0], zh.at[k, 1]], z_ss.at[k], z_rs.at[k])

    def merge_pass(k):
        scatter_pass(
            over_z, own.at[k], zr.at[k], [zh.at[k, 0], zh.at[k, 1]], zc.at[k], z_ss.at[k], z_rs.at[k]
        )

    my_half = dot(leaning[...], wup[:, mine], 1, 0)
    merge(0, my_half[0:T])
    merge(1, dot(cotx[0], wdn[mine, :], 1, 1))

    total_row = jnp.transpose(jnp.broadcast_to(total, (T, EXTRA)))[0:1]
    spread_row = jnp.transpose(jnp.broadcast_to(spread, (T, EXTRA)))[0:1]
    for h, half in ((c, my_half), (1 - c, its_half)):
        lean = jnp.sum(half[T:], axis=0, keepdims=True)
        stat_s[h, 0:1, 0:T] = total_row
        stat_s[h, 1:2, 0:T] = spread_row
        for j in range(FH // 128):
            stat_s[h, 2 + j : 3 + j, :] = lean[:, j * 128 : (j + 1) * 128]

    def tell(k, carry):
        peer = lax.rem(w + k, NW)
        send(stat_s.at[lax.rem(peer, 2)], stat_r.at[k - 1], stat_ss, stat_rs, width=peer)
        return carry
    lax.fori_loop(1, NW, tell, 0)

    right, left = lax.rem(x + 1, NX), lax.rem(x + NX - 1, NX)
    first_rows, last_rows = pl.ds(0, T // 2), pl.ds(T // 2, T // 2)

    def spread_x(k, buf):
        send(buf.at[0], buf.at[1], x_ss.at[k], x_rs.at[k, 0], dp=right)
        send(buf.at[0], buf.at[NX - 1], x_ss.at[k], x_rs.at[k, 1], dp=left)

    def pass_x(k, buf):
        arrived(buf.at[1], x_rs.at[k, 0])
        send(buf.at[1, first_rows], buf.at[2, first_rows], x_ss.at[k], x_rs.at[k, 2], dp=right)
        arrived(buf.at[NX - 1], x_rs.at[k, 1])
        send(buf.at[NX - 1, last_rows], buf.at[2, last_rows], x_ss.at[k], x_rs.at[k, 3], dp=left)

    def end_x(k, buf):
        arrived(buf.at[2, first_rows], x_rs.at[k, 2])
        arrived(buf.at[2, last_rows], x_rs.at[k, 3])

    merge_pass(0)
    merge_pass(1)
    spread_x(0, cotx)

    arrived(stat_r, stat_rs)
    its = stat_r[...]
    my_stat = stat_s[c]
    sums, spreads = its[:, 0, :], its[:, 1, :]
    mean = (jnp.sum(sums, axis=0, keepdims=True) + my_stat[0:1]) * (1.0 / D)
    away, my_away = sums * (1.0 / DS) - mean, my_stat[0:1] * (1.0 / DS) - mean
    variance = (
        jnp.sum(spreads + DS * away * away, axis=0, keepdims=True) + my_stat[1:2] + DS * my_away * my_away
    ) * (1.0 / D)
    inv_std = lax.rsqrt(variance + 1e-06)
    mean_col = jnp.transpose(jnp.broadcast_to(mean[:, 0:T], (EXTRA, T)))
    std_col = jnp.transpose(jnp.broadcast_to(inv_std[:, 0:T], (EXTRA, T)))
    inv_col[...] = std_col
    aways = jnp.concatenate([away[:, 0:T], my_away[:, 0:T], jnp.zeros((EXTRA - NW, T), F32)], axis=0)
    away_col[...] = jnp.transpose(aways)
    token_rows = pl.ds(pl.multiple_of(z * TB, TB), TB)
    my_aways = away_col[token_rows, :]
    leans, shift = [], []
    for j in range(FH // 128):
        piece = [its[s, 2 + j : 3 + j, :] for s in range(NW - 1)] + [my_stat[2 + j : 3 + j, :]]
        leans.append(functools.reduce(jnp.add, piece))
        shift.append(functools.reduce(jnp.add, [my_aways[:, s : s + 1] * piece[s] for s in range(NW)]))
    lean_row = jnp.concatenate(leans, axis=1)
    shift = jnp.concatenate(shift, axis=1)

    def hand_over(k):
        return lambda block: send(block, block, rel_ss.at[k], rel_rs.at[k], width=sibling)

    pre_act = (scatter_sum(over_z, own.at[0], zr.at[0], z_rs.at[0]) + shift) * inv_col[token_rows, 0:1]
    below = 0.5 * (1.0 + lax.erf(pre_act * inv_root_two))
    hid[c, z] = (pre_act * below).astype(BF16)
    units, grads = hid.at[c], gp.at[c]
    gather(over_z, units, ag_ss.at[0], ag_rs.at[0])
    hand_over(0)(hid.at[c, z])
    slope = below + pre_act * jnp.exp(-0.5 * pre_act * pre_act) * inv_root_two_pi
    grad_hidden = scatter_sum(over_z, own.at[1], zr.at[1], z_rs.at[1])
    grad_pre = (grad_hidden * slope).astype(BF16)
    wide = grad_pre.astype(F32)
    gp[c, z, :, 0:FH] = grad_pre
    gp[c, z, :, FH:] = pack(
        jnp.sum(wide * lean_row, axis=1, keepdims=True), jnp.sum(wide * pre_act, axis=1, keepdims=True)
    )
    gather(over_z, grads, ag_ss.at[1], ag_rs.at[1])
    hand_over(1)(gp.at[c, z])

    for j in range(DS // 128):
        cols = slice(j * 128, (j + 1) * 128)
        normal = (tok[:, cols].astype(F32) - mean_col) * std_col
        normed[:, cols] = normal
        scx[0, :, cols] = (normal * g_all[:, cols]).astype(BF16)
    spread_x(1, scx)

    gather_pass(over_z, across_z, units, ag_ss.at[0], ag_rs.at[0], far_rs.at[0], hand_over(0))
    gather_near(over_z, units, ag_rs.at[0], hand_over(0))
    gather_pass(over_z, across_z, grads, ag_ss.at[1], ag_rs.at[1], far_rs.at[1], hand_over(1))
    gather_near(over_z, grads, ag_rs.at[1], hand_over(1))
    pass_x(0, cotx)

    block_of, _ = over_z
    near, far = (0, 1, -1, 2, -2), (3, -3, 4)

    half_ring = NY // 2
    slot = lax.rem(y, half_ring)

    def next_to(o):
        return lax.rem(y + o % NY, NY)

    def own_sums(k, part, got, result):
        arrived(got, y_rs.at[k])
        for side in range(2):
            block = lax.rem(y + side * half_ring, NY)
            summed = part[block] + jnp.sum(got[side].astype(F32), axis=0)
            result[lax.div(block, half_ring), lax.rem(block, half_ring)] = summed.astype(BF16)

    def from_owners(k, buf):
        both = buf.at[:, slot]
        for side, o in ((0, 1), (1, -1)):
            one = buf.at[side, slot]
            send(one, one, yag_ss.at[k], yag_rs.at[k, 2 + side], mlp=next_to(2 * o))
            send(both, both, yag_ss.at[k], yag_rs.at[k, side], mlp=next_to(o))

    def from_owners_end(k, buf):
        for side, o in ((0, -1), (1, 1)):
            arrived(buf.at[:, lax.rem(next_to(o), half_ring)], yag_rs.at[k, side])
            arrived(buf.at[side, lax.rem(next_to(2 * o), half_ring)], yag_rs.at[k, 2 + side])

    def gathered_near(k, buf):
        arrived(buf.at[1 - c, pl.ds(0, 5)], rel_rs.at[k])

    def gathered_far(k, buf):
        gather_far(over_z, buf.at[c], ag_rs.at[k], 4)
        gather_far(over_z, buf.at[1 - c], far_rs.at[k], 0)

    def rows_of(buf, h, blocks, lanes):
        return jnp.concatenate([buf[h, block_of(o), :, lanes] for o in blocks], axis=0)

    def to_owners(k, blocks, terms, part, sent, got):
        for i, o in enumerate(blocks):
            block = block_of(o)
            part[block] = terms[i * TB : (i + 1) * TB]
            sent[block] = terms[i * TB : (i + 1) * TB].astype(BF16)
            for side in range(2):
                owner = lax.rem(block + side * half_ring, NY)

                @pl.when(owner != y)
                def _():
                    place_there = got.at[side, lax.rem(owner - y + NY - 1, NY)]
                    send(sent.at[block], place_there, y_ss.at[k], y_rs.at[k], mlp=owner)

    def output_terms(blocks):
        units = slice(0, FH)
        term = dot(rows_of(hid, 0, blocks, units), wdn[0:FH, :], 1, 0)
        term = term + dot(rows_of(hid, 1, blocks, units), wdn[FH:, :], 1, 0)
        to_owners(0, blocks, term, part0, ys0, yr0)

    def gradient_terms(blocks):
        units, beside = slice(0, FH), slice(FH, FH + EXTRA)
        term = dot(rows_of(gp, 0, blocks, units), wup[:, 0:FH], 1, 1)
        term = term + dot(rows_of(gp, 1, blocks, units), wup[:, FH:], 1, 1)
        side = rows_of(gp, 0, blocks, beside).astype(F32) + rows_of(gp, 1, blocks, beside).astype(F32)
        first, second = unpack(side)
        tokens = [pl.ds(pl.multiple_of(block_of(o) * TB, TB), TB) for o in blocks]
        normal = jnp.concatenate([normed[rows, :] for rows in tokens], axis=0)
        scale = jnp.concatenate([inv_col[rows, 0:1] for rows in tokens], axis=0)
        corrected = scale * (
            term * gain_v[...].reshape(1, DS) - first * (1.0 / D) - normal * (second * (1.0 / D))
        )
        to_owners(1, blocks, corrected, part1, ys1, yr1)
        return jnp.sum((term * normal).reshape(len(blocks) * TB // 8, 8, DS), axis=0)

    my_blocks = pl.ds(pl.multiple_of(c * (NZ // 2), NZ // 2), NZ // 2)
    its_blocks = pl.ds(pl.multiple_of((1 - c) * (NZ // 2), NZ // 2), NZ // 2)

    def share(k, buf, dst):
        def one(o, carry):
            peer = lax.rem(x + o, NX)
            h, lanes = quarter(peer)
            send(buf.at[h, my_blocks, :, lanes], dst.at[o, my_blocks], q_ss.at[k], q_rs.at[k], dp=peer)
            return carry
        lax.fori_loop(1, NX, one, 0)
        h, lanes = quarter(x)
        dst[0] = buf[h, :, :, lanes]

    def join(k, dst):
        halves = dst.at[pl.ds(1, NX - 1), my_blocks]
        arrived(halves, q_rs.at[k])
        send(halves, halves, join_ss.at[k], join_rs.at[k], width=sibling)

    gathered_near(0, hid)
    output_terms(near)
    gathered_near(1, gp)
    gg_sum[...] = gradient_terms(near)
    gathered_far(0, hid)
    output_terms(far)
    share(0, hid, hx)
    gathered_far(1, gp)
    share(1, gp, gpx)
    gains = jnp.sum(gg_sum[...] + gradient_terms(far), axis=0, keepdims=True)
    rows = [gains[:, j * 128 : (j + 1) * 128] for j in range(DS // 128)]
    gg_s[...] = jnp.concatenate(rows + [jnp.zeros((8 - len(rows), 128), F32)], axis=0)

    def gain_x(o, carry):
        send(gg_s, ggx_r.at[o - 1], ggx_ss, ggx_rs, dp=lax.rem(x + o, NX))
        return carry
    lax.fori_loop(1, NX, gain_x, 0)
    pass_x(1, scx)
    join(0, hx)

    own_sums(0, part0, yr0, outv)
    from_owners(0, outv)

    arrived(ggx_r, ggx_rs)
    ggy_s[...] = gg_s[...] + jnp.sum(ggx_r[...], axis=0)

    def gain_y(o, carry):
        send(ggy_s, ggy_r.at[o - 1], ggy_ss, ggy_rs, mlp=lax.rem(y + o, NY))
        return carry
    lax.fori_loop(1, NY, gain_y, 0)

    own_sums(1, part1, yr1, gtv)
    from_owners(1, gtv)
    join(1, gpx)

    end_x(0, cotx)
    arrived(hx.at[pl.ds(1, NX - 1), its_blocks], join_rs.at[0])
    gdn[...] = dot(hx[...].reshape(NX * T, FQ), cotx[...].reshape(NX * T, DS), 0, 0)
    end_x(1, scx)
    arrived(gpx.at[pl.ds(1, NX - 1), its_blocks], join_rs.at[1])
    product = dot(scx[...].reshape(NX * T, DS), gpx[...].reshape(NX * T, FQ), 0, 0)
    pieces = FQ // 128
    for j in range(pieces):
        gup[pl.ds(j, DS, stride=pieces), :] = product[:, j * 128 : (j + 1) * 128]
    from_owners_end(0, outv)
    out[...] = outv[...].reshape(T, DS)
    from_owners_end(1, gtv)
    gt[...] = gtv[...].reshape(T, DS)
    arrived(ggy_r, ggy_rs)
    gains = ggy_s[...] + jnp.sum(ggy_r[...], axis=0)
    gg[...] = jnp.concatenate([gains[j : j + 1] for j in range(DS // 128)], axis=1).reshape(DS)

    for k in range(2):
        arrived(sib_s.at[k], sib_ss.at[k])
        arrived(zs.at[k, pl.ds(0, NZ - 1)], z_ss.at[k])
    arrived(stat_r, stat_ss)
    for k, buf in enumerate((hid, gp)):
        arrived(buf.at[:, pl.ds(0, 5)], ag_ss.at[k])
        arrived(buf.at[0, pl.ds(0, 5)], rel_ss.at[k])
    for k, buf in enumerate((cotx, scx)):
        arrived(buf.at[pl.ds(0, NX - 1)], x_ss.at[k])
    for k, buf in enumerate((hx, gpx)):
        arrived(buf.at[pl.ds(1, NX - 1), my_blocks], q_ss.at[k])
        arrived(buf.at[pl.ds(1, NX - 1), my_blocks], join_ss.at[k])
    arrived(yr0, y_ss.at[0])
    arrived(yr1, y_ss.at[1])
    arrived(outv.at[:, pl.ds(0, 3)], yag_ss.at[0])
    arrived(gtv.at[:, pl.ds(0, 3)], yag_ss.at[1])
    arrived(ggx_r, ggx_ss)
    arrived(ggy_r, ggy_ss)


def place(*refs):
    made, given, sems = refs[0:5], refs[5:10], refs[10]
    copies = [pltpu.make_async_copy(src, dst, sems.at[k]) for k, (src, dst) in enumerate(zip(made, given))]
    for copy in copies:
        copy.start()
    for copy in copies:
        copy.wait()


def solution(mesh):
    NX, NZ, NY = mesh.shape["dp"], mesh.shape["width"] // 2, mesh.shape["mlp"]

    def shards(tokens, gain, up_weight, down_weight, cotangent):
        T, DS = tokens.shape
        FS = up_weight.shape[1]
        FH, FQ = FS // 2, FS // NX
        vmem, dma = pltpu.VMEM, pltpu.SemaphoreType.DMA
        results = (
            jax.ShapeDtypeStruct((T, DS), BF16),
            jax.ShapeDtypeStruct((T, DS), BF16),
            jax.ShapeDtypeStruct((DS,), F32),
            jax.ShapeDtypeStruct((DS * FQ // 128, 128), F32),
            jax.ShapeDtypeStruct((FQ, DS), F32),
        )
        call = pl.pallas_call(
            functools.partial(kernel, (NX, NZ, NY, DS * 2 * NZ)),
            out_shape=results,
            in_specs=[pl.BlockSpec(memory_space=pltpu.HBM)] * 5,
            out_specs=[pl.BlockSpec(memory_space=pltpu.VMEM)] * 5,
            scratch_shapes=[
                vmem((T, DS), BF16), vmem((DS,), F32), vmem((DS, FS), BF16), vmem((FS, DS), BF16),
                vmem((NX, T, DS), BF16), vmem((NX, T, DS), BF16), vmem((T, DS), F32), vmem((T, EXTRA), F32),
                vmem((2, 8, 128), F32), vmem((2 * NZ - 1, 8, 128), F32),
                vmem((2, T, FH), BF16), vmem((2, T, FH), BF16), vmem((2, NZ, TB, FH), F32),
                vmem((2, NZ, TB, FH), BF16), vmem((2, 6, TB, FH), BF16),
                vmem((2, 2, TB, FH // 2), BF16), vmem((2, 2, TB, FH), BF16),
                vmem((T + TB, DS), BF16), vmem((T, EXTRA), F32),
                vmem((2, NZ, TB, FH), BF16), vmem((2, NZ, TB, FH + EXTRA), BF16),
                vmem((NX, NZ, TB, FQ), BF16), vmem((NX, NZ, TB, FQ), BF16),
                *(
                    shape
                    for _ in range(2)
                    for shape in (
                        vmem((NY, TB, DS), BF16), vmem((2, NY - 1, TB, DS), BF16), vmem((NY, TB, DS), F32),
                    )
                ),
                vmem((2, NY // 2, TB, DS), BF16), vmem((2, NY // 2, TB, DS), BF16),
                vmem((8, DS), F32), vmem((8, 128), F32), vmem((NX - 1, 8, 128), F32),
                vmem((8, 128), F32), vmem((NY - 1, 8, 128), F32),
                dma((5,)), dma((2,)), dma((2,)), dma, dma, dma((2,)), dma((2, 8)),
                dma((2,)), dma((2, 8)), dma((2, 4)), dma((2,)), dma((2,)),
                dma((2,)), dma((2, 4)), dma((2,)), dma((2,)), dma((2,)), dma((2,)),
                dma((2,)), dma((2,)), dma((2,)), dma((2, 4)), dma, dma, dma, dma,
            ],
            compiler_params=pltpu.CompilerParams(
                collective_id=0, has_side_effects=True, vmem_limit_bytes=48 * 1024 * 1024
            ),
            cost_estimate=pl.CostEstimate(
                flops=12 * T * DS * FS, bytes_accessed=4 * DS * FS + 8 * DS * FQ, transcendentals=2 * TB * FH
            ),
        )
        put = pl.pallas_call(
            place,
            out_shape=results,
            in_specs=[pl.BlockSpec(memory_space=pltpu.VMEM)] * 5,
            out_specs=[pl.BlockSpec(memory_space=pltpu.HBM)] * 5,
            scratch_shapes=[dma((5,))],
            compiler_params=pltpu.CompilerParams(vmem_limit_bytes=4 * 1024 * 1024),
        )
        output, grad_tokens, grad_gain, grad_up, grad_down = put(
            *call(*(pltpu.with_memory_space_constraint(a, pltpu.HBM) for a in (tokens, gain, up_weight, down_weight, cotangent)))
        )
        return output, grad_tokens, grad_gain, grad_up.reshape(DS, 1, FQ), grad_down[None, :, :]

    placed = (P("dp", "width"), P("width"), P("width", "mlp"), P("mlp", "width"), P("dp", "width"))
    return jax.shard_map(
        shards,
        mesh=mesh,
        in_specs=placed,
        out_specs=(
            P("dp", "width"),
            P("dp", "width"),
            P("width"),
            P("width", "mlp", "dp"),
            P("mlp", "dp", "width"),
        ),
        check_vma=False,
    )
```

```python
import functools

import jax
import jax.numpy as jnp
from jax import lax
from jax.experimental import pallas as pl
from jax.experimental.pallas import tpu as pltpu
from jax.sharding import PartitionSpec as P

MESH = pl.DeviceIdType.MESH
F32, BF16 = jnp.float32, jnp.bfloat16
TB = 16
EXTRA = 128

inv_root_two = 0.7071067811865476
inv_root_two_pi = 0.3989422804014327


def dot(left, right, left_dim, right_dim):
    return lax.dot_general(
        left, right, (((left_dim,), (right_dim,)), ((), ())), preferred_element_type=F32
    )


def pack(first, second):
    lane = lax.broadcasted_iota(jnp.int32, (first.shape[0], EXTRA), 1)
    high_one, high_two = first.astype(BF16).astype(F32), second.astype(BF16).astype(F32)
    held = jnp.where(lane == 0, high_one, 0.0)
    held = jnp.where(lane == 1, high_two, held)
    held = jnp.where(lane == 2, first - high_one, held)
    held = jnp.where(lane == 3, second - high_two, held)
    return held.astype(BF16)


def unpack(held):
    return held[:, 0:1] + held[:, 2:3], held[:, 1:2] + held[:, 3:4]


def send(src, dst, ss, rs, **where):
    pltpu.make_async_remote_copy(
        src_ref=src, dst_ref=dst, send_sem=ss, recv_sem=rs, device_id=where, device_id_type=MESH
    ).start()


def arrived(ref, sem):
    pltpu.make_async_copy(ref, ref, sem).wait()


def ring(axis, me, device=lambda position: position):
    def at(o):
        return lax.rem(me + o % 8, 8)
    return at, lambda o: {axis: device(at(o))}


def lanes_of(block, side):
    cut = block.shape[-1] // 256 * 128
    return block.at[:, pl.ds(0, cut) if side == 0 else pl.ds(cut, block.shape[-1] - cut)]


def scatter(to_whom, terms, got, halves, ss, rs):
    at, to = to_whom
    for side, o in ((0, 1), (1, -1)):
        send(terms.at[at(3 * o)], got.at[4 + side], ss, rs.at[4 + side], **to(o))
    for side, o in ((0, 2), (1, -2)):
        send(lanes_of(terms.at[at(4)], side), halves[side], ss, rs.at[6 + side], **to(o))
    for side, o in ((0, 1), (1, -1)):
        send(terms.at[at(o)], got.at[side], ss, rs.at[side], **to(o))


def scatter_pass(to_whom, own, got, halves, sums, ss, rs):
    at, to = to_whom
    for side, o in ((0, 2), (1, -2)):
        arrived(got.at[4 + side], rs.at[4 + side])
        arrived(halves[side], rs.at[6 + side])
        term = own[at(o)] + got[4 + side].astype(F32)
        half = halves[side][...].astype(F32)
        cut = term.shape[-1] // 256 * 128
        low, high = term[:, 0:cut], term[:, cut:]
        sums[side, :, 0:cut] = (low + half if side == 0 else low).astype(BF16)
        sums[side, :, cut:] = (high if side == 0 else high + half).astype(BF16)
        send(sums.at[side], got.at[2 + side], ss, rs.at[2 + side], **to(o))


def scatter_sum(to_whom, own, got, rs):
    at, _ = to_whom
    for slot in range(4):
        arrived(got.at[slot], rs.at[slot])
    return own[at(0)] + jnp.sum(got[0:4].astype(F32), axis=0)


def gather(to_whom, buf, ss, rs):
    at, to = to_whom
    block = buf.at[at(0)]
    for o, slot in ((2, 2), (-2, 3), (1, 0), (-1, 1)):
        send(block, block, ss, rs.at[slot], **to(o))


def gather_pass(here, buf, ss, sems, use):
    at, _ = here
    for side, o in ((0, 1), (1, -1)):
        block = buf.at[at(-2 * o)]
        arrived(block, sems[0][1].at[2 + side])
        half = lanes_of(block, side)
        for (_, to), there, first in sems:
            send(block, block, ss, there.at[first + side], **to(o))
            send(half, half, ss, there.at[first + 2 + side], **to(2 * o))
        use(block)


def gather_near(here, buf, rs, use):
    at, _ = here
    for side, o in ((0, -1), (1, 1)):
        arrived(buf.at[at(o)], rs.at[side])
        use(buf.at[at(o)])


def gather_far(here, buf, sems, first):
    at, _ = here
    for side, o in ((0, -3), (1, 3)):
        arrived(buf.at[at(o)], sems.at[first + side])
        arrived(lanes_of(buf.at[at(4)], side), sems.at[first + 2 + side])


def kernel(
    sizes, tok_h, gain_h, wup_h, wdn_h, cot_h, out, gt, gg, gup, gdn,
    tok, gain_v, wup, wdn, cotx, scx, normed, inv_col,
    stat_s, stat_r,
    sib_s, sib_r, own, zs, zr, zh, zc, leaning, away_col,
    hid, gp, hx, gpx,
    ys0, yr0, part0, ys1, yr1, part1,
    outv, gtv,
    gg_sum, gg_s, ggx_r, ggy_s, ggy_r,
    ld, sib_ss, sib_rs, stat_ss, stat_rs, z_ss, z_rs, ag_ss, ag_rs, far_rs, rel_ss, rel_rs,
    x_ss, x_rs, q_ss, q_rs, join_ss, join_rs, y_ss, y_rs, yag_ss, yag_rs, ggx_ss, ggx_rs, ggy_ss, ggy_rs,
):
    NX, NZ, NY, D = sizes
    T, DS = tok.shape
    TY = T // NY
    FS = wup.shape[1]
    FH, FQ = FS // 2, FS // NX
    NW = 2 * NZ
    x, w, y = lax.axis_index("dp"), lax.axis_index("width"), lax.axis_index("mlp")
    z = lax.div(w, 2)
    c = w - 2 * z
    sibling = 2 * z + 1 - c

    over_z = ring("width", z, lambda position: 2 * position + c)
    across_z = ring("width", z, lambda position: 2 * position + 1 - c)

    def quarter(q):
        first = q * FQ
        h = lax.div(first, FH)
        return h, pl.ds(pl.multiple_of(first - h * FH, FQ), FQ)

    mine = pl.ds(pl.multiple_of(c * FH, FH), FH)
    other = pl.ds(pl.multiple_of(FH - c * FH, FH), FH)

    barrier = pltpu.get_barrier_semaphore()

    def greet(axis, me, n):
        def one(i, carry):
            step = lax.div(i + 1, 2)
            o = n // 2 + jnp.where(lax.rem(i, 2) == 1, step, -step)
            pl.semaphore_signal(barrier, inc=1, device_id={axis: lax.rem(me + o, n)}, device_id_type=MESH)
            return carry
        lax.fori_loop(0, n - 1, one, 0)

    greet("mlp", y, NY)
    greet("width", w, NW)
    greet("dp", x, NX)

    loads = [
        pltpu.make_async_copy(tok_h, tok, ld.at[0]),
        pltpu.make_async_copy(gain_h, gain_v, ld.at[1]),
        pltpu.make_async_copy(wup_h.at[:, other], wup.at[:, other], ld.at[2]),
        pltpu.make_async_copy(cot_h, cotx.at[0], ld.at[3]),
        pltpu.make_async_copy(wdn_h.at[other], wdn.at[other], ld.at[4]),
        pltpu.make_async_copy(wup_h.at[:, mine], wup.at[:, mine], ld.at[5]),
        pltpu.make_async_copy(wdn_h.at[mine], wdn.at[mine], ld.at[6]),
    ]
    for load in loads:
        load.start()

    loads[0].wait()
    loads[1].wait()
    values = tok[...].astype(F32)
    total = jnp.sum(values, axis=1, keepdims=True)
    shifted = values - total * (1.0 / DS)
    g_all = gain_v[...].reshape(1, DS)
    leaning[0:T] = (shifted * g_all).astype(BF16)
    row = lax.broadcasted_iota(jnp.int32, (TB, DS), 0)
    g_one = g_all.astype(BF16).astype(F32)
    g_two = (g_all - g_one).astype(BF16).astype(F32)
    g_rows = jnp.where(row == 0, g_one, jnp.where(row == 1, g_two, jnp.where(row == 2, g_all - g_one - g_two, 0.0)))
    leaning[T:] = g_rows.astype(BF16)
    loads[2].wait()
    its_half = dot(leaning[...], wup[:, other], 1, 0)
    sib_s[0] = its_half[0:T].astype(BF16)

    loads[3].wait()
    loads[4].wait()
    sib_s[1] = dot(cotx[0], wdn[other, :], 1, 1).astype(BF16)
    loads[5].wait()
    my_half = dot(leaning[...], wup[:, mine], 1, 0)
    own[0] = my_half[0:T].reshape(NZ, TB, FH)
    loads[6].wait()
    own[1] = dot(cotx[0], wdn[mine, :], 1, 1).reshape(NZ, TB, FH)

    shifted = tok[...].astype(F32) - total * (1.0 / DS)
    spread = jnp.sum(shifted * shifted, axis=1, keepdims=True)
    total_row = jnp.transpose(jnp.broadcast_to(total, (T, EXTRA)))[0:1]
    spread_row = jnp.transpose(jnp.broadcast_to(spread, (T, EXTRA)))[0:1]
    for h, half in ((c, my_half), (1 - c, its_half)):
        lean = jnp.sum(half[T:], axis=0, keepdims=True)
        stat_s[h, 0:1, 0:T] = total_row
        stat_s[h, 1:2, 0:T] = spread_row
        for j in range(FH // 128):
            stat_s[h, 2 + j : 3 + j, :] = lean[:, j * 128 : (j + 1) * 128]

    pl.semaphore_wait(barrier, NW - 1 + NY - 1 + NX - 1)
    for k in range(2):
        send(sib_s.at[k], sib_r.at[k], sib_ss.at[k], sib_rs.at[k], width=sibling)

    def tell(k, carry):
        peer = lax.rem(w + k, NW)
        send(stat_s.at[lax.rem(peer, 2)], stat_r.at[k - 1], stat_ss, stat_rs, width=peer)
        return carry
    lax.fori_loop(1, NW, tell, 0)

    def merge(k):
        arrived(sib_r.at[k], sib_rs.at[k])
        both = own[k] + sib_r[k].astype(F32).reshape(NZ, TB, FH)
        own[k] = both
        zs[k] = both.astype(BF16)
        scatter(over_z, zs.at[k], zr.at[k], [zh.at[k, 0], zh.at[k, 1]], z_ss.at[k], z_rs.at[k])

    def merge_pass(k):
        scatter_pass(
            over_z, own.at[k], zr.at[k], [zh.at[k, 0], zh.at[k, 1]], zc.at[k], z_ss.at[k], z_rs.at[k]
        )

    merge(0)
    merge(1)

    right, left = lax.rem(x + 1, NX), lax.rem(x + NX - 1, NX)
    first_rows, last_rows = pl.ds(0, T // 2), pl.ds(T // 2, T // 2)

    def spread_x(k, buf):
        send(buf.at[0], buf.at[1], x_ss.at[k], x_rs.at[k, 0], dp=right)
        send(buf.at[0], buf.at[NX - 1], x_ss.at[k], x_rs.at[k, 1], dp=left)

    def pass_x(k, buf):
        arrived(buf.at[1], x_rs.at[k, 0])
        send(buf.at[1, first_rows], buf.at[2, first_rows], x_ss.at[k], x_rs.at[k, 2], dp=right)
        arrived(buf.at[NX - 1], x_rs.at[k, 1])
        send(buf.at[NX - 1, last_rows], buf.at[2, last_rows], x_ss.at[k], x_rs.at[k, 3], dp=left)

    def end_x(k, buf):
        arrived(buf.at[2, first_rows], x_rs.at[k, 2])
        arrived(buf.at[2, last_rows], x_rs.at[k, 3])

    spread_x(0, cotx)
    merge_pass(0)
    merge_pass(1)

    arrived(stat_r, stat_rs)
    its = stat_r[...]
    my_stat = stat_s[c]
    sums, spreads = its[:, 0, :], its[:, 1, :]
    mean = (jnp.sum(sums, axis=0, keepdims=True) + my_stat[0:1]) * (1.0 / D)
    away, my_away = sums * (1.0 / DS) - mean, my_stat[0:1] * (1.0 / DS) - mean
    variance = (
        jnp.sum(spreads + DS * away * away, axis=0, keepdims=True) + my_stat[1:2] + DS * my_away * my_away
    ) * (1.0 / D)
    inv_std = lax.rsqrt(variance + 1e-06)
    mean_col = jnp.transpose(jnp.broadcast_to(mean[:, 0:T], (EXTRA, T)))
    std_col = jnp.transpose(jnp.broadcast_to(inv_std[:, 0:T], (EXTRA, T)))
    inv_col[...] = std_col
    aways = jnp.concatenate([away[:, 0:T], my_away[:, 0:T], jnp.zeros((EXTRA - NW, T), F32)], axis=0)
    away_col[...] = jnp.transpose(aways)
    token_rows = pl.ds(pl.multiple_of(z * TB, TB), TB)
    my_aways = away_col[token_rows, :]
    leans, shift = [], []
    for j in range(FH // 128):
        piece = [its[s, 2 + j : 3 + j, :] for s in range(NW - 1)] + [my_stat[2 + j : 3 + j, :]]
        leans.append(functools.reduce(jnp.add, piece))
        shift.append(functools.reduce(jnp.add, [my_aways[:, s : s + 1] * piece[s] for s in range(NW)]))
    lean_row = jnp.concatenate(leans, axis=1)
    shift = jnp.concatenate(shift, axis=1)

    def hand_over(k):
        return lambda block: send(block, block, rel_ss.at[k], rel_rs.at[k], width=sibling)

    pre_act = (scatter_sum(over_z, own.at[0], zr.at[0], z_rs.at[0]) + shift) * inv_col[token_rows, 0:1]
    below = 0.5 * (1.0 + lax.erf(pre_act * inv_root_two))
    hid[c, z] = (pre_act * below).astype(BF16)
    units, grads = hid.at[c], gp.at[c]
    gather(over_z, units, ag_ss.at[0], ag_rs.at[0])
    hand_over(0)(hid.at[c, z])
    slope = below + pre_act * jnp.exp(-0.5 * pre_act * pre_act) * inv_root_two_pi
    grad_hidden = scatter_sum(over_z, own.at[1], zr.at[1], z_rs.at[1])
    grad_pre = (grad_hidden * slope).astype(BF16)
    wide = grad_pre.astype(F32)
    gp[c, z, :, 0:FH] = grad_pre
    gp[c, z, :, FH:] = pack(
        jnp.sum(wide * lean_row, axis=1, keepdims=True), jnp.sum(wide * pre_act, axis=1, keepdims=True)
    )
    gather(over_z, grads, ag_ss.at[1], ag_rs.at[1])
    hand_over(1)(gp.at[c, z])

    for j in range(DS // 128):
        cols = slice(j * 128, (j + 1) * 128)
        normal = (tok[:, cols].astype(F32) - mean_col) * std_col
        normed[:, cols] = normal
        scx[0, :, cols] = (normal * g_all[:, cols]).astype(BF16)
    spread_x(1, scx)

    gather_pass(over_z, units, ag_ss.at[0], [(over_z, ag_rs.at[0], 4)], hand_over(0))
    gather_near(over_z, units, ag_rs.at[0], hand_over(0))
    gather_pass(
        over_z, grads, ag_ss.at[1], [(over_z, ag_rs.at[1], 4), (across_z, far_rs, 0)], hand_over(1)
    )
    gather_near(over_z, grads, ag_rs.at[1], hand_over(1))
    pass_x(0, cotx)

    block_of, _ = over_z
    near, far = (0, 1, -1, 2, -2), (3, -3, 4)

    half_ring = NY // 2
    slot = lax.rem(y, half_ring)

    def next_to(o):
        return lax.rem(y + o % NY, NY)

    def own_sums(k, part, got, result):
        arrived(got, y_rs.at[k])
        for side in range(2):
            block = lax.rem(y + side * half_ring, NY)
            summed = part[block] + jnp.sum(got[side].astype(F32), axis=0)
            result[lax.div(block, half_ring), lax.rem(block, half_ring)] = summed.astype(BF16)

    def from_owners(k, buf):
        both = buf.at[:, slot]
        for side, o in ((0, 1), (1, -1)):
            one = buf.at[side, slot]
            send(one, one, yag_ss.at[k], yag_rs.at[k, 2 + side], mlp=next_to(2 * o))
            send(both, both, yag_ss.at[k], yag_rs.at[k, side], mlp=next_to(o))

    def from_owners_end(k, buf):
        for side, o in ((0, -1), (1, 1)):
            arrived(buf.at[:, lax.rem(next_to(o), half_ring)], yag_rs.at[k, side])
            arrived(buf.at[side, lax.rem(next_to(2 * o), half_ring)], yag_rs.at[k, 2 + side])

    def rows_of(buf, h, blocks, lanes):
        return jnp.concatenate([buf[h, block_of(o), :, lanes] for o in blocks], axis=0)

    def to_owners(k, blocks, terms, part, sent, got):
        for i, o in enumerate(blocks):
            block = block_of(o)
            part[block] = terms[i * TB : (i + 1) * TB]
            sent[block] = terms[i * TB : (i + 1) * TB].astype(BF16)
            for side in range(2):
                owner = lax.rem(block + side * half_ring, NY)

                @pl.when(owner != y)
                def _():
                    place_there = got.at[side, lax.rem(owner - y + NY - 1, NY)]
                    send(sent.at[block], place_there, y_ss.at[k], y_rs.at[k], mlp=owner)

    def output_terms(blocks):
        units = slice(0, FH)
        term = dot(rows_of(hid, 0, blocks, units), wdn[0:FH, :], 1, 0)
        term = term + dot(rows_of(hid, 1, blocks, units), wdn[FH:, :], 1, 0)
        to_owners(0, blocks, term, part0, ys0, yr0)

    def gradient_terms(blocks):
        units, beside = slice(0, FH), slice(FH, FH + EXTRA)
        term = dot(rows_of(gp, 0, blocks, units), wup[:, 0:FH], 1, 1)
        term = term + dot(rows_of(gp, 1, blocks, units), wup[:, FH:], 1, 1)
        side = rows_of(gp, 0, blocks, beside).astype(F32) + rows_of(gp, 1, blocks, beside).astype(F32)
        first, second = unpack(side)
        tokens = [pl.ds(pl.multiple_of(block_of(o) * TB, TB), TB) for o in blocks]
        normal = jnp.concatenate([normed[rows, :] for rows in tokens], axis=0)
        scale = jnp.concatenate([inv_col[rows, 0:1] for rows in tokens], axis=0)
        corrected = scale * (
            term * gain_v[...].reshape(1, DS) - first * (1.0 / D) - normal * (second * (1.0 / D))
        )
        to_owners(1, blocks, corrected, part1, ys1, yr1)
        return jnp.sum((term * normal).reshape(len(blocks) * TB // 8, 8, DS), axis=0)

    my_blocks = pl.ds(pl.multiple_of(c * (NZ // 2), NZ // 2), NZ // 2)
    its_blocks = pl.ds(pl.multiple_of((1 - c) * (NZ // 2), NZ // 2), NZ // 2)

    def share(k, buf, dst):
        def one(o, carry):
            peer = lax.rem(x + o, NX)
            h, lanes = quarter(peer)
            send(buf.at[h, my_blocks, :, lanes], dst.at[o, my_blocks], q_ss.at[k], q_rs.at[k], dp=peer)
            return carry
        lax.fori_loop(1, NX, one, 0)
        h, lanes = quarter(x)
        dst[0] = buf[h, :, :, lanes]

    def join(k, dst):
        halves = dst.at[pl.ds(1, NX - 1), my_blocks]
        arrived(halves, q_rs.at[k])
        send(halves, halves, join_ss.at[k], join_rs.at[k], width=sibling)

    arrived(hid.at[1 - c, pl.ds(0, 5)], rel_rs.at[0])
    output_terms(near)
    gather_far(over_z, units, ag_rs.at[0], 4)
    for o in far:
        block = hid.at[c, block_of(o)]
        send(block, block, rel_ss.at[0], rel_rs.at[2], width=sibling)
    arrived(gp.at[1 - c, pl.ds(0, 5)], rel_rs.at[1])
    gg_sum[...] = gradient_terms(near)
    arrived(hid.at[1 - c, pl.ds(0, 3)], rel_rs.at[2])
    output_terms(far)
    share(0, hid, hx)
    gather_far(over_z, grads, ag_rs.at[1], 4)
    gather_far(over_z, gp.at[1 - c], far_rs, 0)
    gains = gg_sum[...] + gradient_terms(far)
    share(1, gp, gpx)
    gains = jnp.sum(gains, axis=0, keepdims=True)
    rows = [gains[:, j * 128 : (j + 1) * 128] for j in range(DS // 128)]
    gg_s[...] = jnp.concatenate(rows + [jnp.zeros((8 - len(rows), 128), F32)], axis=0)

    def gain_x(o, carry):
        send(gg_s, ggx_r.at[o - 1], ggx_ss, ggx_rs, dp=lax.rem(x + o, NX))
        return carry
    lax.fori_loop(1, NX, gain_x, 0)
    pass_x(1, scx)
    join(0, hx)

    own_sums(0, part0, yr0, outv)
    from_owners(0, outv)

    arrived(ggx_r, ggx_rs)
    ggy_s[...] = gg_s[...] + jnp.sum(ggx_r[...], axis=0)

    def gain_y(o, carry):
        send(ggy_s, ggy_r.at[o - 1], ggy_ss, ggy_rs, mlp=lax.rem(y + o, NY))
        return carry
    lax.fori_loop(1, NY, gain_y, 0)

    join(1, gpx)

    end_x(0, cotx)
    arrived(hx.at[pl.ds(1, NX - 1), its_blocks], join_rs.at[0])
    gdn[...] = dot(hx[...].reshape(NX * T, FQ), cotx[...].reshape(NX * T, DS), 0, 0)
    own_sums(1, part1, yr1, gtv)
    from_owners(1, gtv)
    end_x(1, scx)
    arrived(gpx.at[pl.ds(1, NX - 1), its_blocks], join_rs.at[1])
    product = dot(scx[...].reshape(NX * T, DS), gpx[...].reshape(NX * T, FQ), 0, 0)
    pieces = FQ // 128
    for j in range(pieces):
        gup[pl.ds(j, DS, stride=pieces), :] = product[:, j * 128 : (j + 1) * 128]
    for k in range(2):
        arrived(sib_s.at[k], sib_ss.at[k])
        arrived(zs.at[k, pl.ds(0, NZ - 1)], z_ss.at[k])
    arrived(stat_r, stat_ss)
    arrived(hid.at[0, pl.ds(0, NZ - 1)], ag_ss.at[0])
    arrived(hid.at[0], rel_ss.at[0])
    arrived(gp.at[:, pl.ds(0, 5)], ag_ss.at[1])
    arrived(gp.at[0, pl.ds(0, 5)], rel_ss.at[1])
    for k, buf in enumerate((cotx, scx)):
        arrived(buf.at[pl.ds(0, NX - 1)], x_ss.at[k])
    for k, buf in enumerate((hx, gpx)):
        arrived(buf.at[pl.ds(1, NX - 1), my_blocks], q_ss.at[k])
        arrived(buf.at[pl.ds(1, NX - 1), my_blocks], join_ss.at[k])
    arrived(yr0, y_ss.at[0])
    arrived(yr1, y_ss.at[1])
    arrived(outv.at[:, pl.ds(0, 3)], yag_ss.at[0])
    arrived(ggx_r, ggx_ss)

    from_owners_end(0, outv)
    out[...] = outv[...].reshape(T, DS)
    from_owners_end(1, gtv)
    gt[...] = gtv[...].reshape(T, DS)
    arrived(ggy_r, ggy_rs)
    gains = ggy_s[...] + jnp.sum(ggy_r[...], axis=0)
    gg[...] = jnp.concatenate([gains[j : j + 1] for j in range(DS // 128)], axis=1).reshape(DS)
    arrived(gtv.at[:, pl.ds(0, 3)], yag_ss.at[1])
    arrived(ggy_r, ggy_ss)


def place(*refs):
    made, given, sems = refs[0:5], refs[5:10], refs[10]
    copies = [pltpu.make_async_copy(src, dst, sems.at[k]) for k, (src, dst) in enumerate(zip(made, given))]
    for copy in copies:
        copy.start()
    for copy in copies:
        copy.wait()


def solution(mesh):
    NX, NZ, NY = mesh.shape["dp"], mesh.shape["width"] // 2, mesh.shape["mlp"]

    def shards(tokens, gain, up_weight, down_weight, cotangent):
        T, DS = tokens.shape
        FS = up_weight.shape[1]
        FH, FQ = FS // 2, FS // NX
        vmem, dma = pltpu.VMEM, pltpu.SemaphoreType.DMA
        results = (
            jax.ShapeDtypeStruct((T, DS), BF16),
            jax.ShapeDtypeStruct((T, DS), BF16),
            jax.ShapeDtypeStruct((DS,), F32),
            jax.ShapeDtypeStruct((DS * FQ // 128, 128), F32),
            jax.ShapeDtypeStruct((FQ, DS), F32),
        )
        call = pl.pallas_call(
            functools.partial(kernel, (NX, NZ, NY, DS * 2 * NZ)),
            out_shape=results,
            in_specs=[pl.BlockSpec(memory_space=pltpu.HBM)] * 5,
            out_specs=[pl.BlockSpec(memory_space=pltpu.VMEM)] * 5,
            scratch_shapes=[
                vmem((T, DS), BF16), vmem((DS,), F32), vmem((DS, FS), BF16), vmem((FS, DS), BF16),
                vmem((NX, T, DS), BF16), vmem((NX, T, DS), BF16), vmem((T, DS), F32), vmem((T, EXTRA), F32),
                vmem((2, 8, 128), F32), vmem((2 * NZ - 1, 8, 128), F32),
                vmem((2, T, FH), BF16), vmem((2, T, FH), BF16), vmem((2, NZ, TB, FH), F32),
                vmem((2, NZ, TB, FH), BF16), vmem((2, 6, TB, FH), BF16),
                vmem((2, 2, TB, FH // 2), BF16), vmem((2, 2, TB, FH), BF16),
                vmem((T + TB, DS), BF16), vmem((T, EXTRA), F32),
                vmem((2, NZ, TB, FH), BF16), vmem((2, NZ, TB, FH + EXTRA), BF16),
                vmem((NX, NZ, TB, FQ), BF16), vmem((NX, NZ, TB, FQ), BF16),
                *(
                    shape
                    for _ in range(2)
                    for shape in (
                        vmem((NY, TB, DS), BF16), vmem((2, NY - 1, TB, DS), BF16), vmem((NY, TB, DS), F32),
                    )
                ),
                vmem((2, NY // 2, TB, DS), BF16), vmem((2, NY // 2, TB, DS), BF16),
                vmem((8, DS), F32), vmem((8, 128), F32), vmem((NX - 1, 8, 128), F32),
                vmem((8, 128), F32), vmem((NY - 1, 8, 128), F32),
                dma((7,)), dma((2,)), dma((2,)), dma, dma, dma((2,)), dma((2, 8)),
                dma((2,)), dma((2, 8)), dma((4,)), dma((2,)), dma((3,)),
                dma((2,)), dma((2, 4)), dma((2,)), dma((2,)), dma((2,)), dma((2,)),
                dma((2,)), dma((2,)), dma((2,)), dma((2, 4)), dma, dma, dma, dma,
            ],
            compiler_params=pltpu.CompilerParams(
                collective_id=0, has_side_effects=True, vmem_limit_bytes=48 * 1024 * 1024
            ),
            cost_estimate=pl.CostEstimate(
                flops=12 * T * DS * FS, bytes_accessed=4 * DS * FS + 8 * DS * FQ, transcendentals=2 * TB * FH
            ),
        )
        put = pl.pallas_call(
            place,
            out_shape=results,
            in_specs=[pl.BlockSpec(memory_space=pltpu.VMEM)] * 5,
            out_specs=[pl.BlockSpec(memory_space=pltpu.HBM)] * 5,
            scratch_shapes=[dma((5,))],
            compiler_params=pltpu.CompilerParams(vmem_limit_bytes=4 * 1024 * 1024),
        )
        output, grad_tokens, grad_gain, grad_up, grad_down = put(
            *call(*(pltpu.with_memory_space_constraint(a, pltpu.HBM) for a in (tokens, gain, up_weight, down_weight, cotangent)))
        )
        return output, grad_tokens, grad_gain, grad_up.reshape(DS, 1, FQ), grad_down[None, :, :]

    placed = (P("dp", "width"), P("width"), P("width", "mlp"), P("mlp", "width"), P("dp", "width"))
    return jax.shard_map(
        shards,
        mesh=mesh,
        in_specs=placed,
        out_specs=(
            P("dp", "width"),
            P("dp", "width"),
            P("width"),
            P("width", "mlp", "dp"),
            P("mlp", "dp", "width"),
        ),
        check_vma=False,
    )
```

```python
import functools

import jax
import jax.numpy as jnp
from jax import lax
from jax.experimental import pallas as pl
from jax.experimental.pallas import tpu as pltpu
from jax.sharding import PartitionSpec as P

MESH = pl.DeviceIdType.MESH
F32, BF16 = jnp.float32, jnp.bfloat16
TB = 16
EXTRA = 128

inv_root_two = 0.7071067811865476
inv_root_two_pi = 0.3989422804014327


def dot(left, right, left_dim, right_dim):
    return lax.dot_general(
        left, right, (((left_dim,), (right_dim,)), ((), ())), preferred_element_type=F32
    )


def pack(first, second):
    lane = lax.broadcasted_iota(jnp.int32, (first.shape[0], EXTRA), 1)
    high_one, high_two = first.astype(BF16).astype(F32), second.astype(BF16).astype(F32)
    held = jnp.where(lane == 0, high_one, 0.0)
    held = jnp.where(lane == 1, high_two, held)
    held = jnp.where(lane == 2, first - high_one, held)
    held = jnp.where(lane == 3, second - high_two, held)
    return held.astype(BF16)


def unpack(held):
    return held[:, 0:1] + held[:, 2:3], held[:, 1:2] + held[:, 3:4]


def send(src, dst, ss, rs, **where):
    pltpu.make_async_remote_copy(
        src_ref=src, dst_ref=dst, send_sem=ss, recv_sem=rs, device_id=where, device_id_type=MESH
    ).start()


def arrived(ref, sem):
    pltpu.make_async_copy(ref, ref, sem).wait()


def ring(axis, me, device=lambda position: position):
    def at(o):
        return lax.rem(me + o % 8, 8)
    return at, lambda o: {axis: device(at(o))}


def lanes_of(block, side):
    cut = block.shape[-1] // 256 * 128
    return block.at[:, pl.ds(0, cut) if side == 0 else pl.ds(cut, block.shape[-1] - cut)]


def scatter(to_whom, terms, got, halves, ss, rs):
    at, to = to_whom
    for side, o in ((0, 1), (1, -1)):
        send(terms.at[at(3 * o)], got.at[4 + side], ss, rs.at[4 + side], **to(o))
    for side, o in ((0, 2), (1, -2)):
        send(lanes_of(terms.at[at(4)], side), halves[side], ss, rs.at[6 + side], **to(o))
    for side, o in ((0, 1), (1, -1)):
        send(terms.at[at(o)], got.at[side], ss, rs.at[side], **to(o))


def scatter_pass(to_whom, own, got, halves, sums, ss, rs):
    at, to = to_whom
    for side, o in ((0, 2), (1, -2)):
        arrived(got.at[4 + side], rs.at[4 + side])
        arrived(halves[side], rs.at[6 + side])
        term = own[at(o)] + got[4 + side].astype(F32)
        half = halves[side][...].astype(F32)
        cut = term.shape[-1] // 256 * 128
        low, high = term[:, 0:cut], term[:, cut:]
        sums[side, :, 0:cut] = (low + half if side == 0 else low).astype(BF16)
        sums[side, :, cut:] = (high if side == 0 else high + half).astype(BF16)
        send(sums.at[side], got.at[2 + side], ss, rs.at[2 + side], **to(o))


def scatter_sum(to_whom, own, got, rs):
    at, _ = to_whom
    for slot in range(4):
        arrived(got.at[slot], rs.at[slot])
    return own[at(0)] + jnp.sum(got[0:4].astype(F32), axis=0)


def gather(to_whom, buf, ss, rs):
    at, to = to_whom
    block = buf.at[at(0)]
    for o, slot in ((2, 2), (-2, 3), (1, 0), (-1, 1)):
        send(block, block, ss, rs.at[slot], **to(o))


def gather_pass(here, buf, ss, sems, use):
    at, _ = here
    for side, o in ((0, 1), (1, -1)):
        block = buf.at[at(-2 * o)]
        arrived(block, sems[0][1].at[2 + side])
        half = lanes_of(block, side)
        for (_, to), there, first in sems:
            send(block, block, ss, there.at[first + side], **to(o))
            send(half, half, ss, there.at[first + 2 + side], **to(2 * o))
        use(block)


def gather_near(here, buf, rs, use):
    at, _ = here
    for side, o in ((0, -1), (1, 1)):
        arrived(buf.at[at(o)], rs.at[side])
        use(buf.at[at(o)])


def gather_far(here, buf, sems, first):
    at, _ = here
    for side, o in ((0, -3), (1, 3)):
        arrived(buf.at[at(o)], sems.at[first + side])
        arrived(lanes_of(buf.at[at(4)], side), sems.at[first + 2 + side])


def kernel(
    sizes, tok_h, gain_h, wup_h, wdn_h, cot_h, out, gt, gg, gup, gdn,
    tok, gain_v, wup, wdn, cotx, scx, normed, inv_col,
    stat_s, stat_r,
    sib_s, sib_r, own, zs, zr, zh, zc, leaning, away_col,
    hid, gp, hx, gpx,
    ys0, yr0, part0, ys1, yr1, part1,
    outv, gtv,
    gg_sum, gg_s, ggx_r, ggy_s, ggy_r,
    ld, sib_ss, sib_rs, stat_ss, stat_rs, z_ss, z_rs, ag_ss, ag_rs, far_rs, rel_ss, rel_rs,
    x_ss, x_rs, q_ss, q_rs, join_ss, join_rs, y_ss, y_rs, yag_ss, yag_rs, ggx_ss, ggx_rs, ggy_ss, ggy_rs,
    known, all_known,
):
    NX, NZ, NY, D = sizes
    T, DS = tok.shape
    TY = T // NY
    FS = wup.shape[1]
    FH, FQ = FS // 2, FS // NX
    NW = 2 * NZ
    x, w, y = lax.axis_index("dp"), lax.axis_index("width"), lax.axis_index("mlp")
    z = lax.div(w, 2)
    c = w - 2 * z
    sibling = 2 * z + 1 - c

    over_z = ring("width", z, lambda position: 2 * position + c)
    across_z = ring("width", z, lambda position: 2 * position + 1 - c)

    def quarter(q):
        first = q * FQ
        h = lax.div(first, FH)
        return h, pl.ds(pl.multiple_of(first - h * FH, FQ), FQ)

    mine = pl.ds(pl.multiple_of(c * FH, FH), FH)
    other = pl.ds(pl.multiple_of(FH - c * FH, FH), FH)

    barrier = pltpu.get_barrier_semaphore()
    over_y = ring("mlp", y)

    def signal(semaphore, **where):
        pl.semaphore_signal(semaphore, inc=1, device_id=where, device_id_type=MESH)

    for o in (2, -2, 1, -1):
        signal(barrier, **over_z[1](o))
        signal(barrier, **over_y[1](o))
    for o in range(1, NX):
        signal(barrier, dp=lax.rem(x + o, NX))
    signal(barrier, width=sibling)

    loads = [
        pltpu.make_async_copy(tok_h, tok, ld.at[0]),
        pltpu.make_async_copy(gain_h, gain_v, ld.at[1]),
        pltpu.make_async_copy(wup_h.at[:, other], wup.at[:, other], ld.at[2]),
        pltpu.make_async_copy(cot_h, cotx.at[0], ld.at[3]),
        pltpu.make_async_copy(wdn_h.at[other], wdn.at[other], ld.at[4]),
        pltpu.make_async_copy(wup_h.at[:, mine], wup.at[:, mine], ld.at[5]),
        pltpu.make_async_copy(wdn_h.at[mine], wdn.at[mine], ld.at[6]),
    ]
    for load in loads:
        load.start()

    loads[0].wait()
    loads[1].wait()
    values = tok[...].astype(F32)
    total = jnp.sum(values, axis=1, keepdims=True)
    shifted = values - total * (1.0 / DS)
    g_all = gain_v[...].reshape(1, DS)
    leaning[0:T] = (shifted * g_all).astype(BF16)
    row = lax.broadcasted_iota(jnp.int32, (TB, DS), 0)
    g_one = g_all.astype(BF16).astype(F32)
    g_two = (g_all - g_one).astype(BF16).astype(F32)
    g_rows = jnp.where(row == 0, g_one, jnp.where(row == 1, g_two, jnp.where(row == 2, g_all - g_one - g_two, 0.0)))
    leaning[T:] = g_rows.astype(BF16)
    loads[2].wait()
    its_half = dot(leaning[...], wup[:, other], 1, 0)
    sib_s[0] = its_half[0:T].astype(BF16)

    loads[3].wait()
    loads[4].wait()
    sib_s[1] = dot(cotx[0], wdn[other, :], 1, 1).astype(BF16)
    pl.semaphore_wait(barrier, 8 + NX)
    for k in range(2):
        send(sib_s.at[k], sib_r.at[k], sib_ss.at[k], sib_rs.at[k], width=sibling)
    signal(known, width=sibling)
    for o in (2, -2):
        signal(known, **over_z[1](o))
        signal(known, **over_y[1](o))

    loads[5].wait()
    my_half = dot(leaning[...], wup[:, mine], 1, 0)
    own[0] = my_half[0:T].reshape(NZ, TB, FH)
    loads[6].wait()
    own[1] = dot(cotx[0], wdn[mine, :], 1, 1).reshape(NZ, TB, FH)

    shifted = tok[...].astype(F32) - total * (1.0 / DS)
    spread = jnp.sum(shifted * shifted, axis=1, keepdims=True)
    total_row = jnp.transpose(jnp.broadcast_to(total, (T, EXTRA)))[0:1]
    spread_row = jnp.transpose(jnp.broadcast_to(spread, (T, EXTRA)))[0:1]
    for h, half in ((c, my_half), (1 - c, its_half)):
        lean = jnp.sum(half[T:], axis=0, keepdims=True)
        stat_s[h, 0:1, 0:T] = total_row
        stat_s[h, 1:2, 0:T] = spread_row
        for j in range(FH // 128):
            stat_s[h, 2 + j : 3 + j, :] = lean[:, j * 128 : (j + 1) * 128]

    def merge(k):
        arrived(sib_r.at[k], sib_rs.at[k])
        both = own[k] + sib_r[k].astype(F32).reshape(NZ, TB, FH)
        own[k] = both
        zs[k] = both.astype(BF16)
        scatter(over_z, zs.at[k], zr.at[k], [zh.at[k, 0], zh.at[k, 1]], z_ss.at[k], z_rs.at[k])

    def merge_pass(k):
        scatter_pass(
            over_z, own.at[k], zr.at[k], [zh.at[k, 0], zh.at[k, 1]], zc.at[k], z_ss.at[k], z_rs.at[k]
        )

    def tell(k, carry):
        peer = lax.rem(w + k, NW)
        send(stat_s.at[lax.rem(peer, 2)], stat_r.at[k - 1], stat_ss, stat_rs, width=peer)
        return carry

    merge(0)
    pl.semaphore_wait(known, 5)
    signal(all_known, width=sibling)
    merge(1)
    pl.semaphore_wait(all_known, 1)
    lax.fori_loop(1, NW, tell, 0)

    right, left = lax.rem(x + 1, NX), lax.rem(x + NX - 1, NX)
    first_rows, last_rows = pl.ds(0, T // 2), pl.ds(T // 2, T // 2)

    def spread_x(k, buf):
        send(buf.at[0], buf.at[1], x_ss.at[k], x_rs.at[k, 0], dp=right)
        send(buf.at[0], buf.at[NX - 1], x_ss.at[k], x_rs.at[k, 1], dp=left)

    def pass_x(k, buf):
        arrived(buf.at[1], x_rs.at[k, 0])
        send(buf.at[1, first_rows], buf.at[2, first_rows], x_ss.at[k], x_rs.at[k, 2], dp=right)
        arrived(buf.at[NX - 1], x_rs.at[k, 1])
        send(buf.at[NX - 1, last_rows], buf.at[2, last_rows], x_ss.at[k], x_rs.at[k, 3], dp=left)

    def end_x(k, buf):
        arrived(buf.at[2, first_rows], x_rs.at[k, 2])
        arrived(buf.at[2, last_rows], x_rs.at[k, 3])

    spread_x(0, cotx)
    merge_pass(0)
    merge_pass(1)

    arrived(stat_r, stat_rs)
    its = stat_r[...]
    my_stat = stat_s[c]
    sums, spreads = its[:, 0, :], its[:, 1, :]
    mean = (jnp.sum(sums, axis=0, keepdims=True) + my_stat[0:1]) * (1.0 / D)
    away, my_away = sums * (1.0 / DS) - mean, my_stat[0:1] * (1.0 / DS) - mean
    variance = (
        jnp.sum(spreads + DS * away * away, axis=0, keepdims=True) + my_stat[1:2] + DS * my_away * my_away
    ) * (1.0 / D)
    inv_std = lax.rsqrt(variance + 1e-06)
    mean_col = jnp.transpose(jnp.broadcast_to(mean[:, 0:T], (EXTRA, T)))
    std_col = jnp.transpose(jnp.broadcast_to(inv_std[:, 0:T], (EXTRA, T)))
    inv_col[...] = std_col
    aways = jnp.concatenate([away[:, 0:T], my_away[:, 0:T], jnp.zeros((EXTRA - NW, T), F32)], axis=0)
    away_col[...] = jnp.transpose(aways)
    token_rows = pl.ds(pl.multiple_of(z * TB, TB), TB)
    my_aways = away_col[token_rows, :]
    leans, shift = [], []
    for j in range(FH // 128):
        piece = [its[s, 2 + j : 3 + j, :] for s in range(NW - 1)] + [my_stat[2 + j : 3 + j, :]]
        leans.append(functools.reduce(jnp.add, piece))
        shift.append(functools.reduce(jnp.add, [my_aways[:, s : s + 1] * piece[s] for s in range(NW)]))
    lean_row = jnp.concatenate(leans, axis=1)
    shift = jnp.concatenate(shift, axis=1)

    def hand_over(k):
        return lambda block: send(block, block, rel_ss.at[k], rel_rs.at[k], width=sibling)

    pre_act = (scatter_sum(over_z, own.at[0], zr.at[0], z_rs.at[0]) + shift) * inv_col[token_rows, 0:1]
    below = 0.5 * (1.0 + lax.erf(pre_act * inv_root_two))
    hid[c, z] = (pre_act * below).astype(BF16)
    units, grads = hid.at[c], gp.at[c]
    gather(over_z, units, ag_ss.at[0], ag_rs.at[0])
    hand_over(0)(hid.at[c, z])
    slope = below + pre_act * jnp.exp(-0.5 * pre_act * pre_act) * inv_root_two_pi
    grad_hidden = scatter_sum(over_z, own.at[1], zr.at[1], z_rs.at[1])
    grad_pre = (grad_hidden * slope).astype(BF16)
    wide = grad_pre.astype(F32)
    gp[c, z, :, 0:FH] = grad_pre
    gp[c, z, :, FH:] = pack(
        jnp.sum(wide * lean_row, axis=1, keepdims=True), jnp.sum(wide * pre_act, axis=1, keepdims=True)
    )
    gather(over_z, grads, ag_ss.at[1], ag_rs.at[1])
    hand_over(1)(gp.at[c, z])

    for j in range(DS // 128):
        cols = slice(j * 128, (j + 1) * 128)
        normal = (tok[:, cols].astype(F32) - mean_col) * std_col
        normed[:, cols] = normal
        scx[0, :, cols] = (normal * g_all[:, cols]).astype(BF16)
    spread_x(1, scx)

    gather_pass(over_z, units, ag_ss.at[0], [(over_z, ag_rs.at[0], 4)], hand_over(0))
    gather_near(over_z, units, ag_rs.at[0], hand_over(0))
    gather_pass(
        over_z, grads, ag_ss.at[1], [(over_z, ag_rs.at[1], 4), (across_z, far_rs, 0)], hand_over(1)
    )
    gather_near(over_z, grads, ag_rs.at[1], hand_over(1))
    pass_x(0, cotx)

    block_of, _ = over_z
    near, far = (0, 1, -1, 2, -2), (3, -3, 4)

    half_ring = NY // 2
    slot = lax.rem(y, half_ring)

    def next_to(o):
        return lax.rem(y + o % NY, NY)

    def own_sums(k, part, got, result):
        arrived(got, y_rs.at[k])
        for side in range(2):
            block = lax.rem(y + side * half_ring, NY)
            summed = part[block] + jnp.sum(got[side].astype(F32), axis=0)
            result[lax.div(block, half_ring), lax.rem(block, half_ring)] = summed.astype(BF16)

    def from_owners(k, buf):
        both = buf.at[:, slot]
        for side, o in ((0, 1), (1, -1)):
            one = buf.at[side, slot]
            send(one, one, yag_ss.at[k], yag_rs.at[k, 2 + side], mlp=next_to(2 * o))
            send(both, both, yag_ss.at[k], yag_rs.at[k, side], mlp=next_to(o))

    def from_owners_end(k, buf):
        for side, o in ((0, -1), (1, 1)):
            arrived(buf.at[:, lax.rem(next_to(o), half_ring)], yag_rs.at[k, side])
            arrived(buf.at[side, lax.rem(next_to(2 * o), half_ring)], yag_rs.at[k, 2 + side])

    def rows_of(buf, h, blocks, lanes):
        return jnp.concatenate([buf[h, block_of(o), :, lanes] for o in blocks], axis=0)

    def to_owners(k, blocks, terms, part, sent, got):
        for i, o in enumerate(blocks):
            block = block_of(o)
            part[block] = terms[i * TB : (i + 1) * TB]
            sent[block] = terms[i * TB : (i + 1) * TB].astype(BF16)
            for side in range(2):
                owner = lax.rem(block + side * half_ring, NY)

                @pl.when(owner != y)
                def _():
                    place_there = got.at[side, lax.rem(owner - y + NY - 1, NY)]
                    send(sent.at[block], place_there, y_ss.at[k], y_rs.at[k], mlp=owner)

    def output_terms(blocks):
        units = slice(0, FH)
        term = dot(rows_of(hid, 0, blocks, units), wdn[0:FH, :], 1, 0)
        term = term + dot(rows_of(hid, 1, blocks, units), wdn[FH:, :], 1, 0)
        to_owners(0, blocks, term, part0, ys0, yr0)

    def gradient_terms(blocks):
        units, beside = slice(0, FH), slice(FH, FH + EXTRA)
        term = dot(rows_of(gp, 0, blocks, units), wup[:, 0:FH], 1, 1)
        term = term + dot(rows_of(gp, 1, blocks, units), wup[:, FH:], 1, 1)
        side = rows_of(gp, 0, blocks, beside).astype(F32) + rows_of(gp, 1, blocks, beside).astype(F32)
        first, second = unpack(side)
        tokens = [pl.ds(pl.multiple_of(block_of(o) * TB, TB), TB) for o in blocks]
        normal = jnp.concatenate([normed[rows, :] for rows in tokens], axis=0)
        scale = jnp.concatenate([inv_col[rows, 0:1] for rows in tokens], axis=0)
        corrected = scale * (
            term * gain_v[...].reshape(1, DS) - first * (1.0 / D) - normal * (second * (1.0 / D))
        )
        to_owners(1, blocks, corrected, part1, ys1, yr1)
        return jnp.sum((term * normal).reshape(len(blocks) * TB // 8, 8, DS), axis=0)

    my_blocks = pl.ds(pl.multiple_of(c * (NZ // 2), NZ // 2), NZ // 2)
    its_blocks = pl.ds(pl.multiple_of((1 - c) * (NZ // 2), NZ // 2), NZ // 2)

    def share(k, buf, dst):
        def one(o, carry):
            peer = lax.rem(x + o, NX)
            h, lanes = quarter(peer)
            send(buf.at[h, my_blocks, :, lanes], dst.at[o, my_blocks], q_ss.at[k], q_rs.at[k], dp=peer)
            return carry
        lax.fori_loop(1, NX, one, 0)
        h, lanes = quarter(x)
        dst[0] = buf[h, :, :, lanes]

    def join(k, dst):
        halves = dst.at[pl.ds(1, NX - 1), my_blocks]
        arrived(halves, q_rs.at[k])
        send(halves, halves, join_ss.at[k], join_rs.at[k], width=sibling)

    arrived(hid.at[1 - c, pl.ds(0, 5)], rel_rs.at[0])
    output_terms(near)
    gather_far(over_z, units, ag_rs.at[0], 4)
    for o in far:
        block = hid.at[c, block_of(o)]
        send(block, block, rel_ss.at[0], rel_rs.at[2], width=sibling)
    arrived(gp.at[1 - c, pl.ds(0, 5)], rel_rs.at[1])
    gg_sum[...] = gradient_terms(near)
    arrived(hid.at[1 - c, pl.ds(0, 3)], rel_rs.at[2])
    output_terms(far)
    share(0, hid, hx)
    gather_far(over_z, grads, ag_rs.at[1], 4)
    gather_far(over_z, gp.at[1 - c], far_rs, 0)
    gains = gg_sum[...] + gradient_terms(far)
    share(1, gp, gpx)
    gains = jnp.sum(gains, axis=0, keepdims=True)
    rows = [gains[:, j * 128 : (j + 1) * 128] for j in range(DS // 128)]
    gg_s[...] = jnp.concatenate(rows + [jnp.zeros((8 - len(rows), 128), F32)], axis=0)

    def gain_x(o, carry):
        send(gg_s, ggx_r.at[o - 1], ggx_ss, ggx_rs, dp=lax.rem(x + o, NX))
        return carry
    lax.fori_loop(1, NX, gain_x, 0)
    pass_x(1, scx)
    join(0, hx)

    own_sums(0, part0, yr0, outv)
    from_owners(0, outv)

    arrived(ggx_r, ggx_rs)
    ggy_s[...] = gg_s[...] + jnp.sum(ggx_r[...], axis=0)

    def gain_y(o, carry):
        send(ggy_s, ggy_r.at[o - 1], ggy_ss, ggy_rs, mlp=lax.rem(y + o, NY))
        return carry
    lax.fori_loop(1, NY, gain_y, 0)

    join(1, gpx)

    end_x(0, cotx)
    arrived(hx.at[pl.ds(1, NX - 1), its_blocks], join_rs.at[0])
    gdn[...] = dot(hx[...].reshape(NX * T, FQ), cotx[...].reshape(NX * T, DS), 0, 0)
    own_sums(1, part1, yr1, gtv)
    from_owners(1, gtv)
    end_x(1, scx)
    arrived(gpx.at[pl.ds(1, NX - 1), its_blocks], join_rs.at[1])
    product = dot(scx[...].reshape(NX * T, DS), gpx[...].reshape(NX * T, FQ), 0, 0)
    pieces = FQ // 128
    for j in range(pieces):
        gup[pl.ds(j, DS, stride=pieces), :] = product[:, j * 128 : (j + 1) * 128]
    for k in range(2):
        arrived(sib_s.at[k], sib_ss.at[k])
        arrived(zs.at[k, pl.ds(0, NZ - 1)], z_ss.at[k])
    arrived(stat_r, stat_ss)
    arrived(hid.at[0, pl.ds(0, NZ - 1)], ag_ss.at[0])
    arrived(hid.at[0], rel_ss.at[0])
    arrived(gp.at[:, pl.ds(0, 5)], ag_ss.at[1])
    arrived(gp.at[0, pl.ds(0, 5)], rel_ss.at[1])
    for k, buf in enumerate((cotx, scx)):
        arrived(buf.at[pl.ds(0, NX - 1)], x_ss.at[k])
    for k, buf in enumerate((hx, gpx)):
        arrived(buf.at[pl.ds(1, NX - 1), my_blocks], q_ss.at[k])
        arrived(buf.at[pl.ds(1, NX - 1), my_blocks], join_ss.at[k])
    arrived(yr0, y_ss.at[0])
    arrived(yr1, y_ss.at[1])
    arrived(outv.at[:, pl.ds(0, 3)], yag_ss.at[0])
    arrived(ggx_r, ggx_ss)

    from_owners_end(0, outv)
    out[...] = outv[...].reshape(T, DS)
    from_owners_end(1, gtv)
    gt[...] = gtv[...].reshape(T, DS)
    arrived(ggy_r, ggy_rs)
    gains = ggy_s[...] + jnp.sum(ggy_r[...], axis=0)
    gg[...] = jnp.concatenate([gains[j : j + 1] for j in range(DS // 128)], axis=1).reshape(DS)
    arrived(gtv.at[:, pl.ds(0, 3)], yag_ss.at[1])
    arrived(ggy_r, ggy_ss)


def place(*refs):
    made, given, sems = refs[0:5], refs[5:10], refs[10]
    copies = [pltpu.make_async_copy(src, dst, sems.at[k]) for k, (src, dst) in enumerate(zip(made, given))]
    for copy in copies:
        copy.start()
    for copy in copies:
        copy.wait()


def solution(mesh):
    NX, NZ, NY = mesh.shape["dp"], mesh.shape["width"] // 2, mesh.shape["mlp"]

    def shards(tokens, gain, up_weight, down_weight, cotangent):
        T, DS = tokens.shape
        FS = up_weight.shape[1]
        FH, FQ = FS // 2, FS // NX
        vmem, dma = pltpu.VMEM, pltpu.SemaphoreType.DMA
        results = (
            jax.ShapeDtypeStruct((T, DS), BF16),
            jax.ShapeDtypeStruct((T, DS), BF16),
            jax.ShapeDtypeStruct((DS,), F32),
            jax.ShapeDtypeStruct((DS * FQ // 128, 128), F32),
            jax.ShapeDtypeStruct((FQ, DS), F32),
        )
        call = pl.pallas_call(
            functools.partial(kernel, (NX, NZ, NY, DS * 2 * NZ)),
            out_shape=results,
            in_specs=[pl.BlockSpec(memory_space=pltpu.HBM)] * 5,
            out_specs=[pl.BlockSpec(memory_space=pltpu.VMEM)] * 5,
            scratch_shapes=[
                vmem((T, DS), BF16), vmem((DS,), F32), vmem((DS, FS), BF16), vmem((FS, DS), BF16),
                vmem((NX, T, DS), BF16), vmem((NX, T, DS), BF16), vmem((T, DS), F32), vmem((T, EXTRA), F32),
                vmem((2, 8, 128), F32), vmem((2 * NZ - 1, 8, 128), F32),
                vmem((2, T, FH), BF16), vmem((2, T, FH), BF16), vmem((2, NZ, TB, FH), F32),
                vmem((2, NZ, TB, FH), BF16), vmem((2, 6, TB, FH), BF16),
                vmem((2, 2, TB, FH // 2), BF16), vmem((2, 2, TB, FH), BF16),
                vmem((T + TB, DS), BF16), vmem((T, EXTRA), F32),
                vmem((2, NZ, TB, FH), BF16), vmem((2, NZ, TB, FH + EXTRA), BF16),
                vmem((NX, NZ, TB, FQ), BF16), vmem((NX, NZ, TB, FQ), BF16),
                *(
                    shape
                    for _ in range(2)
                    for shape in (
                        vmem((NY, TB, DS), BF16), vmem((2, NY - 1, TB, DS), BF16), vmem((NY, TB, DS), F32),
                    )
                ),
                vmem((2, NY // 2, TB, DS), BF16), vmem((2, NY // 2, TB, DS), BF16),
                vmem((8, DS), F32), vmem((8, 128), F32), vmem((NX - 1, 8, 128), F32),
                vmem((8, 128), F32), vmem((NY - 1, 8, 128), F32),
                dma((7,)), dma((2,)), dma((2,)), dma, dma, dma((2,)), dma((2, 8)),
                dma((2,)), dma((2, 8)), dma((4,)), dma((2,)), dma((3,)),
                dma((2,)), dma((2, 4)), dma((2,)), dma((2,)), dma((2,)), dma((2,)),
                dma((2,)), dma((2,)), dma((2,)), dma((2, 4)), dma, dma, dma, dma,
                pltpu.SemaphoreType.REGULAR, pltpu.SemaphoreType.REGULAR,
            ],
            compiler_params=pltpu.CompilerParams(
                collective_id=0, has_side_effects=True, vmem_limit_bytes=48 * 1024 * 1024
            ),
            cost_estimate=pl.CostEstimate(
                flops=12 * T * DS * FS, bytes_accessed=4 * DS * FS + 8 * DS * FQ, transcendentals=2 * TB * FH
            ),
        )
        put = pl.pallas_call(
            place,
            out_shape=results,
            in_specs=[pl.BlockSpec(memory_space=pltpu.VMEM)] * 5,
            out_specs=[pl.BlockSpec(memory_space=pltpu.HBM)] * 5,
            scratch_shapes=[dma((5,))],
            compiler_params=pltpu.CompilerParams(vmem_limit_bytes=4 * 1024 * 1024),
        )
        output, grad_tokens, grad_gain, grad_up, grad_down = put(
            *call(*(pltpu.with_memory_space_constraint(a, pltpu.HBM) for a in (tokens, gain, up_weight, down_weight, cotangent)))
        )
        return output, grad_tokens, grad_gain, grad_up.reshape(DS, 1, FQ), grad_down[None, :, :]

    placed = (P("dp", "width"), P("width"), P("width", "mlp"), P("mlp", "width"), P("dp", "width"))
    return jax.shard_map(
        shards,
        mesh=mesh,
        in_specs=placed,
        out_specs=(
            P("dp", "width"),
            P("dp", "width"),
            P("width"),
            P("width", "mlp", "dp"),
            P("mlp", "dp", "width"),
        ),
        check_vma=False,
    )
```

```python
import functools

import jax
import jax.numpy as jnp
from jax import lax
from jax.experimental import pallas as pl
from jax.experimental.pallas import tpu as pltpu
from jax.sharding import PartitionSpec as P

MESH = pl.DeviceIdType.MESH
F32, BF16 = jnp.float32, jnp.bfloat16
TB = 16
EXTRA = 128

inv_root_two = 0.7071067811865476
inv_root_two_pi = 0.3989422804014327


def dot(left, right, left_dim, right_dim):
    return lax.dot_general(
        left, right, (((left_dim,), (right_dim,)), ((), ())), preferred_element_type=F32
    )


def pack(first, second):
    lane = lax.broadcasted_iota(jnp.int32, (first.shape[0], EXTRA), 1)
    high_one, high_two = first.astype(BF16).astype(F32), second.astype(BF16).astype(F32)
    held = jnp.where(lane == 0, high_one, 0.0)
    held = jnp.where(lane == 1, high_two, held)
    held = jnp.where(lane == 2, first - high_one, held)
    held = jnp.where(lane == 3, second - high_two, held)
    return held.astype(BF16)


def unpack(held):
    return held[:, 0:1] + held[:, 2:3], held[:, 1:2] + held[:, 3:4]


def send(src, dst, ss, rs, **where):
    pltpu.make_async_remote_copy(
        src_ref=src, dst_ref=dst, send_sem=ss, recv_sem=rs, device_id=where, device_id_type=MESH
    ).start()


def arrived(ref, sem):
    pltpu.make_async_copy(ref, ref, sem).wait()


def ring(axis, me, device=lambda position: position):
    def at(o):
        return lax.rem(me + o % 8, 8)
    return at, lambda o: {axis: device(at(o))}


def lanes_of(block, side):
    cut = block.shape[-1] // 256 * 128
    return block.at[:, pl.ds(0, cut) if side == 0 else pl.ds(cut, block.shape[-1] - cut)]


def scatter(to_whom, terms, got, halves, ss, rs):
    at, to = to_whom
    for side, o in ((0, 1), (1, -1)):
        send(terms.at[at(3 * o)], got.at[4 + side], ss, rs.at[4 + side], **to(o))
    for side, o in ((0, 2), (1, -2)):
        send(lanes_of(terms.at[at(4)], side), halves[side], ss, rs.at[6 + side], **to(o))
    for side, o in ((0, 1), (1, -1)):
        send(terms.at[at(o)], got.at[side], ss, rs.at[side], **to(o))


def scatter_pass(to_whom, own, got, halves, sums, ss, rs):
    at, to = to_whom
    for side, o in ((0, 2), (1, -2)):
        arrived(got.at[4 + side], rs.at[4 + side])
        arrived(halves[side], rs.at[6 + side])
        term = own[at(o)] + got[4 + side].astype(F32)
        half = halves[side][...].astype(F32)
        cut = term.shape[-1] // 256 * 128
        low, high = term[:, 0:cut], term[:, cut:]
        sums[side, :, 0:cut] = (low + half if side == 0 else low).astype(BF16)
        sums[side, :, cut:] = (high if side == 0 else high + half).astype(BF16)
        send(sums.at[side], got.at[2 + side], ss, rs.at[2 + side], **to(o))


def scatter_sum(to_whom, own, got, rs):
    at, _ = to_whom
    for slot in range(4):
        arrived(got.at[slot], rs.at[slot])
    return own[at(0)] + jnp.sum(got[0:4].astype(F32), axis=0)


def gather(to_whom, buf, ss, rs):
    at, to = to_whom
    block = buf.at[at(0)]
    for o, slot in ((2, 2), (-2, 3), (1, 0), (-1, 1)):
        send(block, block, ss, rs.at[slot], **to(o))


def gather_pass(here, buf, ss, sems, use):
    at, _ = here
    for side, o in ((0, 1), (1, -1)):
        block = buf.at[at(-2 * o)]
        arrived(block, sems[0][1].at[2 + side])
        half = lanes_of(block, side)
        for (_, to), there, first in sems:
            send(block, block, ss, there.at[first + side], **to(o))
            send(half, half, ss, there.at[first + 2 + side], **to(2 * o))
        use(block)


def gather_near(here, buf, rs, use):
    at, _ = here
    for side, o in ((0, -1), (1, 1)):
        arrived(buf.at[at(o)], rs.at[side])
        use(buf.at[at(o)])


def gather_far(here, buf, sems, first):
    at, _ = here
    for side, o in ((0, -3), (1, 3)):
        arrived(buf.at[at(o)], sems.at[first + side])
        arrived(lanes_of(buf.at[at(4)], side), sems.at[first + 2 + side])


def kernel(
    sizes, tok_h, gain_h, wup_h, wdn_h, cot_h, out, gt, gg, gup, gdn,
    tok, gain_v, wup, wdn, cotx, scx, normed, inv_col,
    stat_s, stat_r,
    sib_s, sib_r, own, zs, zr, zh, zc, leaning, away_col,
    hid, gp, hx, gpx,
    ys0, yr0, part0, ys1, yr1, part1,
    outv, gtv,
    gg_sum, gg_s, ggx_r, ggy_s, ggy_r,
    ld, sib_ss, sib_rs, stat_ss, stat_rs, z_ss, z_rs, ag_ss, ag_rs, far_rs, rel_ss, rel_rs,
    x_ss, x_rs, q_ss, q_rs, join_ss, join_rs, y_ss, y_rs, yag_ss, yag_rs, ggx_ss, ggx_rs, ggy_ss, ggy_rs,
    known, all_known,
):
    NX, NZ, NY, D = sizes
    T, DS = tok.shape
    TY = T // NY
    FS = wup.shape[1]
    FH, FQ = FS // 2, FS // NX
    NW = 2 * NZ
    x, w, y = lax.axis_index("dp"), lax.axis_index("width"), lax.axis_index("mlp")
    z = lax.div(w, 2)
    c = w - 2 * z
    sibling = 2 * z + 1 - c

    over_z = ring("width", z, lambda position: 2 * position + c)
    across_z = ring("width", z, lambda position: 2 * position + 1 - c)

    def quarter(q):
        first = q * FQ
        h = lax.div(first, FH)
        return h, pl.ds(pl.multiple_of(first - h * FH, FQ), FQ)

    mine = pl.ds(pl.multiple_of(c * FH, FH), FH)
    other = pl.ds(pl.multiple_of(FH - c * FH, FH), FH)

    barrier = pltpu.get_barrier_semaphore()
    over_y = ring("mlp", y)

    def signal(semaphore, **where):
        pl.semaphore_signal(semaphore, inc=1, device_id=where, device_id_type=MESH)

    for o in (2, -2, 1, -1):
        signal(barrier, **over_z[1](o))
        signal(barrier, **over_y[1](o))
    for o in range(1, NX):
        signal(barrier, dp=lax.rem(x + o, NX))
    signal(barrier, width=sibling)

    loads = [
        pltpu.make_async_copy(tok_h, tok, ld.at[0]),
        pltpu.make_async_copy(gain_h, gain_v, ld.at[1]),
        pltpu.make_async_copy(wup_h.at[:, other], wup.at[:, other], ld.at[2]),
        pltpu.make_async_copy(cot_h, cotx.at[0], ld.at[3]),
        pltpu.make_async_copy(wdn_h.at[other], wdn.at[other], ld.at[4]),
        pltpu.make_async_copy(wup_h.at[:, mine], wup.at[:, mine], ld.at[5]),
        pltpu.make_async_copy(wdn_h.at[mine], wdn.at[mine], ld.at[6]),
    ]
    for load in loads:
        load.start()

    loads[0].wait()
    loads[1].wait()
    values = tok[...].astype(F32)
    total = jnp.sum(values, axis=1, keepdims=True)
    shifted = values - total * (1.0 / DS)
    g_all = gain_v[...].reshape(1, DS)
    leaning[0:T] = (shifted * g_all).astype(BF16)
    row = lax.broadcasted_iota(jnp.int32, (TB, DS), 0)
    g_one = g_all.astype(BF16).astype(F32)
    g_two = (g_all - g_one).astype(BF16).astype(F32)
    g_rows = jnp.where(row == 0, g_one, jnp.where(row == 1, g_two, jnp.where(row == 2, g_all - g_one - g_two, 0.0)))
    leaning[T:] = g_rows.astype(BF16)
    loads[2].wait()
    its_half = dot(leaning[...], wup[:, other], 1, 0)
    sib_s[0] = its_half[0:T].astype(BF16)

    pl.semaphore_wait(barrier, 8 + NX)
    send(sib_s.at[0], sib_r.at[0], sib_ss.at[0], sib_rs.at[0], width=sibling)
    signal(known, width=sibling)
    for o in (2, -2):
        signal(known, **over_z[1](o))
        signal(known, **over_y[1](o))

    loads[3].wait()
    loads[4].wait()
    sib_s[1] = dot(cotx[0], wdn[other, :], 1, 1).astype(BF16)
    send(sib_s.at[1], sib_r.at[1], sib_ss.at[1], sib_rs.at[1], width=sibling)
    loads[5].wait()
    my_half = dot(leaning[...], wup[:, mine], 1, 0)
    own[0] = my_half[0:T].reshape(NZ, TB, FH)
    loads[6].wait()
    own[1] = dot(cotx[0], wdn[mine, :], 1, 1).reshape(NZ, TB, FH)

    shifted = tok[...].astype(F32) - total * (1.0 / DS)
    spread = jnp.sum(shifted * shifted, axis=1, keepdims=True)
    total_row = jnp.transpose(jnp.broadcast_to(total, (T, EXTRA)))[0:1]
    spread_row = jnp.transpose(jnp.broadcast_to(spread, (T, EXTRA)))[0:1]
    for h, half in ((c, my_half), (1 - c, its_half)):
        lean = jnp.sum(half[T:], axis=0, keepdims=True)
        stat_s[h, 0:1, 0:T] = total_row
        stat_s[h, 1:2, 0:T] = spread_row
        for j in range(FH // 128):
            stat_s[h, 2 + j : 3 + j, :] = lean[:, j * 128 : (j + 1) * 128]

    def merge(k):
        arrived(sib_r.at[k], sib_rs.at[k])
        both = own[k] + sib_r[k].astype(F32).reshape(NZ, TB, FH)
        own[k] = both
        zs[k] = both.astype(BF16)
        scatter(over_z, zs.at[k], zr.at[k], [zh.at[k, 0], zh.at[k, 1]], z_ss.at[k], z_rs.at[k])

    def merge_pass(k):
        scatter_pass(
            over_z, own.at[k], zr.at[k], [zh.at[k, 0], zh.at[k, 1]], zc.at[k], z_ss.at[k], z_rs.at[k]
        )

    def tell(k, carry):
        peer = lax.rem(w + k, NW)
        send(stat_s.at[lax.rem(peer, 2)], stat_r.at[k - 1], stat_ss, stat_rs, width=peer)
        return carry

    merge(0)
    pl.semaphore_wait(known, 5)
    signal(all_known, width=sibling)
    merge(1)
    pl.semaphore_wait(all_known, 1)
    lax.fori_loop(1, NW, tell, 0)

    right, left = lax.rem(x + 1, NX), lax.rem(x + NX - 1, NX)
    first_rows, last_rows = pl.ds(0, T // 2), pl.ds(T // 2, T // 2)

    def spread_x(k, buf):
        send(buf.at[0], buf.at[1], x_ss.at[k], x_rs.at[k, 0], dp=right)
        send(buf.at[0], buf.at[NX - 1], x_ss.at[k], x_rs.at[k, 1], dp=left)

    def pass_x(k, buf):
        arrived(buf.at[1], x_rs.at[k, 0])
        send(buf.at[1, first_rows], buf.at[2, first_rows], x_ss.at[k], x_rs.at[k, 2], dp=right)
        arrived(buf.at[NX - 1], x_rs.at[k, 1])
        send(buf.at[NX - 1, last_rows], buf.at[2, last_rows], x_ss.at[k], x_rs.at[k, 3], dp=left)

    def end_x(k, buf):
        arrived(buf.at[2, first_rows], x_rs.at[k, 2])
        arrived(buf.at[2, last_rows], x_rs.at[k, 3])

    spread_x(0, cotx)
    merge_pass(0)
    merge_pass(1)

    arrived(stat_r, stat_rs)
    its = stat_r[...]
    my_stat = stat_s[c]
    sums, spreads = its[:, 0, :], its[:, 1, :]
    mean = (jnp.sum(sums, axis=0, keepdims=True) + my_stat[0:1]) * (1.0 / D)
    away, my_away = sums * (1.0 / DS) - mean, my_stat[0:1] * (1.0 / DS) - mean
    variance = (
        jnp.sum(spreads + DS * away * away, axis=0, keepdims=True) + my_stat[1:2] + DS * my_away * my_away
    ) * (1.0 / D)
    inv_std = lax.rsqrt(variance + 1e-06)
    mean_col = jnp.transpose(jnp.broadcast_to(mean[:, 0:T], (EXTRA, T)))
    std_col = jnp.transpose(jnp.broadcast_to(inv_std[:, 0:T], (EXTRA, T)))
    inv_col[...] = std_col
    aways = jnp.concatenate([away[:, 0:T], my_away[:, 0:T], jnp.zeros((EXTRA - NW, T), F32)], axis=0)
    away_col[...] = jnp.transpose(aways)
    token_rows = pl.ds(pl.multiple_of(z * TB, TB), TB)
    my_aways = away_col[token_rows, :]
    leans, shift = [], []
    for j in range(FH // 128):
        piece = [its[s, 2 + j : 3 + j, :] for s in range(NW - 1)] + [my_stat[2 + j : 3 + j, :]]
        leans.append(functools.reduce(jnp.add, piece))
        shift.append(functools.reduce(jnp.add, [my_aways[:, s : s + 1] * piece[s] for s in range(NW)]))
    lean_row = jnp.concatenate(leans, axis=1)
    shift = jnp.concatenate(shift, axis=1)

    def hand_over(k):
        return lambda block: send(block, block, rel_ss.at[k], rel_rs.at[k], width=sibling)

    pre_act = (scatter_sum(over_z, own.at[0], zr.at[0], z_rs.at[0]) + shift) * inv_col[token_rows, 0:1]
    below = 0.5 * (1.0 + lax.erf(pre_act * inv_root_two))
    hid[c, z] = (pre_act * below).astype(BF16)
    units, grads = hid.at[c], gp.at[c]
    gather(over_z, units, ag_ss.at[0], ag_rs.at[0])
    hand_over(0)(hid.at[c, z])
    slope = below + pre_act * jnp.exp(-0.5 * pre_act * pre_act) * inv_root_two_pi
    grad_hidden = scatter_sum(over_z, own.at[1], zr.at[1], z_rs.at[1])
    grad_pre = (grad_hidden * slope).astype(BF16)
    wide = grad_pre.astype(F32)
    gp[c, z, :, 0:FH] = grad_pre
    gp[c, z, :, FH:] = pack(
        jnp.sum(wide * lean_row, axis=1, keepdims=True), jnp.sum(wide * pre_act, axis=1, keepdims=True)
    )
    gather(over_z, grads, ag_ss.at[1], ag_rs.at[1])
    hand_over(1)(gp.at[c, z])

    for j in range(DS // 128):
        cols = slice(j * 128, (j + 1) * 128)
        normal = (tok[:, cols].astype(F32) - mean_col) * std_col
        normed[:, cols] = normal
        scx[0, :, cols] = (normal * g_all[:, cols]).astype(BF16)
    spread_x(1, scx)

    gather_pass(over_z, units, ag_ss.at[0], [(over_z, ag_rs.at[0], 4)], hand_over(0))
    gather_near(over_z, units, ag_rs.at[0], hand_over(0))
    gather_pass(
        over_z, grads, ag_ss.at[1], [(over_z, ag_rs.at[1], 4), (across_z, far_rs, 0)], hand_over(1)
    )
    gather_near(over_z, grads, ag_rs.at[1], hand_over(1))
    pass_x(0, cotx)

    block_of, _ = over_z
    near, far = (0, 1, -1, 2, -2), (3, -3, 4)

    half_ring = NY // 2
    slot = lax.rem(y, half_ring)

    def next_to(o):
        return lax.rem(y + o % NY, NY)

    def own_sums(k, part, got, result):
        arrived(got, y_rs.at[k])
        for side in range(2):
            block = lax.rem(y + side * half_ring, NY)
            summed = part[block] + jnp.sum(got[side].astype(F32), axis=0)
            result[lax.div(block, half_ring), lax.rem(block, half_ring)] = summed.astype(BF16)

    def from_owners(k, buf):
        both = buf.at[:, slot]
        for side, o in ((0, 1), (1, -1)):
            one = buf.at[side, slot]
            send(one, one, yag_ss.at[k], yag_rs.at[k, 2 + side], mlp=next_to(2 * o))
            send(both, both, yag_ss.at[k], yag_rs.at[k, side], mlp=next_to(o))

    def from_owners_end(k, buf):
        for side, o in ((0, -1), (1, 1)):
            arrived(buf.at[:, lax.rem(next_to(o), half_ring)], yag_rs.at[k, side])
            arrived(buf.at[side, lax.rem(next_to(2 * o), half_ring)], yag_rs.at[k, 2 + side])

    def rows_of(buf, h, blocks, lanes):
        return jnp.concatenate([buf[h, block_of(o), :, lanes] for o in blocks], axis=0)

    def to_owners(k, blocks, terms, part, sent, got):
        for i, o in enumerate(blocks):
            block = block_of(o)
            part[block] = terms[i * TB : (i + 1) * TB]
            sent[block] = terms[i * TB : (i + 1) * TB].astype(BF16)
            for side in range(2):
                owner = lax.rem(block + side * half_ring, NY)

                @pl.when(owner != y)
                def _():
                    place_there = got.at[side, lax.rem(owner - y + NY - 1, NY)]
                    send(sent.at[block], place_there, y_ss.at[k], y_rs.at[k], mlp=owner)

    def output_terms(blocks):
        units = slice(0, FH)
        term = dot(rows_of(hid, 0, blocks, units), wdn[0:FH, :], 1, 0)
        term = term + dot(rows_of(hid, 1, blocks, units), wdn[FH:, :], 1, 0)
        to_owners(0, blocks, term, part0, ys0, yr0)

    def gradient_terms(blocks):
        units, beside = slice(0, FH), slice(FH, FH + EXTRA)
        term = dot(rows_of(gp, 0, blocks, units), wup[:, 0:FH], 1, 1)
        term = term + dot(rows_of(gp, 1, blocks, units), wup[:, FH:], 1, 1)
        side = rows_of(gp, 0, blocks, beside).astype(F32) + rows_of(gp, 1, blocks, beside).astype(F32)
        first, second = unpack(side)
        tokens = [pl.ds(pl.multiple_of(block_of(o) * TB, TB), TB) for o in blocks]
        normal = jnp.concatenate([normed[rows, :] for rows in tokens], axis=0)
        scale = jnp.concatenate([inv_col[rows, 0:1] for rows in tokens], axis=0)
        corrected = scale * (
            term * gain_v[...].reshape(1, DS) - first * (1.0 / D) - normal * (second * (1.0 / D))
        )
        to_owners(1, blocks, corrected, part1, ys1, yr1)
        return jnp.sum((term * normal).reshape(len(blocks) * TB // 8, 8, DS), axis=0)

    my_blocks = pl.ds(pl.multiple_of(c * (NZ // 2), NZ // 2), NZ // 2)
    its_blocks = pl.ds(pl.multiple_of((1 - c) * (NZ // 2), NZ // 2), NZ // 2)

    def share(k, buf, dst):
        def one(o, carry):
            peer = lax.rem(x + o, NX)
            h, lanes = quarter(peer)
            send(buf.at[h, my_blocks, :, lanes], dst.at[o, my_blocks], q_ss.at[k], q_rs.at[k], dp=peer)
            return carry
        lax.fori_loop(1, NX, one, 0)
        h, lanes = quarter(x)
        dst[0] = buf[h, :, :, lanes]

    def join(k, dst):
        halves = dst.at[pl.ds(1, NX - 1), my_blocks]
        arrived(halves, q_rs.at[k])
        send(halves, halves, join_ss.at[k], join_rs.at[k], width=sibling)

    arrived(hid.at[1 - c, pl.ds(0, 5)], rel_rs.at[0])
    output_terms(near)
    gather_far(over_z, units, ag_rs.at[0], 4)
    for o in far:
        block = hid.at[c, block_of(o)]
        send(block, block, rel_ss.at[0], rel_rs.at[2], width=sibling)
    arrived(gp.at[1 - c, pl.ds(0, 5)], rel_rs.at[1])
    gg_sum[...] = gradient_terms(near)
    arrived(hid.at[1 - c, pl.ds(0, 3)], rel_rs.at[2])
    output_terms(far)
    gather_far(over_z, grads, ag_rs.at[1], 4)
    gather_far(over_z, gp.at[1 - c], far_rs, 0)
    gains = gg_sum[...] + gradient_terms(far)
    share(0, hid, hx)
    share(1, gp, gpx)
    gains = jnp.sum(gains, axis=0, keepdims=True)
    rows = [gains[:, j * 128 : (j + 1) * 128] for j in range(DS // 128)]
    gg_s[...] = jnp.concatenate(rows + [jnp.zeros((8 - len(rows), 128), F32)], axis=0)

    def gain_x(o, carry):
        send(gg_s, ggx_r.at[o - 1], ggx_ss, ggx_rs, dp=lax.rem(x + o, NX))
        return carry
    lax.fori_loop(1, NX, gain_x, 0)
    pass_x(1, scx)
    join(0, hx)

    own_sums(0, part0, yr0, outv)
    from_owners(0, outv)

    arrived(ggx_r, ggx_rs)
    ggy_s[...] = gg_s[...] + jnp.sum(ggx_r[...], axis=0)

    def gain_y(o, carry):
        send(ggy_s, ggy_r.at[o - 1], ggy_ss, ggy_rs, mlp=lax.rem(y + o, NY))
        return carry
    lax.fori_loop(1, NY, gain_y, 0)

    end_x(0, cotx)
    arrived(hx.at[pl.ds(1, NX - 1), its_blocks], join_rs.at[0])
    gdn[...] = dot(hx[...].reshape(NX * T, FQ), cotx[...].reshape(NX * T, DS), 0, 0)
    own_sums(1, part1, yr1, gtv)
    from_owners(1, gtv)
    join(1, gpx)
    end_x(1, scx)
    arrived(gpx.at[pl.ds(1, NX - 1), its_blocks], join_rs.at[1])
    product = dot(scx[...].reshape(NX * T, DS), gpx[...].reshape(NX * T, FQ), 0, 0)
    pieces = FQ // 128
    for j in range(pieces):
        gup[pl.ds(j, DS, stride=pieces), :] = product[:, j * 128 : (j + 1) * 128]
    for k in range(2):
        arrived(sib_s.at[k], sib_ss.at[k])
        arrived(zs.at[k, pl.ds(0, NZ - 1)], z_ss.at[k])
    arrived(stat_r, stat_ss)
    arrived(hid.at[0, pl.ds(0, NZ - 1)], ag_ss.at[0])
    arrived(hid.at[0], rel_ss.at[0])
    arrived(gp.at[:, pl.ds(0, 5)], ag_ss.at[1])
    arrived(gp.at[0, pl.ds(0, 5)], rel_ss.at[1])
    for k, buf in enumerate((cotx, scx)):
        arrived(buf.at[pl.ds(0, NX - 1)], x_ss.at[k])
    for k, buf in enumerate((hx, gpx)):
        arrived(buf.at[pl.ds(1, NX - 1), my_blocks], q_ss.at[k])
        arrived(buf.at[pl.ds(1, NX - 1), my_blocks], join_ss.at[k])
    arrived(yr0, y_ss.at[0])
    arrived(yr1, y_ss.at[1])
    arrived(outv.at[:, pl.ds(0, 3)], yag_ss.at[0])
    arrived(ggx_r, ggx_ss)

    from_owners_end(0, outv)
    out[...] = outv[...].reshape(T, DS)
    from_owners_end(1, gtv)
    gt[...] = gtv[...].reshape(T, DS)
    arrived(ggy_r, ggy_rs)
    gains = ggy_s[...] + jnp.sum(ggy_r[...], axis=0)
    gg[...] = jnp.concatenate([gains[j : j + 1] for j in range(DS // 128)], axis=1).reshape(DS)
    arrived(gtv.at[:, pl.ds(0, 3)], yag_ss.at[1])
    arrived(ggy_r, ggy_ss)


def place(*refs):
    made, given, sems = refs[0:5], refs[5:10], refs[10]
    copies = [pltpu.make_async_copy(src, dst, sems.at[k]) for k, (src, dst) in enumerate(zip(made, given))]
    for copy in copies:
        copy.start()
    for copy in copies:
        copy.wait()


def solution(mesh):
    NX, NZ, NY = mesh.shape["dp"], mesh.shape["width"] // 2, mesh.shape["mlp"]

    def shards(tokens, gain, up_weight, down_weight, cotangent):
        T, DS = tokens.shape
        FS = up_weight.shape[1]
        FH, FQ = FS // 2, FS // NX
        vmem, dma = pltpu.VMEM, pltpu.SemaphoreType.DMA
        results = (
            jax.ShapeDtypeStruct((T, DS), BF16),
            jax.ShapeDtypeStruct((T, DS), BF16),
            jax.ShapeDtypeStruct((DS,), F32),
            jax.ShapeDtypeStruct((DS * FQ // 128, 128), F32),
            jax.ShapeDtypeStruct((FQ, DS), F32),
        )
        call = pl.pallas_call(
            functools.partial(kernel, (NX, NZ, NY, DS * 2 * NZ)),
            out_shape=results,
            in_specs=[pl.BlockSpec(memory_space=pltpu.HBM)] * 5,
            out_specs=[pl.BlockSpec(memory_space=pltpu.VMEM)] * 5,
            scratch_shapes=[
                vmem((T, DS), BF16), vmem((DS,), F32), vmem((DS, FS), BF16), vmem((FS, DS), BF16),
                vmem((NX, T, DS), BF16), vmem((NX, T, DS), BF16), vmem((T, DS), F32), vmem((T, EXTRA), F32),
                vmem((2, 8, 128), F32), vmem((2 * NZ - 1, 8, 128), F32),
                vmem((2, T, FH), BF16), vmem((2, T, FH), BF16), vmem((2, NZ, TB, FH), F32),
                vmem((2, NZ, TB, FH), BF16), vmem((2, 6, TB, FH), BF16),
                vmem((2, 2, TB, FH // 2), BF16), vmem((2, 2, TB, FH), BF16),
                vmem((T + TB, DS), BF16), vmem((T, EXTRA), F32),
                vmem((2, NZ, TB, FH), BF16), vmem((2, NZ, TB, FH + EXTRA), BF16),
                vmem((NX, NZ, TB, FQ), BF16), vmem((NX, NZ, TB, FQ), BF16),
                *(
                    shape
                    for _ in range(2)
                    for shape in (
                        vmem((NY, TB, DS), BF16), vmem((2, NY - 1, TB, DS), BF16), vmem((NY, TB, DS), F32),
                    )
                ),
                vmem((2, NY // 2, TB, DS), BF16), vmem((2, NY // 2, TB, DS), BF16),
                vmem((8, DS), F32), vmem((8, 128), F32), vmem((NX - 1, 8, 128), F32),
                vmem((8, 128), F32), vmem((NY - 1, 8, 128), F32),
                dma((7,)), dma((2,)), dma((2,)), dma, dma, dma((2,)), dma((2, 8)),
                dma((2,)), dma((2, 8)), dma((4,)), dma((2,)), dma((3,)),
                dma((2,)), dma((2, 4)), dma((2,)), dma((2,)), dma((2,)), dma((2,)),
                dma((2,)), dma((2,)), dma((2,)), dma((2, 4)), dma, dma, dma, dma,
                pltpu.SemaphoreType.REGULAR, pltpu.SemaphoreType.REGULAR,
            ],
            compiler_params=pltpu.CompilerParams(
                collective_id=0, has_side_effects=True, vmem_limit_bytes=48 * 1024 * 1024
            ),
            cost_estimate=pl.CostEstimate(
                flops=12 * T * DS * FS, bytes_accessed=4 * DS * FS + 8 * DS * FQ, transcendentals=2 * TB * FH
            ),
        )
        put = pl.pallas_call(
            place,
            out_shape=results,
            in_specs=[pl.BlockSpec(memory_space=pltpu.VMEM)] * 5,
            out_specs=[pl.BlockSpec(memory_space=pltpu.HBM)] * 5,
            scratch_shapes=[dma((5,))],
            compiler_params=pltpu.CompilerParams(vmem_limit_bytes=4 * 1024 * 1024),
        )
        output, grad_tokens, grad_gain, grad_up, grad_down = put(
            *call(*(pltpu.with_memory_space_constraint(a, pltpu.HBM) for a in (tokens, gain, up_weight, down_weight, cotangent)))
        )
        return output, grad_tokens, grad_gain, grad_up.reshape(DS, 1, FQ), grad_down[None, :, :]

    placed = (P("dp", "width"), P("width"), P("width", "mlp"), P("mlp", "width"), P("dp", "width"))
    return jax.shard_map(
        shards,
        mesh=mesh,
        in_specs=placed,
        out_specs=(
            P("dp", "width"),
            P("dp", "width"),
            P("width"),
            P("width", "mlp", "dp"),
            P("mlp", "dp", "width"),
        ),
        check_vma=False,
    )
```

```python
import functools

import jax
import jax.numpy as jnp
from jax import lax
from jax.experimental import pallas as pl
from jax.experimental.pallas import tpu as pltpu
from jax.sharding import PartitionSpec as P

MESH = pl.DeviceIdType.MESH
F32, BF16 = jnp.float32, jnp.bfloat16
TB = 16
EXTRA = 128

inv_root_two = 0.7071067811865476
inv_root_two_pi = 0.3989422804014327


def dot(left, right, left_dim, right_dim):
    return lax.dot_general(
        left, right, (((left_dim,), (right_dim,)), ((), ())), preferred_element_type=F32
    )


def pack(first, second):
    lane = lax.broadcasted_iota(jnp.int32, (first.shape[0], EXTRA), 1)
    high_one, high_two = first.astype(BF16).astype(F32), second.astype(BF16).astype(F32)
    held = jnp.where(lane == 0, high_one, 0.0)
    held = jnp.where(lane == 1, high_two, held)
    held = jnp.where(lane == 2, first - high_one, held)
    held = jnp.where(lane == 3, second - high_two, held)
    return held.astype(BF16)


def unpack(held):
    return held[:, 0:1] + held[:, 2:3], held[:, 1:2] + held[:, 3:4]


def send(src, dst, ss, rs, **where):
    pltpu.make_async_remote_copy(
        src_ref=src, dst_ref=dst, send_sem=ss, recv_sem=rs, device_id=where, device_id_type=MESH
    ).start()


def arrived(ref, sem):
    pltpu.make_async_copy(ref, ref, sem).wait()


def ring(axis, me, device=lambda position: position):
    def at(o):
        return lax.rem(me + o % 8, 8)
    return at, lambda o: {axis: device(at(o))}


def lanes_of(block, side):
    cut = block.shape[-1] // 256 * 128
    return block.at[:, pl.ds(0, cut) if side == 0 else pl.ds(cut, block.shape[-1] - cut)]


def scatter(to_whom, terms, got, halves, ss, rs):
    at, to = to_whom
    for side, o in ((0, 1), (1, -1)):
        send(terms.at[at(3 * o)], got.at[4 + side], ss, rs.at[4 + side], **to(o))
    for side, o in ((0, 2), (1, -2)):
        send(lanes_of(terms.at[at(4)], side), halves[side], ss, rs.at[6 + side], **to(o))
    for side, o in ((0, 1), (1, -1)):
        send(terms.at[at(o)], got.at[side], ss, rs.at[side], **to(o))


def scatter_pass(to_whom, own, got, halves, sums, ss, rs):
    at, to = to_whom
    for side, o in ((0, 2), (1, -2)):
        arrived(got.at[4 + side], rs.at[4 + side])
        arrived(halves[side], rs.at[6 + side])
        term = own[at(o)] + got[4 + side].astype(F32)
        half = halves[side][...].astype(F32)
        cut = term.shape[-1] // 256 * 128
        low, high = term[:, 0:cut], term[:, cut:]
        sums[side, :, 0:cut] = (low + half if side == 0 else low).astype(BF16)
        sums[side, :, cut:] = (high if side == 0 else high + half).astype(BF16)
        send(sums.at[side], got.at[2 + side], ss, rs.at[2 + side], **to(o))


def scatter_sum(to_whom, own, got, rs):
    at, _ = to_whom
    for slot in range(4):
        arrived(got.at[slot], rs.at[slot])
    return own[at(0)] + jnp.sum(got[0:4].astype(F32), axis=0)


def gather(to_whom, buf, ss, rs):
    at, to = to_whom
    block = buf.at[at(0)]
    for o, slot in ((2, 2), (-2, 3), (1, 0), (-1, 1)):
        send(block, block, ss, rs.at[slot], **to(o))


def gather_pass(here, buf, ss, sems, use):
    at, _ = here
    for side, o in ((0, 1), (1, -1)):
        block = buf.at[at(-2 * o)]
        arrived(block, sems[0][1].at[2 + side])
        half = lanes_of(block, side)
        for (_, to), there, first in sems:
            send(block, block, ss, there.at[first + side], **to(o))
            send(half, half, ss, there.at[first + 2 + side], **to(2 * o))
        use(block)


def gather_near(here, buf, rs, use):
    at, _ = here
    for side, o in ((0, -1), (1, 1)):
        arrived(buf.at[at(o)], rs.at[side])
        use(buf.at[at(o)])


def gather_far(here, buf, sems, first):
    at, _ = here
    for side, o in ((0, -3), (1, 3)):
        arrived(buf.at[at(o)], sems.at[first + side])
        arrived(lanes_of(buf.at[at(4)], side), sems.at[first + 2 + side])


def kernel(
    sizes, tok_h, gain_h, wup_h, wdn_h, cot_h, out, gt, gg, gup, gdn,
    tok, gain_v, wup, wdn, cotx, scx, normed, inv_col,
    stat_s, stat_r,
    sib_s, sib_r, own, zs, zr, zh, zc, leaning, away_col,
    hid, gp, hx, gpx,
    ys0, yr0, part0, ys1, yr1, part1,
    outv, gtv,
    gg_sum, gg_s, ggx_r, ggy_s, ggy_r,
    ld, sib_ss, sib_rs, stat_ss, stat_rs, z_ss, z_rs, ag_ss, ag_rs, far_rs, rel_ss, rel_rs,
    x_ss, x_rs, q_ss, q_rs, join_ss, join_rs, y_ss, y_rs, yag_ss, yag_rs, ggx_ss, ggx_rs, ggy_ss, ggy_rs,
    known, all_known,
):
    NX, NZ, NY, D = sizes
    T, DS = tok.shape
    TY = T // NY
    FS = wup.shape[1]
    FH, FQ = FS // 2, FS // NX
    NW = 2 * NZ
    x, w, y = lax.axis_index("dp"), lax.axis_index("width"), lax.axis_index("mlp")
    z = lax.div(w, 2)
    c = w - 2 * z
    sibling = 2 * z + 1 - c

    over_z = ring("width", z, lambda position: 2 * position + c)
    across_z = ring("width", z, lambda position: 2 * position + 1 - c)

    def quarter(q):
        first = q * FQ
        h = lax.div(first, FH)
        return h, pl.ds(pl.multiple_of(first - h * FH, FQ), FQ)

    mine = pl.ds(pl.multiple_of(c * FH, FH), FH)
    other = pl.ds(pl.multiple_of(FH - c * FH, FH), FH)

    barrier = pltpu.get_barrier_semaphore()
    over_y = ring("mlp", y)

    def signal(semaphore, **where):
        pl.semaphore_signal(semaphore, inc=1, device_id=where, device_id_type=MESH)

    for o in (2, -2, 1, -1):
        signal(barrier, **over_z[1](o))
        signal(barrier, **over_y[1](o))
    for o in range(1, NX):
        signal(barrier, dp=lax.rem(x + o, NX))
    signal(barrier, width=sibling)

    loads = [
        pltpu.make_async_copy(tok_h, tok, ld.at[0]),
        pltpu.make_async_copy(gain_h, gain_v, ld.at[1]),
        pltpu.make_async_copy(wup_h.at[:, other], wup.at[:, other], ld.at[2]),
        pltpu.make_async_copy(cot_h, cotx.at[0], ld.at[3]),
        pltpu.make_async_copy(wdn_h.at[other], wdn.at[other], ld.at[4]),
        pltpu.make_async_copy(wup_h.at[:, mine], wup.at[:, mine], ld.at[5]),
        pltpu.make_async_copy(wdn_h.at[mine], wdn.at[mine], ld.at[6]),
    ]
    for load in loads:
        load.start()

    loads[0].wait()
    loads[1].wait()
    values = tok[...].astype(F32)
    total = jnp.sum(values, axis=1, keepdims=True)
    shifted = values - total * (1.0 / DS)
    g_all = gain_v[...].reshape(1, DS)
    leaning[0:T] = (shifted * g_all).astype(BF16)
    row = lax.broadcasted_iota(jnp.int32, (TB, DS), 0)
    g_one = g_all.astype(BF16).astype(F32)
    g_two = (g_all - g_one).astype(BF16).astype(F32)
    g_rows = jnp.where(row == 0, g_one, jnp.where(row == 1, g_two, jnp.where(row == 2, g_all - g_one - g_two, 0.0)))
    leaning[T:] = g_rows.astype(BF16)
    loads[2].wait()
    its_half = dot(leaning[...], wup[:, other], 1, 0)
    sib_s[0] = its_half[0:T].astype(BF16)

    loads[3].wait()
    loads[4].wait()
    sib_s[1] = dot(cotx[0], wdn[other, :], 1, 1).astype(BF16)
    pl.semaphore_wait(barrier, 8 + NX)
    for k in range(2):
        send(sib_s.at[k], sib_r.at[k], sib_ss.at[k], sib_rs.at[k], width=sibling)
    signal(known, width=sibling)
    for o in (2, -2):
        signal(known, **over_z[1](o))
        signal(known, **over_y[1](o))

    loads[5].wait()
    my_half = dot(leaning[...], wup[:, mine], 1, 0)
    own[0] = my_half[0:T].reshape(NZ, TB, FH)
    loads[6].wait()
    own[1] = dot(cotx[0], wdn[mine, :], 1, 1).reshape(NZ, TB, FH)

    shifted = tok[...].astype(F32) - total * (1.0 / DS)
    spread = jnp.sum(shifted * shifted, axis=1, keepdims=True)
    total_row = jnp.transpose(jnp.broadcast_to(total, (T, EXTRA)))[0:1]
    spread_row = jnp.transpose(jnp.broadcast_to(spread, (T, EXTRA)))[0:1]
    for h, half in ((c, my_half), (1 - c, its_half)):
        lean = jnp.sum(half[T:], axis=0, keepdims=True)
        stat_s[h, 0:1, 0:T] = total_row
        stat_s[h, 1:2, 0:T] = spread_row
        for j in range(FH // 128):
            stat_s[h, 2 + j : 3 + j, :] = lean[:, j * 128 : (j + 1) * 128]

    def merge(k):
        arrived(sib_r.at[k], sib_rs.at[k])
        both = own[k] + sib_r[k].astype(F32).reshape(NZ, TB, FH)
        own[k] = both
        zs[k] = both.astype(BF16)
        scatter(over_z, zs.at[k], zr.at[k], [zh.at[k, 0], zh.at[k, 1]], z_ss.at[k], z_rs.at[k])

    def merge_pass(k):
        scatter_pass(
            over_z, own.at[k], zr.at[k], [zh.at[k, 0], zh.at[k, 1]], zc.at[k], z_ss.at[k], z_rs.at[k]
        )

    def tell(k, carry):
        peer = lax.rem(w + k, NW)
        send(stat_s.at[lax.rem(peer, 2)], stat_r.at[k - 1], stat_ss, stat_rs, width=peer)
        return carry

    merge(0)
    pl.semaphore_wait(known, 5)
    signal(all_known, width=sibling)
    merge(1)
    pl.semaphore_wait(all_known, 1)
    lax.fori_loop(1, NW, tell, 0)

    right, left = lax.rem(x + 1, NX), lax.rem(x + NX - 1, NX)
    first_rows, last_rows = pl.ds(0, T // 2), pl.ds(T // 2, T // 2)

    def spread_x(k, buf):
        send(buf.at[0], buf.at[1], x_ss.at[k], x_rs.at[k, 0], dp=right)
        send(buf.at[0], buf.at[NX - 1], x_ss.at[k], x_rs.at[k, 1], dp=left)

    def pass_x(k, buf):
        arrived(buf.at[1], x_rs.at[k, 0])
        send(buf.at[1, first_rows], buf.at[2, first_rows], x_ss.at[k], x_rs.at[k, 2], dp=right)
        arrived(buf.at[NX - 1], x_rs.at[k, 1])
        send(buf.at[NX - 1, last_rows], buf.at[2, last_rows], x_ss.at[k], x_rs.at[k, 3], dp=left)

    def end_x(k, buf):
        arrived(buf.at[2, first_rows], x_rs.at[k, 2])
        arrived(buf.at[2, last_rows], x_rs.at[k, 3])

    spread_x(0, cotx)
    merge_pass(0)
    merge_pass(1)

    arrived(stat_r, stat_rs)
    its = stat_r[...]
    my_stat = stat_s[c]
    sums, spreads = its[:, 0, :], its[:, 1, :]
    mean = (jnp.sum(sums, axis=0, keepdims=True) + my_stat[0:1]) * (1.0 / D)
    away, my_away = sums * (1.0 / DS) - mean, my_stat[0:1] * (1.0 / DS) - mean
    variance = (
        jnp.sum(spreads + DS * away * away, axis=0, keepdims=True) + my_stat[1:2] + DS * my_away * my_away
    ) * (1.0 / D)
    inv_std = lax.rsqrt(variance + 1e-06)
    mean_col = jnp.transpose(jnp.broadcast_to(mean[:, 0:T], (EXTRA, T)))
    std_col = jnp.transpose(jnp.broadcast_to(inv_std[:, 0:T], (EXTRA, T)))
    inv_col[...] = std_col
    aways = jnp.concatenate([away[:, 0:T], my_away[:, 0:T], jnp.zeros((EXTRA - NW, T), F32)], axis=0)
    away_col[...] = jnp.transpose(aways)
    token_rows = pl.ds(pl.multiple_of(z * TB, TB), TB)
    my_aways = away_col[token_rows, :]
    leans, shift = [], []
    for j in range(FH // 128):
        piece = [its[s, 2 + j : 3 + j, :] for s in range(NW - 1)] + [my_stat[2 + j : 3 + j, :]]
        leans.append(functools.reduce(jnp.add, piece))
        shift.append(functools.reduce(jnp.add, [my_aways[:, s : s + 1] * piece[s] for s in range(NW)]))
    lean_row = jnp.concatenate(leans, axis=1)
    shift = jnp.concatenate(shift, axis=1)

    def hand_over(k):
        return lambda block: send(block, block, rel_ss.at[k], rel_rs.at[k], width=sibling)

    pre_act = (scatter_sum(over_z, own.at[0], zr.at[0], z_rs.at[0]) + shift) * inv_col[token_rows, 0:1]
    below = 0.5 * (1.0 + lax.erf(pre_act * inv_root_two))
    hid[c, z] = (pre_act * below).astype(BF16)
    units, grads = hid.at[c], gp.at[c]
    gather(over_z, units, ag_ss.at[0], ag_rs.at[0])
    hand_over(0)(hid.at[c, z])
    slope = below + pre_act * jnp.exp(-0.5 * pre_act * pre_act) * inv_root_two_pi
    grad_hidden = scatter_sum(over_z, own.at[1], zr.at[1], z_rs.at[1])
    grad_pre = (grad_hidden * slope).astype(BF16)
    wide = grad_pre.astype(F32)
    gp[c, z, :, 0:FH] = grad_pre
    gp[c, z, :, FH:] = pack(
        jnp.sum(wide * lean_row, axis=1, keepdims=True), jnp.sum(wide * pre_act, axis=1, keepdims=True)
    )
    gather(over_z, grads, ag_ss.at[1], ag_rs.at[1])
    hand_over(1)(gp.at[c, z])

    for j in range(DS // 128):
        cols = slice(j * 128, (j + 1) * 128)
        normal = (tok[:, cols].astype(F32) - mean_col) * std_col
        normed[:, cols] = normal
        scx[0, :, cols] = (normal * g_all[:, cols]).astype(BF16)
    spread_x(1, scx)

    gather_pass(over_z, units, ag_ss.at[0], [(over_z, ag_rs.at[0], 4)], hand_over(0))
    gather_near(over_z, units, ag_rs.at[0], hand_over(0))
    gather_pass(
        over_z, grads, ag_ss.at[1], [(over_z, ag_rs.at[1], 4), (across_z, far_rs, 0)], hand_over(1)
    )
    gather_near(over_z, grads, ag_rs.at[1], hand_over(1))
    pass_x(0, cotx)
    pass_x(1, scx)

    block_of, _ = over_z
    near, far = (0, 1, -1, 2, -2), (3, -3, 4)

    half_ring = NY // 2
    slot = lax.rem(y, half_ring)

    def next_to(o):
        return lax.rem(y + o % NY, NY)

    def own_sums(k, part, got, result):
        arrived(got, y_rs.at[k])
        for side in range(2):
            block = lax.rem(y + side * half_ring, NY)
            summed = part[block] + jnp.sum(got[side].astype(F32), axis=0)
            result[lax.div(block, half_ring), lax.rem(block, half_ring)] = summed.astype(BF16)

    def from_owners(k, buf):
        both = buf.at[:, slot]
        for side, o in ((0, 1), (1, -1)):
            one = buf.at[side, slot]
            send(one, one, yag_ss.at[k], yag_rs.at[k, 2 + side], mlp=next_to(2 * o))
            send(both, both, yag_ss.at[k], yag_rs.at[k, side], mlp=next_to(o))

    def from_owners_end(k, buf):
        for side, o in ((0, -1), (1, 1)):
            arrived(buf.at[:, lax.rem(next_to(o), half_ring)], yag_rs.at[k, side])
            arrived(buf.at[side, lax.rem(next_to(2 * o), half_ring)], yag_rs.at[k, 2 + side])

    def rows_of(buf, h, blocks, lanes):
        return jnp.concatenate([buf[h, block_of(o), :, lanes] for o in blocks], axis=0)

    def to_owners(k, blocks, terms, part, sent, got):
        for i, o in enumerate(blocks):
            block = block_of(o)
            part[block] = terms[i * TB : (i + 1) * TB]
            sent[block] = terms[i * TB : (i + 1) * TB].astype(BF16)
            for side in range(2):
                owner = lax.rem(block + side * half_ring, NY)

                @pl.when(owner != y)
                def _():
                    place_there = got.at[side, lax.rem(owner - y + NY - 1, NY)]
                    send(sent.at[block], place_there, y_ss.at[k], y_rs.at[k], mlp=owner)

    def output_terms(blocks):
        units = slice(0, FH)
        term = dot(rows_of(hid, 0, blocks, units), wdn[0:FH, :], 1, 0)
        term = term + dot(rows_of(hid, 1, blocks, units), wdn[FH:, :], 1, 0)
        to_owners(0, blocks, term, part0, ys0, yr0)

    def gradient_terms(blocks):
        units, beside = slice(0, FH), slice(FH, FH + EXTRA)
        term = dot(rows_of(gp, 0, blocks, units), wup[:, 0:FH], 1, 1)
        term = term + dot(rows_of(gp, 1, blocks, units), wup[:, FH:], 1, 1)
        side = rows_of(gp, 0, blocks, beside).astype(F32) + rows_of(gp, 1, blocks, beside).astype(F32)
        first, second = unpack(side)
        tokens = [pl.ds(pl.multiple_of(block_of(o) * TB, TB), TB) for o in blocks]
        normal = jnp.concatenate([normed[rows, :] for rows in tokens], axis=0)
        scale = jnp.concatenate([inv_col[rows, 0:1] for rows in tokens], axis=0)
        corrected = scale * (
            term * gain_v[...].reshape(1, DS) - first * (1.0 / D) - normal * (second * (1.0 / D))
        )
        to_owners(1, blocks, corrected, part1, ys1, yr1)
        return jnp.sum((term * normal).reshape(len(blocks) * TB // 8, 8, DS), axis=0)

    my_blocks = pl.ds(pl.multiple_of(c * (NZ // 2), NZ // 2), NZ // 2)
    its_blocks = pl.ds(pl.multiple_of((1 - c) * (NZ // 2), NZ // 2), NZ // 2)

    def share(k, buf, dst):
        def one(o, carry):
            peer = lax.rem(x + o, NX)
            h, lanes = quarter(peer)
            send(buf.at[h, my_blocks, :, lanes], dst.at[o, my_blocks], q_ss.at[k], q_rs.at[k], dp=peer)
            return carry
        lax.fori_loop(1, NX, one, 0)
        h, lanes = quarter(x)
        dst[0] = buf[h, :, :, lanes]

    def join(k, dst):
        halves = dst.at[pl.ds(1, NX - 1), my_blocks]
        arrived(halves, q_rs.at[k])
        send(halves, halves, join_ss.at[k], join_rs.at[k], width=sibling)

    arrived(hid.at[1 - c, pl.ds(0, 5)], rel_rs.at[0])
    output_terms(near)
    gather_far(over_z, units, ag_rs.at[0], 4)
    for o in far:
        block = hid.at[c, block_of(o)]
        send(block, block, rel_ss.at[0], rel_rs.at[2], width=sibling)
    arrived(gp.at[1 - c, pl.ds(0, 5)], rel_rs.at[1])
    gg_sum[...] = gradient_terms(near)
    arrived(hid.at[1 - c, pl.ds(0, 3)], rel_rs.at[2])
    output_terms(far)
    share(0, hid, hx)
    gather_far(over_z, grads, ag_rs.at[1], 4)
    gather_far(over_z, gp.at[1 - c], far_rs, 0)
    share(1, gp, gpx)
    gains = gg_sum[...] + gradient_terms(far)
    gains = jnp.sum(gains, axis=0, keepdims=True)
    rows = [gains[:, j * 128 : (j + 1) * 128] for j in range(DS // 128)]
    gg_s[...] = jnp.concatenate(rows + [jnp.zeros((8 - len(rows), 128), F32)], axis=0)

    def gain_x(o, carry):
        send(gg_s, ggx_r.at[o - 1], ggx_ss, ggx_rs, dp=lax.rem(x + o, NX))
        return carry
    lax.fori_loop(1, NX, gain_x, 0)
    join(0, hx)

    own_sums(0, part0, yr0, outv)
    from_owners(0, outv)

    arrived(ggx_r, ggx_rs)
    ggy_s[...] = gg_s[...] + jnp.sum(ggx_r[...], axis=0)

    def gain_y(o, carry):
        send(ggy_s, ggy_r.at[o - 1], ggy_ss, ggy_rs, mlp=lax.rem(y + o, NY))
        return carry
    lax.fori_loop(1, NY, gain_y, 0)

    join(1, gpx)

    end_x(0, cotx)
    arrived(hx.at[pl.ds(1, NX - 1), its_blocks], join_rs.at[0])
    gdn[...] = dot(hx[...].reshape(NX * T, FQ), cotx[...].reshape(NX * T, DS), 0, 0)
    own_sums(1, part1, yr1, gtv)
    from_owners(1, gtv)
    end_x(1, scx)
    arrived(gpx.at[pl.ds(1, NX - 1), its_blocks], join_rs.at[1])
    product = dot(scx[...].reshape(NX * T, DS), gpx[...].reshape(NX * T, FQ), 0, 0)
    pieces = FQ // 128
    for j in range(pieces):
        gup[pl.ds(j, DS, stride=pieces), :] = product[:, j * 128 : (j + 1) * 128]
    for k in range(2):
        arrived(sib_s.at[k], sib_ss.at[k])
        arrived(zs.at[k, pl.ds(0, NZ - 1)], z_ss.at[k])
    arrived(stat_r, stat_ss)
    arrived(hid.at[0, pl.ds(0, NZ - 1)], ag_ss.at[0])
    arrived(hid.at[0], rel_ss.at[0])
    arrived(gp.at[:, pl.ds(0, 5)], ag_ss.at[1])
    arrived(gp.at[0, pl.ds(0, 5)], rel_ss.at[1])
    for k, buf in enumerate((cotx, scx)):
        arrived(buf.at[pl.ds(0, NX - 1)], x_ss.at[k])
    for k, buf in enumerate((hx, gpx)):
        arrived(buf.at[pl.ds(1, NX - 1), my_blocks], q_ss.at[k])
        arrived(buf.at[pl.ds(1, NX - 1), my_blocks], join_ss.at[k])
    arrived(yr0, y_ss.at[0])
    arrived(yr1, y_ss.at[1])
    arrived(outv.at[:, pl.ds(0, 3)], yag_ss.at[0])
    arrived(ggx_r, ggx_ss)

    from_owners_end(0, outv)
    out[...] = outv[...].reshape(T, DS)
    from_owners_end(1, gtv)
    gt[...] = gtv[...].reshape(T, DS)
    arrived(ggy_r, ggy_rs)
    gains = ggy_s[...] + jnp.sum(ggy_r[...], axis=0)
    gg[...] = jnp.concatenate([gains[j : j + 1] for j in range(DS // 128)], axis=1).reshape(DS)
    arrived(gtv.at[:, pl.ds(0, 3)], yag_ss.at[1])
    arrived(ggy_r, ggy_ss)


def place(*refs):
    made, given, sems = refs[0:5], refs[5:10], refs[10]
    copies = [pltpu.make_async_copy(src, dst, sems.at[k]) for k, (src, dst) in enumerate(zip(made, given))]
    for copy in copies:
        copy.start()
    for copy in copies:
        copy.wait()


def solution(mesh):
    NX, NZ, NY = mesh.shape["dp"], mesh.shape["width"] // 2, mesh.shape["mlp"]

    def shards(tokens, gain, up_weight, down_weight, cotangent):
        T, DS = tokens.shape
        FS = up_weight.shape[1]
        FH, FQ = FS // 2, FS // NX
        vmem, dma = pltpu.VMEM, pltpu.SemaphoreType.DMA
        results = (
            jax.ShapeDtypeStruct((T, DS), BF16),
            jax.ShapeDtypeStruct((T, DS), BF16),
            jax.ShapeDtypeStruct((DS,), F32),
            jax.ShapeDtypeStruct((DS * FQ // 128, 128), F32),
            jax.ShapeDtypeStruct((FQ, DS), F32),
        )
        call = pl.pallas_call(
            functools.partial(kernel, (NX, NZ, NY, DS * 2 * NZ)),
            out_shape=results,
            in_specs=[pl.BlockSpec(memory_space=pltpu.HBM)] * 5,
            out_specs=[pl.BlockSpec(memory_space=pltpu.VMEM)] * 5,
            scratch_shapes=[
                vmem((T, DS), BF16), vmem((DS,), F32), vmem((DS, FS), BF16), vmem((FS, DS), BF16),
                vmem((NX, T, DS), BF16), vmem((NX, T, DS), BF16), vmem((T, DS), F32), vmem((T, EXTRA), F32),
                vmem((2, 8, 128), F32), vmem((2 * NZ - 1, 8, 128), F32),
                vmem((2, T, FH), BF16), vmem((2, T, FH), BF16), vmem((2, NZ, TB, FH), F32),
                vmem((2, NZ, TB, FH), BF16), vmem((2, 6, TB, FH), BF16),
                vmem((2, 2, TB, FH // 2), BF16), vmem((2, 2, TB, FH), BF16),
                vmem((T + TB, DS), BF16), vmem((T, EXTRA), F32),
                vmem((2, NZ, TB, FH), BF16), vmem((2, NZ, TB, FH + EXTRA), BF16),
                vmem((NX, NZ, TB, FQ), BF16), vmem((NX, NZ, TB, FQ), BF16),
                *(
                    shape
                    for _ in range(2)
                    for shape in (
                        vmem((NY, TB, DS), BF16), vmem((2, NY - 1, TB, DS), BF16), vmem((NY, TB, DS), F32),
                    )
                ),
                vmem((2, NY // 2, TB, DS), BF16), vmem((2, NY // 2, TB, DS), BF16),
                vmem((8, DS), F32), vmem((8, 128), F32), vmem((NX - 1, 8, 128), F32),
                vmem((8, 128), F32), vmem((NY - 1, 8, 128), F32),
                dma((7,)), dma((2,)), dma((2,)), dma, dma, dma((2,)), dma((2, 8)),
                dma((2,)), dma((2, 8)), dma((4,)), dma((2,)), dma((3,)),
                dma((2,)), dma((2, 4)), dma((2,)), dma((2,)), dma((2,)), dma((2,)),
                dma((2,)), dma((2,)), dma((2,)), dma((2, 4)), dma, dma, dma, dma,
                pltpu.SemaphoreType.REGULAR, pltpu.SemaphoreType.REGULAR,
            ],
            compiler_params=pltpu.CompilerParams(
                collective_id=0, has_side_effects=True, vmem_limit_bytes=48 * 1024 * 1024
            ),
            cost_estimate=pl.CostEstimate(
                flops=12 * T * DS * FS, bytes_accessed=4 * DS * FS + 8 * DS * FQ, transcendentals=2 * TB * FH
            ),
        )
        put = pl.pallas_call(
            place,
            out_shape=results,
            in_specs=[pl.BlockSpec(memory_space=pltpu.VMEM)] * 5,
            out_specs=[pl.BlockSpec(memory_space=pltpu.HBM)] * 5,
            scratch_shapes=[dma((5,))],
            compiler_params=pltpu.CompilerParams(vmem_limit_bytes=4 * 1024 * 1024),
        )
        output, grad_tokens, grad_gain, grad_up, grad_down = put(
            *call(*(pltpu.with_memory_space_constraint(a, pltpu.HBM) for a in (tokens, gain, up_weight, down_weight, cotangent)))
        )
        return output, grad_tokens, grad_gain, grad_up.reshape(DS, 1, FQ), grad_down[None, :, :]

    placed = (P("dp", "width"), P("width"), P("width", "mlp"), P("mlp", "width"), P("dp", "width"))
    return jax.shard_map(
        shards,
        mesh=mesh,
        in_specs=placed,
        out_specs=(
            P("dp", "width"),
            P("dp", "width"),
            P("width"),
            P("width", "mlp", "dp"),
            P("mlp", "dp", "width"),
        ),
        check_vma=False,
    )
```

```python
import functools

import jax
import jax.numpy as jnp
from jax import lax
from jax.experimental import pallas as pl
from jax.experimental.pallas import tpu as pltpu
from jax.sharding import PartitionSpec as P

MESH = pl.DeviceIdType.MESH
F32, BF16 = jnp.float32, jnp.bfloat16
TB = 16
EXTRA = 128

inv_root_two = 0.7071067811865476
inv_root_two_pi = 0.3989422804014327


def dot(left, right, left_dim, right_dim):
    return lax.dot_general(
        left, right, (((left_dim,), (right_dim,)), ((), ())), preferred_element_type=F32
    )


def pack(first, second):
    lane = lax.broadcasted_iota(jnp.int32, (first.shape[0], EXTRA), 1)
    high_one, high_two = first.astype(BF16).astype(F32), second.astype(BF16).astype(F32)
    held = jnp.where(lane == 0, high_one, 0.0)
    held = jnp.where(lane == 1, high_two, held)
    held = jnp.where(lane == 2, first - high_one, held)
    held = jnp.where(lane == 3, second - high_two, held)
    return held.astype(BF16)


def unpack(held):
    return held[:, 0:1] + held[:, 2:3], held[:, 1:2] + held[:, 3:4]


def send(src, dst, ss, rs, **where):
    pltpu.make_async_remote_copy(
        src_ref=src, dst_ref=dst, send_sem=ss, recv_sem=rs, device_id=where, device_id_type=MESH
    ).start()


def arrived(ref, sem):
    pltpu.make_async_copy(ref, ref, sem).wait()


def ring(axis, me, device=lambda position: position):
    def at(o):
        return lax.rem(me + o % 8, 8)
    return at, lambda o: {axis: device(at(o))}


def lanes_of(block, side):
    cut = block.shape[-1] // 256 * 128
    return block.at[:, pl.ds(0, cut) if side == 0 else pl.ds(cut, block.shape[-1] - cut)]


def scatter(to_whom, terms, got, halves, ss, rs):
    at, to = to_whom
    for side, o in ((0, 1), (1, -1)):
        send(terms.at[at(3 * o)], got.at[4 + side], ss, rs.at[4 + side], **to(o))
    for side, o in ((0, 2), (1, -2)):
        send(lanes_of(terms.at[at(4)], side), halves[side], ss, rs.at[6 + side], **to(o))
    for side, o in ((0, 1), (1, -1)):
        send(terms.at[at(o)], got.at[side], ss, rs.at[side], **to(o))


def scatter_pass(to_whom, own, got, halves, sums, ss, rs):
    at, to = to_whom
    for side, o in ((0, 2), (1, -2)):
        arrived(got.at[4 + side], rs.at[4 + side])
        arrived(halves[side], rs.at[6 + side])
        term = own[at(o)] + got[4 + side].astype(F32)
        half = halves[side][...].astype(F32)
        cut = term.shape[-1] // 256 * 128
        low, high = term[:, 0:cut], term[:, cut:]
        sums[side, :, 0:cut] = (low + half if side == 0 else low).astype(BF16)
        sums[side, :, cut:] = (high if side == 0 else high + half).astype(BF16)
        send(sums.at[side], got.at[2 + side], ss, rs.at[2 + side], **to(o))


def scatter_sum(to_whom, own, got, rs):
    at, _ = to_whom
    for slot in range(4):
        arrived(got.at[slot], rs.at[slot])
    return own[at(0)] + jnp.sum(got[0:4].astype(F32), axis=0)


def gather(to_whom, buf, ss, rs):
    at, to = to_whom
    block = buf.at[at(0)]
    for o, slot in ((2, 2), (-2, 3), (1, 0), (-1, 1)):
        send(block, block, ss, rs.at[slot], **to(o))


def gather_pass(here, buf, ss, sems, use):
    at, _ = here
    for side, o in ((0, 1), (1, -1)):
        block = buf.at[at(-2 * o)]
        arrived(block, sems[0][1].at[2 + side])
        half = lanes_of(block, side)
        for (_, to), there, first in sems:
            send(block, block, ss, there.at[first + side], **to(o))
            send(half, half, ss, there.at[first + 2 + side], **to(2 * o))
        use(block)


def gather_near(here, buf, rs, use):
    at, _ = here
    for side, o in ((0, -1), (1, 1)):
        arrived(buf.at[at(o)], rs.at[side])
        use(buf.at[at(o)])


def gather_far(here, buf, sems, first):
    at, _ = here
    for side, o in ((0, -3), (1, 3)):
        arrived(buf.at[at(o)], sems.at[first + side])
        arrived(lanes_of(buf.at[at(4)], side), sems.at[first + 2 + side])


def kernel(
    sizes, tok_h, gain_h, wup_h, wdn_h, cot_h, out, gt, gg, gup, gdn,
    tok, gain_v, wup, wdn, cotx, scx, normed, inv_col,
    stat_s, stat_r,
    sib_s, sib_r, own, zs, zr, zh, zc, leaning, away_col,
    hid, gp, hx, gpx,
    ys0, yr0, part0, ys1, yr1, part1,
    outv, gtv,
    gg_sum, gg_s, ggx_r, ggy_s, ggy_r,
    ld, sib_ss, sib_rs, stat_ss, stat_rs, z_ss, z_rs, ag_ss, ag_rs, far_rs, rel_ss, rel_rs,
    x_ss, x_rs, q_ss, q_rs, join_ss, join_rs, y_ss, y_rs, yag_ss, yag_rs, ggx_ss, ggx_rs, ggy_ss, ggy_rs,
    known, all_known,
):
    NX, NZ, NY, D = sizes
    T, DS = tok.shape
    TY = T // NY
    FS = wup.shape[1]
    FH, FQ = FS // 2, FS // NX
    NW = 2 * NZ
    x, w, y = lax.axis_index("dp"), lax.axis_index("width"), lax.axis_index("mlp")
    z = lax.div(w, 2)
    c = w - 2 * z
    sibling = 2 * z + 1 - c

    over_z = ring("width", z, lambda position: 2 * position + c)
    across_z = ring("width", z, lambda position: 2 * position + 1 - c)

    def quarter(q):
        first = q * FQ
        h = lax.div(first, FH)
        return h, pl.ds(pl.multiple_of(first - h * FH, FQ), FQ)

    mine = pl.ds(pl.multiple_of(c * FH, FH), FH)
    other = pl.ds(pl.multiple_of(FH - c * FH, FH), FH)

    barrier = pltpu.get_barrier_semaphore()
    over_y = ring("mlp", y)

    def signal(semaphore, **where):
        pl.semaphore_signal(semaphore, inc=1, device_id=where, device_id_type=MESH)

    for o in (2, -2, 1, -1):
        signal(barrier, **over_z[1](o))
        signal(barrier, **over_y[1](o))
    for o in range(1, NX):
        signal(barrier, dp=lax.rem(x + o, NX))
    signal(barrier, width=sibling)

    loads = [
        pltpu.make_async_copy(tok_h, tok, ld.at[0]),
        pltpu.make_async_copy(gain_h, gain_v, ld.at[1]),
        pltpu.make_async_copy(wup_h.at[:, other], wup.at[:, other], ld.at[2]),
        pltpu.make_async_copy(cot_h, cotx.at[0], ld.at[3]),
        pltpu.make_async_copy(wdn_h.at[other], wdn.at[other], ld.at[4]),
        pltpu.make_async_copy(wup_h.at[:, mine], wup.at[:, mine], ld.at[5]),
        pltpu.make_async_copy(wdn_h.at[mine], wdn.at[mine], ld.at[6]),
    ]
    for load in loads:
        load.start()

    loads[0].wait()
    loads[1].wait()
    values = tok[...].astype(F32)
    total = jnp.sum(values, axis=1, keepdims=True)
    shifted = values - total * (1.0 / DS)
    g_all = gain_v[...].reshape(1, DS)
    leaning[0:T] = (shifted * g_all).astype(BF16)
    row = lax.broadcasted_iota(jnp.int32, (TB, DS), 0)
    g_one = g_all.astype(BF16).astype(F32)
    g_two = (g_all - g_one).astype(BF16).astype(F32)
    g_rows = jnp.where(row == 0, g_one, jnp.where(row == 1, g_two, jnp.where(row == 2, g_all - g_one - g_two, 0.0)))
    leaning[T:] = g_rows.astype(BF16)
    loads[2].wait()
    its_half = dot(leaning[...], wup[:, other], 1, 0)
    sib_s[0] = its_half[0:T].astype(BF16)

    pl.semaphore_wait(barrier, 8 + NX)
    send(sib_s.at[0], sib_r.at[0], sib_ss.at[0], sib_rs.at[0], width=sibling)
    signal(known, width=sibling)
    for o in (2, -2):
        signal(known, **over_z[1](o))
        signal(known, **over_y[1](o))

    loads[3].wait()
    loads[4].wait()
    sib_s[1] = dot(cotx[0], wdn[other, :], 1, 1).astype(BF16)
    send(sib_s.at[1], sib_r.at[1], sib_ss.at[1], sib_rs.at[1], width=sibling)
    loads[5].wait()
    my_half = dot(leaning[...], wup[:, mine], 1, 0)
    own[0] = my_half[0:T].reshape(NZ, TB, FH)
    loads[6].wait()
    own[1] = dot(cotx[0], wdn[mine, :], 1, 1).reshape(NZ, TB, FH)

    shifted = tok[...].astype(F32) - total * (1.0 / DS)
    spread = jnp.sum(shifted * shifted, axis=1, keepdims=True)
    total_row = jnp.transpose(jnp.broadcast_to(total, (T, EXTRA)))[0:1]
    spread_row = jnp.transpose(jnp.broadcast_to(spread, (T, EXTRA)))[0:1]
    for h, half in ((c, my_half), (1 - c, its_half)):
        lean = jnp.sum(half[T:], axis=0, keepdims=True)
        stat_s[h, 0:1, 0:T] = total_row
        stat_s[h, 1:2, 0:T] = spread_row
        for j in range(FH // 128):
            stat_s[h, 2 + j : 3 + j, :] = lean[:, j * 128 : (j + 1) * 128]

    def merge(k):
        arrived(sib_r.at[k], sib_rs.at[k])
        both = own[k] + sib_r[k].astype(F32).reshape(NZ, TB, FH)
        own[k] = both
        zs[k] = both.astype(BF16)
        scatter(over_z, zs.at[k], zr.at[k], [zh.at[k, 0], zh.at[k, 1]], z_ss.at[k], z_rs.at[k])

    def merge_pass(k):
        scatter_pass(
            over_z, own.at[k], zr.at[k], [zh.at[k, 0], zh.at[k, 1]], zc.at[k], z_ss.at[k], z_rs.at[k]
        )

    def tell(k, carry):
        peer = lax.rem(w + k, NW)
        send(stat_s.at[lax.rem(peer, 2)], stat_r.at[k - 1], stat_ss, stat_rs, width=peer)
        return carry

    merge(0)
    pl.semaphore_wait(known, 5)
    signal(all_known, width=sibling)
    merge(1)
    pl.semaphore_wait(all_known, 1)
    lax.fori_loop(1, NW, tell, 0)

    right, left = lax.rem(x + 1, NX), lax.rem(x + NX - 1, NX)
    first_rows, last_rows = pl.ds(0, T // 2), pl.ds(T // 2, T // 2)

    def spread_x(k, buf):
        send(buf.at[0], buf.at[1], x_ss.at[k], x_rs.at[k, 0], dp=right)
        send(buf.at[0], buf.at[NX - 1], x_ss.at[k], x_rs.at[k, 1], dp=left)

    def pass_x(k, buf):
        arrived(buf.at[1], x_rs.at[k, 0])
        send(buf.at[1, first_rows], buf.at[2, first_rows], x_ss.at[k], x_rs.at[k, 2], dp=right)
        arrived(buf.at[NX - 1], x_rs.at[k, 1])
        send(buf.at[NX - 1, last_rows], buf.at[2, last_rows], x_ss.at[k], x_rs.at[k, 3], dp=left)

    def end_x(k, buf):
        arrived(buf.at[2, first_rows], x_rs.at[k, 2])
        arrived(buf.at[2, last_rows], x_rs.at[k, 3])

    spread_x(0, cotx)
    merge_pass(0)
    merge_pass(1)

    arrived(stat_r, stat_rs)
    its = stat_r[...]
    my_stat = stat_s[c]
    sums, spreads = its[:, 0, :], its[:, 1, :]
    mean = (jnp.sum(sums, axis=0, keepdims=True) + my_stat[0:1]) * (1.0 / D)
    away, my_away = sums * (1.0 / DS) - mean, my_stat[0:1] * (1.0 / DS) - mean
    variance = (
        jnp.sum(spreads + DS * away * away, axis=0, keepdims=True) + my_stat[1:2] + DS * my_away * my_away
    ) * (1.0 / D)
    inv_std = lax.rsqrt(variance + 1e-06)
    mean_col = jnp.transpose(jnp.broadcast_to(mean[:, 0:T], (EXTRA, T)))
    std_col = jnp.transpose(jnp.broadcast_to(inv_std[:, 0:T], (EXTRA, T)))
    inv_col[...] = std_col
    aways = jnp.concatenate([away[:, 0:T], my_away[:, 0:T], jnp.zeros((EXTRA - NW, T), F32)], axis=0)
    away_col[...] = jnp.transpose(aways)
    token_rows = pl.ds(pl.multiple_of(z * TB, TB), TB)
    my_aways = away_col[token_rows, :]
    leans, shift = [], []
    for j in range(FH // 128):
        piece = [its[s, 2 + j : 3 + j, :] for s in range(NW - 1)] + [my_stat[2 + j : 3 + j, :]]
        leans.append(functools.reduce(jnp.add, piece))
        shift.append(functools.reduce(jnp.add, [my_aways[:, s : s + 1] * piece[s] for s in range(NW)]))
    lean_row = jnp.concatenate(leans, axis=1)
    shift = jnp.concatenate(shift, axis=1)

    def hand_over(k):
        return lambda block: send(block, block, rel_ss.at[k], rel_rs.at[k], width=sibling)

    pre_act = (scatter_sum(over_z, own.at[0], zr.at[0], z_rs.at[0]) + shift) * inv_col[token_rows, 0:1]
    below = 0.5 * (1.0 + lax.erf(pre_act * inv_root_two))
    hid[c, z] = (pre_act * below).astype(BF16)
    units, grads = hid.at[c], gp.at[c]
    gather(over_z, units, ag_ss.at[0], ag_rs.at[0])
    hand_over(0)(hid.at[c, z])
    slope = below + pre_act * jnp.exp(-0.5 * pre_act * pre_act) * inv_root_two_pi
    grad_hidden = scatter_sum(over_z, own.at[1], zr.at[1], z_rs.at[1])
    grad_pre = (grad_hidden * slope).astype(BF16)
    wide = grad_pre.astype(F32)
    gp[c, z, :, 0:FH] = grad_pre
    gp[c, z, :, FH:] = pack(
        jnp.sum(wide * lean_row, axis=1, keepdims=True), jnp.sum(wide * pre_act, axis=1, keepdims=True)
    )
    gather(over_z, grads, ag_ss.at[1], ag_rs.at[1])
    hand_over(1)(gp.at[c, z])

    for j in range(DS // 128):
        cols = slice(j * 128, (j + 1) * 128)
        normal = (tok[:, cols].astype(F32) - mean_col) * std_col
        normed[:, cols] = normal
        scx[0, :, cols] = (normal * g_all[:, cols]).astype(BF16)
    spread_x(1, scx)

    gather_pass(over_z, units, ag_ss.at[0], [(over_z, ag_rs.at[0], 4)], hand_over(0))
    gather_near(over_z, units, ag_rs.at[0], hand_over(0))
    gather_pass(
        over_z, grads, ag_ss.at[1], [(over_z, ag_rs.at[1], 4), (across_z, far_rs, 0)], hand_over(1)
    )
    gather_near(over_z, grads, ag_rs.at[1], hand_over(1))
    pass_x(0, cotx)
    pass_x(1, scx)

    block_of, _ = over_z
    near, far = (0, 1, -1, 2, -2), (3, -3, 4)

    half_ring = NY // 2
    slot = lax.rem(y, half_ring)

    def next_to(o):
        return lax.rem(y + o % NY, NY)

    def own_sums(k, part, got, result):
        arrived(got, y_rs.at[k])
        for side in range(2):
            block = lax.rem(y + side * half_ring, NY)
            summed = part[block] + jnp.sum(got[side].astype(F32), axis=0)
            result[lax.div(block, half_ring), lax.rem(block, half_ring)] = summed.astype(BF16)

    def from_owners(k, buf):
        both = buf.at[:, slot]
        for side, o in ((0, 1), (1, -1)):
            one = buf.at[side, slot]
            send(one, one, yag_ss.at[k], yag_rs.at[k, 2 + side], mlp=next_to(2 * o))
            send(both, both, yag_ss.at[k], yag_rs.at[k, side], mlp=next_to(o))

    def from_owners_end(k, buf):
        for side, o in ((0, -1), (1, 1)):
            arrived(buf.at[:, lax.rem(next_to(o), half_ring)], yag_rs.at[k, side])
            arrived(buf.at[side, lax.rem(next_to(2 * o), half_ring)], yag_rs.at[k, 2 + side])

    def rows_of(buf, h, blocks, lanes):
        return jnp.concatenate([buf[h, block_of(o), :, lanes] for o in blocks], axis=0)

    def to_owners(k, blocks, terms, part, sent, got):
        for i, o in enumerate(blocks):
            block = block_of(o)
            part[block] = terms[i * TB : (i + 1) * TB]
            sent[block] = terms[i * TB : (i + 1) * TB].astype(BF16)
            for side in range(2):
                owner = lax.rem(block + side * half_ring, NY)

                @pl.when(owner != y)
                def _():
                    place_there = got.at[side, lax.rem(owner - y + NY - 1, NY)]
                    send(sent.at[block], place_there, y_ss.at[k], y_rs.at[k], mlp=owner)

    def output_terms(blocks):
        units = slice(0, FH)
        term = dot(rows_of(hid, 0, blocks, units), wdn[0:FH, :], 1, 0)
        term = term + dot(rows_of(hid, 1, blocks, units), wdn[FH:, :], 1, 0)
        to_owners(0, blocks, term, part0, ys0, yr0)

    def gradient_terms(blocks):
        units, beside = slice(0, FH), slice(FH, FH + EXTRA)
        term = dot(rows_of(gp, 0, blocks, units), wup[:, 0:FH], 1, 1)
        term = term + dot(rows_of(gp, 1, blocks, units), wup[:, FH:], 1, 1)
        side = rows_of(gp, 0, blocks, beside).astype(F32) + rows_of(gp, 1, blocks, beside).astype(F32)
        first, second = unpack(side)
        tokens = [pl.ds(pl.multiple_of(block_of(o) * TB, TB), TB) for o in blocks]
        normal = jnp.concatenate([normed[rows, :] for rows in tokens], axis=0)
        scale = jnp.concatenate([inv_col[rows, 0:1] for rows in tokens], axis=0)
        corrected = scale * (
            term * gain_v[...].reshape(1, DS) - first * (1.0 / D) - normal * (second * (1.0 / D))
        )
        to_owners(1, blocks, corrected, part1, ys1, yr1)
        return jnp.sum((term * normal).reshape(len(blocks) * TB // 8, 8, DS), axis=0)

    my_blocks = pl.ds(pl.multiple_of(c * (NZ // 2), NZ // 2), NZ // 2)
    its_blocks = pl.ds(pl.multiple_of((1 - c) * (NZ // 2), NZ // 2), NZ // 2)

    def share(k, buf, dst):
        def one(o, carry):
            peer = lax.rem(x + o, NX)
            h, lanes = quarter(peer)
            send(buf.at[h, my_blocks, :, lanes], dst.at[o, my_blocks], q_ss.at[k], q_rs.at[k], dp=peer)
            return carry
        lax.fori_loop(1, NX, one, 0)
        h, lanes = quarter(x)
        dst[0] = buf[h, :, :, lanes]

    def join(k, dst):
        halves = dst.at[pl.ds(1, NX - 1), my_blocks]
        arrived(halves, q_rs.at[k])
        send(halves, halves, join_ss.at[k], join_rs.at[k], width=sibling)

    arrived(hid.at[1 - c, pl.ds(0, 5)], rel_rs.at[0])
    output_terms(near)
    gather_far(over_z, units, ag_rs.at[0], 4)
    for o in far:
        block = hid.at[c, block_of(o)]
        send(block, block, rel_ss.at[0], rel_rs.at[2], width=sibling)
    arrived(gp.at[1 - c, pl.ds(0, 5)], rel_rs.at[1])
    gg_sum[...] = gradient_terms(near)
    arrived(hid.at[1 - c, pl.ds(0, 3)], rel_rs.at[2])
    output_terms(far)
    share(0, hid, hx)
    gather_far(over_z, grads, ag_rs.at[1], 4)
    gather_far(over_z, gp.at[1 - c], far_rs, 0)
    share(1, gp, gpx)
    gains = gg_sum[...] + gradient_terms(far)
    gains = jnp.sum(gains, axis=0, keepdims=True)
    rows = [gains[:, j * 128 : (j + 1) * 128] for j in range(DS // 128)]
    gg_s[...] = jnp.concatenate(rows + [jnp.zeros((8 - len(rows), 128), F32)], axis=0)

    def gain_x(o, carry):
        send(gg_s, ggx_r.at[o - 1], ggx_ss, ggx_rs, dp=lax.rem(x + o, NX))
        return carry
    lax.fori_loop(1, NX, gain_x, 0)
    join(0, hx)

    own_sums(0, part0, yr0, outv)
    from_owners(0, outv)

    arrived(ggx_r, ggx_rs)
    ggy_s[...] = gg_s[...] + jnp.sum(ggx_r[...], axis=0)

    def gain_y(o, carry):
        send(ggy_s, ggy_r.at[o - 1], ggy_ss, ggy_rs, mlp=lax.rem(y + o, NY))
        return carry
    lax.fori_loop(1, NY, gain_y, 0)

    join(1, gpx)

    end_x(0, cotx)
    arrived(hx.at[pl.ds(1, NX - 1), its_blocks], join_rs.at[0])
    gdn[...] = dot(hx[...].reshape(NX * T, FQ), cotx[...].reshape(NX * T, DS), 0, 0)
    own_sums(1, part1, yr1, gtv)
    from_owners(1, gtv)
    end_x(1, scx)
    arrived(gpx.at[pl.ds(1, NX - 1), its_blocks], join_rs.at[1])
    product = dot(scx[...].reshape(NX * T, DS), gpx[...].reshape(NX * T, FQ), 0, 0)
    pieces = FQ // 128
    for j in range(pieces):
        gup[pl.ds(j, DS, stride=pieces), :] = product[:, j * 128 : (j + 1) * 128]
    for k in range(2):
        arrived(sib_s.at[k], sib_ss.at[k])
        arrived(zs.at[k, pl.ds(0, NZ - 1)], z_ss.at[k])
    arrived(stat_r, stat_ss)
    arrived(hid.at[0, pl.ds(0, NZ - 1)], ag_ss.at[0])
    arrived(hid.at[0], rel_ss.at[0])
    arrived(gp.at[:, pl.ds(0, 5)], ag_ss.at[1])
    arrived(gp.at[0, pl.ds(0, 5)], rel_ss.at[1])
    for k, buf in enumerate((cotx, scx)):
        arrived(buf.at[pl.ds(0, NX - 1)], x_ss.at[k])
    for k, buf in enumerate((hx, gpx)):
        arrived(buf.at[pl.ds(1, NX - 1), my_blocks], q_ss.at[k])
        arrived(buf.at[pl.ds(1, NX - 1), my_blocks], join_ss.at[k])
    arrived(yr0, y_ss.at[0])
    arrived(yr1, y_ss.at[1])
    arrived(outv.at[:, pl.ds(0, 3)], yag_ss.at[0])
    arrived(ggx_r, ggx_ss)

    from_owners_end(0, outv)
    out[...] = outv[...].reshape(T, DS)
    from_owners_end(1, gtv)
    gt[...] = gtv[...].reshape(T, DS)
    arrived(ggy_r, ggy_rs)
    gains = ggy_s[...] + jnp.sum(ggy_r[...], axis=0)
    gg[...] = jnp.concatenate([gains[j : j + 1] for j in range(DS // 128)], axis=1).reshape(DS)
    arrived(gtv.at[:, pl.ds(0, 3)], yag_ss.at[1])
    arrived(ggy_r, ggy_ss)


def place(*refs):
    made, given, sems = refs[0:5], refs[5:10], refs[10]
    copies = [pltpu.make_async_copy(src, dst, sems.at[k]) for k, (src, dst) in enumerate(zip(made, given))]
    for copy in copies:
        copy.start()
    for copy in copies:
        copy.wait()


def solution(mesh):
    NX, NZ, NY = mesh.shape["dp"], mesh.shape["width"] // 2, mesh.shape["mlp"]

    def shards(tokens, gain, up_weight, down_weight, cotangent):
        T, DS = tokens.shape
        FS = up_weight.shape[1]
        FH, FQ = FS // 2, FS // NX
        vmem, dma = pltpu.VMEM, pltpu.SemaphoreType.DMA
        results = (
            jax.ShapeDtypeStruct((T, DS), BF16),
            jax.ShapeDtypeStruct((T, DS), BF16),
            jax.ShapeDtypeStruct((DS,), F32),
            jax.ShapeDtypeStruct((DS * FQ // 128, 128), F32),
            jax.ShapeDtypeStruct((FQ, DS), F32),
        )
        call = pl.pallas_call(
            functools.partial(kernel, (NX, NZ, NY, DS * 2 * NZ)),
            out_shape=results,
            in_specs=[pl.BlockSpec(memory_space=pltpu.HBM)] * 5,
            out_specs=[pl.BlockSpec(memory_space=pltpu.VMEM)] * 5,
            scratch_shapes=[
                vmem((T, DS), BF16), vmem((DS,), F32), vmem((DS, FS), BF16), vmem((FS, DS), BF16),
                vmem((NX, T, DS), BF16), vmem((NX, T, DS), BF16), vmem((T, DS), F32), vmem((T, EXTRA), F32),
                vmem((2, 8, 128), F32), vmem((2 * NZ - 1, 8, 128), F32),
                vmem((2, T, FH), BF16), vmem((2, T, FH), BF16), vmem((2, NZ, TB, FH), F32),
                vmem((2, NZ, TB, FH), BF16), vmem((2, 6, TB, FH), BF16),
                vmem((2, 2, TB, FH // 2), BF16), vmem((2, 2, TB, FH), BF16),
                vmem((T + TB, DS), BF16), vmem((T, EXTRA), F32),
                vmem((2, NZ, TB, FH), BF16), vmem((2, NZ, TB, FH + EXTRA), BF16),
                vmem((NX, NZ, TB, FQ), BF16), vmem((NX, NZ, TB, FQ), BF16),
                *(
                    shape
                    for _ in range(2)
                    for shape in (
                        vmem((NY, TB, DS), BF16), vmem((2, NY - 1, TB, DS), BF16), vmem((NY, TB, DS), F32),
                    )
                ),
                vmem((2, NY // 2, TB, DS), BF16), vmem((2, NY // 2, TB, DS), BF16),
                vmem((8, DS), F32), vmem((8, 128), F32), vmem((NX - 1, 8, 128), F32),
                vmem((8, 128), F32), vmem((NY - 1, 8, 128), F32),
                dma((7,)), dma((2,)), dma((2,)), dma, dma, dma((2,)), dma((2, 8)),
                dma((2,)), dma((2, 8)), dma((4,)), dma((2,)), dma((3,)),
                dma((2,)), dma((2, 4)), dma((2,)), dma((2,)), dma((2,)), dma((2,)),
                dma((2,)), dma((2,)), dma((2,)), dma((2, 4)), dma, dma, dma, dma,
                pltpu.SemaphoreType.REGULAR, pltpu.SemaphoreType.REGULAR,
            ],
            compiler_params=pltpu.CompilerParams(
                collective_id=0, has_side_effects=True, vmem_limit_bytes=48 * 1024 * 1024
            ),
            cost_estimate=pl.CostEstimate(
                flops=12 * T * DS * FS, bytes_accessed=4 * DS * FS + 8 * DS * FQ, transcendentals=2 * TB * FH
            ),
        )
        put = pl.pallas_call(
            place,
            out_shape=results,
            in_specs=[pl.BlockSpec(memory_space=pltpu.VMEM)] * 5,
            out_specs=[pl.BlockSpec(memory_space=pltpu.HBM)] * 5,
            scratch_shapes=[dma((5,))],
            compiler_params=pltpu.CompilerParams(vmem_limit_bytes=4 * 1024 * 1024),
        )
        output, grad_tokens, grad_gain, grad_up, grad_down = put(
            *call(*(pltpu.with_memory_space_constraint(a, pltpu.HBM) for a in (tokens, gain, up_weight, down_weight, cotangent)))
        )
        return output, grad_tokens, grad_gain, grad_up.reshape(DS, 1, FQ), grad_down[None, :, :]

    placed = (P("dp", "width"), P("width"), P("width", "mlp"), P("mlp", "width"), P("dp", "width"))
    return jax.shard_map(
        shards,
        mesh=mesh,
        in_specs=placed,
        out_specs=(
            P("dp", "width"),
            P("dp", "width"),
            P("width"),
            P("width", "mlp", "dp"),
            P("mlp", "dp", "width"),
        ),
        check_vma=False,
    )
```

```python
import functools

import jax
import jax.numpy as jnp
from jax import lax
from jax.experimental import pallas as pl
from jax.experimental.pallas import tpu as pltpu
from jax.sharding import PartitionSpec as P

MESH = pl.DeviceIdType.MESH
F32, BF16 = jnp.float32, jnp.bfloat16
TB = 16
EXTRA = 128

inv_root_two = 0.7071067811865476
inv_root_two_pi = 0.3989422804014327


def dot(left, right, left_dim, right_dim):
    return lax.dot_general(
        left, right, (((left_dim,), (right_dim,)), ((), ())), preferred_element_type=F32
    )


def pack(first, second):
    lane = lax.broadcasted_iota(jnp.int32, (first.shape[0], EXTRA), 1)
    high_one, high_two = first.astype(BF16).astype(F32), second.astype(BF16).astype(F32)
    held = jnp.where(lane == 0, high_one, 0.0)
    held = jnp.where(lane == 1, high_two, held)
    held = jnp.where(lane == 2, first - high_one, held)
    held = jnp.where(lane == 3, second - high_two, held)
    return held.astype(BF16)


def unpack(held):
    return held[:, 0:1] + held[:, 2:3], held[:, 1:2] + held[:, 3:4]


def send(src, dst, ss, rs, **where):
    pltpu.make_async_remote_copy(
        src_ref=src, dst_ref=dst, send_sem=ss, recv_sem=rs, device_id=where, device_id_type=MESH
    ).start()


def arrived(ref, sem):
    pltpu.make_async_copy(ref, ref, sem).wait()


def ring(axis, me, device=lambda position: position):
    def at(o):
        return lax.rem(me + o % 8, 8)
    return at, lambda o: {axis: device(at(o))}


def lanes_of(block, side):
    cut = block.shape[-1] // 256 * 128
    return block.at[:, pl.ds(0, cut) if side == 0 else pl.ds(cut, block.shape[-1] - cut)]


def scatter(to_whom, terms, got, halves, ss, rs):
    at, to = to_whom
    for side, o in ((0, 1), (1, -1)):
        send(terms.at[at(3 * o)], got.at[4 + side], ss, rs.at[4 + side], **to(o))
    for side, o in ((0, 2), (1, -2)):
        send(lanes_of(terms.at[at(4)], side), halves[side], ss, rs.at[6 + side], **to(o))
    for side, o in ((0, 1), (1, -1)):
        send(terms.at[at(o)], got.at[side], ss, rs.at[side], **to(o))


def scatter_pass(to_whom, own, got, halves, sums, ss, rs):
    at, to = to_whom
    for side, o in ((0, 2), (1, -2)):
        arrived(got.at[4 + side], rs.at[4 + side])
        arrived(halves[side], rs.at[6 + side])
        term = own[at(o)] + got[4 + side].astype(F32)
        half = halves[side][...].astype(F32)
        cut = term.shape[-1] // 256 * 128
        low, high = term[:, 0:cut], term[:, cut:]
        sums[side, :, 0:cut] = (low + half if side == 0 else low).astype(BF16)
        sums[side, :, cut:] = (high if side == 0 else high + half).astype(BF16)
        send(sums.at[side], got.at[2 + side], ss, rs.at[2 + side], **to(o))


def scatter_sum(to_whom, own, got, rs):
    at, _ = to_whom
    for slot in range(4):
        arrived(got.at[slot], rs.at[slot])
    return own[at(0)] + jnp.sum(got[0:4].astype(F32), axis=0)


def gather(to_whom, buf, ss, rs):
    at, to = to_whom
    block = buf.at[at(0)]
    for o, slot in ((2, 2), (-2, 3), (1, 0), (-1, 1)):
        send(block, block, ss, rs.at[slot], **to(o))


def gather_pass(here, buf, ss, sems, use):
    at, _ = here
    for side, o in ((0, 1), (1, -1)):
        block = buf.at[at(-2 * o)]
        arrived(block, sems[0][1].at[2 + side])
        half = lanes_of(block, side)
        for (_, to), there, first in sems:
            send(block, block, ss, there.at[first + side], **to(o))
            send(half, half, ss, there.at[first + 2 + side], **to(2 * o))
        use(block)


def gather_near(here, buf, rs, use):
    at, _ = here
    for side, o in ((0, -1), (1, 1)):
        arrived(buf.at[at(o)], rs.at[side])
        use(buf.at[at(o)])


def gather_far(here, buf, sems, first):
    at, _ = here
    for side, o in ((0, -3), (1, 3)):
        arrived(buf.at[at(o)], sems.at[first + side])
        arrived(lanes_of(buf.at[at(4)], side), sems.at[first + 2 + side])


def kernel(
    sizes, tok_h, gain_h, wup_h, wdn_h, cot_h, out, gt, gg, gup, gdn,
    tok, gain_v, wup, wdn, cotx, scx, normed, inv_col,
    stat_s, stat_r,
    sib_s, sib_r, own, zs, zr, zh, zc, leaning, away_col,
    hid, gp, hx, gpx,
    ys0, yr0, part0, ys1, yr1, part1,
    outv, gtv,
    gg_sum, gg_s, ggx_r, ggy_s, ggy_r,
    ld, sib_ss, sib_rs, stat_ss, stat_rs, z_ss, z_rs, ag_ss, ag_rs, far_rs, rel_ss, rel_rs,
    x_ss, x_rs, q_ss, q_rs, join_ss, join_rs, y_ss, y_rs, yag_ss, yag_rs, ggx_ss, ggx_rs, ggy_ss, ggy_rs,
    known, all_known,
):
    NX, NZ, NY, D = sizes
    T, DS = tok.shape
    TY = T // NY
    FS = wup.shape[1]
    FH, FQ = FS // 2, FS // NX
    NW = 2 * NZ
    x, w, y = lax.axis_index("dp"), lax.axis_index("width"), lax.axis_index("mlp")
    z = lax.div(w, 2)
    c = w - 2 * z
    sibling = 2 * z + 1 - c

    over_z = ring("width", z, lambda position: 2 * position + c)
    across_z = ring("width", z, lambda position: 2 * position + 1 - c)

    def quarter(q):
        first = q * FQ
        h = lax.div(first, FH)
        return h, pl.ds(pl.multiple_of(first - h * FH, FQ), FQ)

    mine = pl.ds(pl.multiple_of(c * FH, FH), FH)
    other = pl.ds(pl.multiple_of(FH - c * FH, FH), FH)

    barrier = pltpu.get_barrier_semaphore()
    over_y = ring("mlp", y)

    def signal(semaphore, **where):
        pl.semaphore_signal(semaphore, inc=1, device_id=where, device_id_type=MESH)

    for o in (2, -2, 1, -1):
        signal(barrier, **over_z[1](o))
        signal(barrier, **over_y[1](o))
    for o in range(1, NX):
        signal(barrier, dp=lax.rem(x + o, NX))
    signal(barrier, width=sibling)

    loads = [
        pltpu.make_async_copy(tok_h, tok, ld.at[0]),
        pltpu.make_async_copy(gain_h, gain_v, ld.at[1]),
        pltpu.make_async_copy(wup_h.at[:, other], wup.at[:, other], ld.at[2]),
        pltpu.make_async_copy(cot_h, cotx.at[0], ld.at[3]),
        pltpu.make_async_copy(wdn_h.at[other], wdn.at[other], ld.at[4]),
        pltpu.make_async_copy(wup_h.at[:, mine], wup.at[:, mine], ld.at[5]),
        pltpu.make_async_copy(wdn_h.at[mine], wdn.at[mine], ld.at[6]),
    ]
    for load in loads:
        load.start()

    loads[0].wait()
    loads[1].wait()
    values = tok[...].astype(F32)
    total = jnp.sum(values, axis=1, keepdims=True)
    shifted = values - total * (1.0 / DS)
    g_all = gain_v[...].reshape(1, DS)
    leaning[0:T] = (shifted * g_all).astype(BF16)
    row = lax.broadcasted_iota(jnp.int32, (TB, DS), 0)
    g_one = g_all.astype(BF16).astype(F32)
    g_two = (g_all - g_one).astype(BF16).astype(F32)
    g_rows = jnp.where(row == 0, g_one, jnp.where(row == 1, g_two, jnp.where(row == 2, g_all - g_one - g_two, 0.0)))
    leaning[T:] = g_rows.astype(BF16)
    loads[2].wait()
    its_half = dot(leaning[...], wup[:, other], 1, 0)
    sib_s[0] = its_half[0:T].astype(BF16)

    loads[3].wait()
    loads[4].wait()
    sib_s[1] = dot(cotx[0], wdn[other, :], 1, 1).astype(BF16)
    pl.semaphore_wait(barrier, 8 + NX)
    for k in range(2):
        send(sib_s.at[k], sib_r.at[k], sib_ss.at[k], sib_rs.at[k], width=sibling)
    signal(known, width=sibling)
    for o in (2, -2):
        signal(known, **over_z[1](o))
        signal(known, **over_y[1](o))

    loads[5].wait()
    my_half = dot(leaning[...], wup[:, mine], 1, 0)
    own[0] = my_half[0:T].reshape(NZ, TB, FH)
    loads[6].wait()
    own[1] = dot(cotx[0], wdn[mine, :], 1, 1).reshape(NZ, TB, FH)

    shifted = tok[...].astype(F32) - total * (1.0 / DS)
    spread = jnp.sum(shifted * shifted, axis=1, keepdims=True)
    total_row = jnp.transpose(jnp.broadcast_to(total, (T, EXTRA)))[0:1]
    spread_row = jnp.transpose(jnp.broadcast_to(spread, (T, EXTRA)))[0:1]
    for h, half in ((c, my_half), (1 - c, its_half)):
        lean = jnp.sum(half[T:], axis=0, keepdims=True)
        stat_s[h, 0:1, 0:T] = total_row
        stat_s[h, 1:2, 0:T] = spread_row
        for j in range(FH // 128):
            stat_s[h, 2 + j : 3 + j, :] = lean[:, j * 128 : (j + 1) * 128]

    def merge(k):
        arrived(sib_r.at[k], sib_rs.at[k])
        both = own[k] + sib_r[k].astype(F32).reshape(NZ, TB, FH)
        own[k] = both
        zs[k] = both.astype(BF16)
        scatter(over_z, zs.at[k], zr.at[k], [zh.at[k, 0], zh.at[k, 1]], z_ss.at[k], z_rs.at[k])

    def merge_pass(k):
        scatter_pass(
            over_z, own.at[k], zr.at[k], [zh.at[k, 0], zh.at[k, 1]], zc.at[k], z_ss.at[k], z_rs.at[k]
        )

    def tell(k, carry):
        peer = lax.rem(w + k, NW)
        send(stat_s.at[lax.rem(peer, 2)], stat_r.at[k - 1], stat_ss, stat_rs, width=peer)
        return carry

    merge(0)
    merge(1)
    pl.semaphore_wait(known, 5)
    signal(all_known, width=sibling)

    right, left = lax.rem(x + 1, NX), lax.rem(x + NX - 1, NX)
    first_rows, last_rows = pl.ds(0, T // 2), pl.ds(T // 2, T // 2)

    def spread_x(k, buf):
        send(buf.at[0], buf.at[1], x_ss.at[k], x_rs.at[k, 0], dp=right)
        send(buf.at[0], buf.at[NX - 1], x_ss.at[k], x_rs.at[k, 1], dp=left)

    def pass_x(k, buf):
        arrived(buf.at[1], x_rs.at[k, 0])
        send(buf.at[1, first_rows], buf.at[2, first_rows], x_ss.at[k], x_rs.at[k, 2], dp=right)
        arrived(buf.at[NX - 1], x_rs.at[k, 1])
        send(buf.at[NX - 1, last_rows], buf.at[2, last_rows], x_ss.at[k], x_rs.at[k, 3], dp=left)

    def end_x(k, buf):
        arrived(buf.at[2, first_rows], x_rs.at[k, 2])
        arrived(buf.at[2, last_rows], x_rs.at[k, 3])

    spread_x(0, cotx)
    pl.semaphore_wait(all_known, 1)
    lax.fori_loop(1, NW, tell, 0)
    merge_pass(0)
    merge_pass(1)

    arrived(stat_r, stat_rs)
    its = stat_r[...]
    my_stat = stat_s[c]
    sums, spreads = its[:, 0, :], its[:, 1, :]
    mean = (jnp.sum(sums, axis=0, keepdims=True) + my_stat[0:1]) * (1.0 / D)
    away, my_away = sums * (1.0 / DS) - mean, my_stat[0:1] * (1.0 / DS) - mean
    variance = (
        jnp.sum(spreads + DS * away * away, axis=0, keepdims=True) + my_stat[1:2] + DS * my_away * my_away
    ) * (1.0 / D)
    inv_std = lax.rsqrt(variance + 1e-06)
    mean_col = jnp.transpose(jnp.broadcast_to(mean[:, 0:T], (EXTRA, T)))
    std_col = jnp.transpose(jnp.broadcast_to(inv_std[:, 0:T], (EXTRA, T)))
    inv_col[...] = std_col
    aways = jnp.concatenate([away[:, 0:T], my_away[:, 0:T], jnp.zeros((EXTRA - NW, T), F32)], axis=0)
    away_col[...] = jnp.transpose(aways)
    token_rows = pl.ds(pl.multiple_of(z * TB, TB), TB)
    my_aways = away_col[token_rows, :]
    leans, shift = [], []
    for j in range(FH // 128):
        piece = [its[s, 2 + j : 3 + j, :] for s in range(NW - 1)] + [my_stat[2 + j : 3 + j, :]]
        leans.append(functools.reduce(jnp.add, piece))
        shift.append(functools.reduce(jnp.add, [my_aways[:, s : s + 1] * piece[s] for s in range(NW)]))
    lean_row = jnp.concatenate(leans, axis=1)
    shift = jnp.concatenate(shift, axis=1)

    def hand_over(k):
        return lambda block: send(block, block, rel_ss.at[k], rel_rs.at[k], width=sibling)

    pre_act = (scatter_sum(over_z, own.at[0], zr.at[0], z_rs.at[0]) + shift) * inv_col[token_rows, 0:1]
    below = 0.5 * (1.0 + lax.erf(pre_act * inv_root_two))
    hid[c, z] = (pre_act * below).astype(BF16)
    units, grads = hid.at[c], gp.at[c]
    gather(over_z, units, ag_ss.at[0], ag_rs.at[0])
    hand_over(0)(hid.at[c, z])
    slope = below + pre_act * jnp.exp(-0.5 * pre_act * pre_act) * inv_root_two_pi
    grad_hidden = scatter_sum(over_z, own.at[1], zr.at[1], z_rs.at[1])
    grad_pre = (grad_hidden * slope).astype(BF16)
    wide = grad_pre.astype(F32)
    gp[c, z, :, 0:FH] = grad_pre
    gp[c, z, :, FH:] = pack(
        jnp.sum(wide * lean_row, axis=1, keepdims=True), jnp.sum(wide * pre_act, axis=1, keepdims=True)
    )
    gather(over_z, grads, ag_ss.at[1], ag_rs.at[1])
    hand_over(1)(gp.at[c, z])

    for j in range(DS // 128):
        cols = slice(j * 128, (j + 1) * 128)
        normal = (tok[:, cols].astype(F32) - mean_col) * std_col
        normed[:, cols] = normal
        scx[0, :, cols] = (normal * g_all[:, cols]).astype(BF16)
    spread_x(1, scx)

    gather_pass(over_z, units, ag_ss.at[0], [(over_z, ag_rs.at[0], 4)], hand_over(0))
    gather_near(over_z, units, ag_rs.at[0], hand_over(0))
    gather_pass(
        over_z, grads, ag_ss.at[1], [(over_z, ag_rs.at[1], 4), (across_z, far_rs, 0)], hand_over(1)
    )
    gather_near(over_z, grads, ag_rs.at[1], hand_over(1))
    pass_x(0, cotx)
    pass_x(1, scx)

    block_of, _ = over_z
    near, far = (0, 1, -1, 2, -2), (3, -3, 4)

    half_ring = NY // 2
    slot = lax.rem(y, half_ring)

    def next_to(o):
        return lax.rem(y + o % NY, NY)

    def own_sums(k, part, got, result):
        arrived(got, y_rs.at[k])
        for side in range(2):
            block = lax.rem(y + side * half_ring, NY)
            summed = part[block] + jnp.sum(got[side].astype(F32), axis=0)
            result[lax.div(block, half_ring), lax.rem(block, half_ring)] = summed.astype(BF16)

    def from_owners(k, buf):
        both = buf.at[:, slot]
        for side, o in ((0, 1), (1, -1)):
            one = buf.at[side, slot]
            send(one, one, yag_ss.at[k], yag_rs.at[k, 2 + side], mlp=next_to(2 * o))
            send(both, both, yag_ss.at[k], yag_rs.at[k, side], mlp=next_to(o))

    def from_owners_end(k, buf):
        for side, o in ((0, -1), (1, 1)):
            arrived(buf.at[:, lax.rem(next_to(o), half_ring)], yag_rs.at[k, side])
            arrived(buf.at[side, lax.rem(next_to(2 * o), half_ring)], yag_rs.at[k, 2 + side])

    def rows_of(buf, h, blocks, lanes):
        return jnp.concatenate([buf[h, block_of(o), :, lanes] for o in blocks], axis=0)

    def to_owners(k, blocks, terms, part, sent, got):
        for i, o in enumerate(blocks):
            block = block_of(o)
            part[block] = terms[i * TB : (i + 1) * TB]
            sent[block] = terms[i * TB : (i + 1) * TB].astype(BF16)
            for side in range(2):
                owner = lax.rem(block + side * half_ring, NY)

                @pl.when(owner != y)
                def _():
                    place_there = got.at[side, lax.rem(owner - y + NY - 1, NY)]
                    send(sent.at[block], place_there, y_ss.at[k], y_rs.at[k], mlp=owner)

    def output_terms(blocks):
        units = slice(0, FH)
        term = dot(rows_of(hid, 0, blocks, units), wdn[0:FH, :], 1, 0)
        term = term + dot(rows_of(hid, 1, blocks, units), wdn[FH:, :], 1, 0)
        to_owners(0, blocks, term, part0, ys0, yr0)

    def gradient_terms(blocks):
        units, beside = slice(0, FH), slice(FH, FH + EXTRA)
        term = dot(rows_of(gp, 0, blocks, units), wup[:, 0:FH], 1, 1)
        term = term + dot(rows_of(gp, 1, blocks, units), wup[:, FH:], 1, 1)
        side = rows_of(gp, 0, blocks, beside).astype(F32) + rows_of(gp, 1, blocks, beside).astype(F32)
        first, second = unpack(side)
        tokens = [pl.ds(pl.multiple_of(block_of(o) * TB, TB), TB) for o in blocks]
        normal = jnp.concatenate([normed[rows, :] for rows in tokens], axis=0)
        scale = jnp.concatenate([inv_col[rows, 0:1] for rows in tokens], axis=0)
        corrected = scale * (
            term * gain_v[...].reshape(1, DS) - first * (1.0 / D) - normal * (second * (1.0 / D))
        )
        to_owners(1, blocks, corrected, part1, ys1, yr1)
        return jnp.sum((term * normal).reshape(len(blocks) * TB // 8, 8, DS), axis=0)

    my_blocks = pl.ds(pl.multiple_of(c * (NZ // 2), NZ // 2), NZ // 2)
    its_blocks = pl.ds(pl.multiple_of((1 - c) * (NZ // 2), NZ // 2), NZ // 2)

    def share(k, buf, dst):
        def one(o, carry):
            peer = lax.rem(x + o, NX)
            h, lanes = quarter(peer)
            send(buf.at[h, my_blocks, :, lanes], dst.at[o, my_blocks], q_ss.at[k], q_rs.at[k], dp=peer)
            return carry
        lax.fori_loop(1, NX, one, 0)
        h, lanes = quarter(x)
        dst[0] = buf[h, :, :, lanes]

    def join(k, dst):
        halves = dst.at[pl.ds(1, NX - 1), my_blocks]
        arrived(halves, q_rs.at[k])
        send(halves, halves, join_ss.at[k], join_rs.at[k], width=sibling)

    arrived(hid.at[1 - c, pl.ds(0, 5)], rel_rs.at[0])
    output_terms(near)
    gather_far(over_z, units, ag_rs.at[0], 4)
    for o in far:
        block = hid.at[c, block_of(o)]
        send(block, block, rel_ss.at[0], rel_rs.at[2], width=sibling)
    arrived(gp.at[1 - c, pl.ds(0, 5)], rel_rs.at[1])
    gg_sum[...] = gradient_terms(near)
    arrived(hid.at[1 - c, pl.ds(0, 3)], rel_rs.at[2])
    output_terms(far)
    share(0, hid, hx)
    gather_far(over_z, grads, ag_rs.at[1], 4)
    gather_far(over_z, gp.at[1 - c], far_rs, 0)
    share(1, gp, gpx)
    gains = gg_sum[...] + gradient_terms(far)
    gains = jnp.sum(gains, axis=0, keepdims=True)
    rows = [gains[:, j * 128 : (j + 1) * 128] for j in range(DS // 128)]
    gg_s[...] = jnp.concatenate(rows + [jnp.zeros((8 - len(rows), 128), F32)], axis=0)

    def gain_x(o, carry):
        send(gg_s, ggx_r.at[o - 1], ggx_ss, ggx_rs, dp=lax.rem(x + o, NX))
        return carry
    lax.fori_loop(1, NX, gain_x, 0)
    join(0, hx)

    own_sums(0, part0, yr0, outv)
    from_owners(0, outv)

    arrived(ggx_r, ggx_rs)
    ggy_s[...] = gg_s[...] + jnp.sum(ggx_r[...], axis=0)

    def gain_y(o, carry):
        send(ggy_s, ggy_r.at[o - 1], ggy_ss, ggy_rs, mlp=lax.rem(y + o, NY))
        return carry
    lax.fori_loop(1, NY, gain_y, 0)

    join(1, gpx)

    end_x(0, cotx)
    arrived(hx.at[pl.ds(1, NX - 1), its_blocks], join_rs.at[0])
    gdn[...] = dot(hx[...].reshape(NX * T, FQ), cotx[...].reshape(NX * T, DS), 0, 0)
    own_sums(1, part1, yr1, gtv)
    from_owners(1, gtv)
    end_x(1, scx)
    arrived(gpx.at[pl.ds(1, NX - 1), its_blocks], join_rs.at[1])
    product = dot(scx[...].reshape(NX * T, DS), gpx[...].reshape(NX * T, FQ), 0, 0)
    pieces = FQ // 128
    for j in range(pieces):
        gup[pl.ds(j, DS, stride=pieces), :] = product[:, j * 128 : (j + 1) * 128]
    for k in range(2):
        arrived(sib_s.at[k], sib_ss.at[k])
        arrived(zs.at[k, pl.ds(0, NZ - 1)], z_ss.at[k])
    arrived(stat_r, stat_ss)
    arrived(hid.at[0, pl.ds(0, NZ - 1)], ag_ss.at[0])
    arrived(hid.at[0], rel_ss.at[0])
    arrived(gp.at[:, pl.ds(0, 5)], ag_ss.at[1])
    arrived(gp.at[0, pl.ds(0, 5)], rel_ss.at[1])
    for k, buf in enumerate((cotx, scx)):
        arrived(buf.at[pl.ds(0, NX - 1)], x_ss.at[k])
    for k, buf in enumerate((hx, gpx)):
        arrived(buf.at[pl.ds(1, NX - 1), my_blocks], q_ss.at[k])
        arrived(buf.at[pl.ds(1, NX - 1), my_blocks], join_ss.at[k])
    arrived(yr0, y_ss.at[0])
    arrived(yr1, y_ss.at[1])
    arrived(outv.at[:, pl.ds(0, 3)], yag_ss.at[0])
    arrived(ggx_r, ggx_ss)

    from_owners_end(0, outv)
    out[...] = outv[...].reshape(T, DS)
    from_owners_end(1, gtv)
    gt[...] = gtv[...].reshape(T, DS)
    arrived(ggy_r, ggy_rs)
    gains = ggy_s[...] + jnp.sum(ggy_r[...], axis=0)
    gg[...] = jnp.concatenate([gains[j : j + 1] for j in range(DS // 128)], axis=1).reshape(DS)
    arrived(gtv.at[:, pl.ds(0, 3)], yag_ss.at[1])
    arrived(ggy_r, ggy_ss)


def place(*refs):
    made, given, sems = refs[0:5], refs[5:10], refs[10]
    copies = [pltpu.make_async_copy(src, dst, sems.at[k]) for k, (src, dst) in enumerate(zip(made, given))]
    for copy in copies:
        copy.start()
    for copy in copies:
        copy.wait()


def solution(mesh):
    NX, NZ, NY = mesh.shape["dp"], mesh.shape["width"] // 2, mesh.shape["mlp"]

    def shards(tokens, gain, up_weight, down_weight, cotangent):
        T, DS = tokens.shape
        FS = up_weight.shape[1]
        FH, FQ = FS // 2, FS // NX
        vmem, dma = pltpu.VMEM, pltpu.SemaphoreType.DMA
        results = (
            jax.ShapeDtypeStruct((T, DS), BF16),
            jax.ShapeDtypeStruct((T, DS), BF16),
            jax.ShapeDtypeStruct((DS,), F32),
            jax.ShapeDtypeStruct((DS * FQ // 128, 128), F32),
            jax.ShapeDtypeStruct((FQ, DS), F32),
        )
        call = pl.pallas_call(
            functools.partial(kernel, (NX, NZ, NY, DS * 2 * NZ)),
            out_shape=results,
            in_specs=[pl.BlockSpec(memory_space=pltpu.HBM)] * 5,
            out_specs=[pl.BlockSpec(memory_space=pltpu.VMEM)] * 5,
            scratch_shapes=[
                vmem((T, DS), BF16), vmem((DS,), F32), vmem((DS, FS), BF16), vmem((FS, DS), BF16),
                vmem((NX, T, DS), BF16), vmem((NX, T, DS), BF16), vmem((T, DS), F32), vmem((T, EXTRA), F32),
                vmem((2, 8, 128), F32), vmem((2 * NZ - 1, 8, 128), F32),
                vmem((2, T, FH), BF16), vmem((2, T, FH), BF16), vmem((2, NZ, TB, FH), F32),
                vmem((2, NZ, TB, FH), BF16), vmem((2, 6, TB, FH), BF16),
                vmem((2, 2, TB, FH // 2), BF16), vmem((2, 2, TB, FH), BF16),
                vmem((T + TB, DS), BF16), vmem((T, EXTRA), F32),
                vmem((2, NZ, TB, FH), BF16), vmem((2, NZ, TB, FH + EXTRA), BF16),
                vmem((NX, NZ, TB, FQ), BF16), vmem((NX, NZ, TB, FQ), BF16),
                *(
                    shape
                    for _ in range(2)
                    for shape in (
                        vmem((NY, TB, DS), BF16), vmem((2, NY - 1, TB, DS), BF16), vmem((NY, TB, DS), F32),
                    )
                ),
                vmem((2, NY // 2, TB, DS), BF16), vmem((2, NY // 2, TB, DS), BF16),
                vmem((8, DS), F32), vmem((8, 128), F32), vmem((NX - 1, 8, 128), F32),
                vmem((8, 128), F32), vmem((NY - 1, 8, 128), F32),
                dma((7,)), dma((2,)), dma((2,)), dma, dma, dma((2,)), dma((2, 8)),
                dma((2,)), dma((2, 8)), dma((4,)), dma((2,)), dma((3,)),
                dma((2,)), dma((2, 4)), dma((2,)), dma((2,)), dma((2,)), dma((2,)),
                dma((2,)), dma((2,)), dma((2,)), dma((2, 4)), dma, dma, dma, dma,
                pltpu.SemaphoreType.REGULAR, pltpu.SemaphoreType.REGULAR,
            ],
            compiler_params=pltpu.CompilerParams(
                collective_id=0, has_side_effects=True, vmem_limit_bytes=48 * 1024 * 1024
            ),
            cost_estimate=pl.CostEstimate(
                flops=12 * T * DS * FS, bytes_accessed=4 * DS * FS + 8 * DS * FQ, transcendentals=2 * TB * FH
            ),
        )
        put = pl.pallas_call(
            place,
            out_shape=results,
            in_specs=[pl.BlockSpec(memory_space=pltpu.VMEM)] * 5,
            out_specs=[pl.BlockSpec(memory_space=pltpu.HBM)] * 5,
            scratch_shapes=[dma((5,))],
            compiler_params=pltpu.CompilerParams(vmem_limit_bytes=4 * 1024 * 1024),
        )
        output, grad_tokens, grad_gain, grad_up, grad_down = put(
            *call(*(pltpu.with_memory_space_constraint(a, pltpu.HBM) for a in (tokens, gain, up_weight, down_weight, cotangent)))
        )
        return output, grad_tokens, grad_gain, grad_up.reshape(DS, 1, FQ), grad_down[None, :, :]

    placed = (P("dp", "width"), P("width"), P("width", "mlp"), P("mlp", "width"), P("dp", "width"))
    return jax.shard_map(
        shards,
        mesh=mesh,
        in_specs=placed,
        out_specs=(
            P("dp", "width"),
            P("dp", "width"),
            P("width"),
            P("width", "mlp", "dp"),
            P("mlp", "dp", "width"),
        ),
        check_vma=False,
    )
```

```python
import functools

import jax
import jax.numpy as jnp
from jax import lax
from jax.experimental import pallas as pl
from jax.experimental.pallas import tpu as pltpu
from jax.sharding import PartitionSpec as P

MESH = pl.DeviceIdType.MESH
F32, BF16 = jnp.float32, jnp.bfloat16
TB = 16
EXTRA = 128

inv_root_two = 0.7071067811865476
inv_root_two_pi = 0.3989422804014327


def dot(left, right, left_dim, right_dim):
    return lax.dot_general(
        left, right, (((left_dim,), (right_dim,)), ((), ())), preferred_element_type=F32
    )


def pack(first, second):
    lane = lax.broadcasted_iota(jnp.int32, (first.shape[0], EXTRA), 1)
    high_one, high_two = first.astype(BF16).astype(F32), second.astype(BF16).astype(F32)
    held = jnp.where(lane == 0, high_one, 0.0)
    held = jnp.where(lane == 1, high_two, held)
    held = jnp.where(lane == 2, first - high_one, held)
    held = jnp.where(lane == 3, second - high_two, held)
    return held.astype(BF16)


def unpack(held):
    return held[:, 0:1] + held[:, 2:3], held[:, 1:2] + held[:, 3:4]


def send(src, dst, ss, rs, **where):
    pltpu.make_async_remote_copy(
        src_ref=src, dst_ref=dst, send_sem=ss, recv_sem=rs, device_id=where, device_id_type=MESH
    ).start()


def arrived(ref, sem):
    pltpu.make_async_copy(ref, ref, sem).wait()


def ring(axis, me, device=lambda position: position):
    def at(o):
        return lax.rem(me + o % 8, 8)
    return at, lambda o: {axis: device(at(o))}


def lanes_of(block, side):
    cut = block.shape[-1] // 256 * 128
    return block.at[:, pl.ds(0, cut) if side == 0 else pl.ds(cut, block.shape[-1] - cut)]


def scatter(to_whom, terms, got, halves, ss, rs):
    at, to = to_whom
    for side, o in ((0, 1), (1, -1)):
        send(terms.at[at(3 * o)], got.at[4 + side], ss, rs.at[4 + side], **to(o))
    for side, o in ((0, 2), (1, -2)):
        send(lanes_of(terms.at[at(4)], side), halves[side], ss, rs.at[6 + side], **to(o))
    for side, o in ((0, 1), (1, -1)):
        send(terms.at[at(o)], got.at[side], ss, rs.at[side], **to(o))


def scatter_pass(to_whom, own, got, halves, sums, ss, rs):
    at, to = to_whom
    for side, o in ((0, 2), (1, -2)):
        arrived(got.at[4 + side], rs.at[4 + side])
        arrived(halves[side], rs.at[6 + side])
        term = own[at(o)] + got[4 + side].astype(F32)
        half = halves[side][...].astype(F32)
        cut = term.shape[-1] // 256 * 128
        low, high = term[:, 0:cut], term[:, cut:]
        sums[side, :, 0:cut] = (low + half if side == 0 else low).astype(BF16)
        sums[side, :, cut:] = (high if side == 0 else high + half).astype(BF16)
        send(sums.at[side], got.at[2 + side], ss, rs.at[2 + side], **to(o))


def scatter_sum(to_whom, own, got, rs):
    at, _ = to_whom
    for slot in range(4):
        arrived(got.at[slot], rs.at[slot])
    return own[at(0)] + jnp.sum(got[0:4].astype(F32), axis=0)


def gather(to_whom, buf, ss, rs):
    at, to = to_whom
    block = buf.at[at(0)]
    for o, slot in ((2, 2), (-2, 3), (1, 0), (-1, 1)):
        send(block, block, ss, rs.at[slot], **to(o))


def gather_pass(here, buf, ss, sems, use):
    at, _ = here
    for side, o in ((0, 1), (1, -1)):
        block = buf.at[at(-2 * o)]
        arrived(block, sems[0][1].at[2 + side])
        half = lanes_of(block, side)
        for (_, to), there, first in sems:
            send(block, block, ss, there.at[first + side], **to(o))
            send(half, half, ss, there.at[first + 2 + side], **to(2 * o))
        use(block)


def gather_near(here, buf, rs, use):
    at, _ = here
    for side, o in ((0, -1), (1, 1)):
        arrived(buf.at[at(o)], rs.at[side])
        use(buf.at[at(o)])


def gather_far(here, buf, sems, first):
    at, _ = here
    for side, o in ((0, -3), (1, 3)):
        arrived(buf.at[at(o)], sems.at[first + side])
        arrived(lanes_of(buf.at[at(4)], side), sems.at[first + 2 + side])


def kernel(
    sizes, tok_h, gain_h, wup_h, wdn_h, cot_h, out, gt, gg, gup, gdn,
    tok, gain_v, wup, wdn, cotx, scx, normed, inv_col,
    stat_s, stat_r,
    sib_s, sib_r, own, zs, zr, zh, zc, leaning, away_col,
    hid, gp, hx, gpx,
    ys0, yr0, part0, ys1, yr1, part1,
    outv, gtv,
    gg_sum, gg_s, ggx_r, ggy_s, ggy_r,
    ld, sib_ss, sib_rs, stat_ss, stat_rs, z_ss, z_rs, ag_ss, ag_rs, far_rs, rel_ss, rel_rs,
    x_ss, x_rs, q_ss, q_rs, join_ss, join_rs, y_ss, y_rs, yag_ss, yag_rs, ggx_ss, ggx_rs, ggy_ss, ggy_rs,
    known, all_known,
):
    NX, NZ, NY, D = sizes
    T, DS = tok.shape
    TY = T // NY
    FS = wup.shape[1]
    FH, FQ = FS // 2, FS // NX
    NW = 2 * NZ
    x, w, y = lax.axis_index("dp"), lax.axis_index("width"), lax.axis_index("mlp")
    z = lax.div(w, 2)
    c = w - 2 * z
    sibling = 2 * z + 1 - c

    over_z = ring("width", z, lambda position: 2 * position + c)
    across_z = ring("width", z, lambda position: 2 * position + 1 - c)

    def quarter(q):
        first = q * FQ
        h = lax.div(first, FH)
        return h, pl.ds(pl.multiple_of(first - h * FH, FQ), FQ)

    mine = pl.ds(pl.multiple_of(c * FH, FH), FH)
    other = pl.ds(pl.multiple_of(FH - c * FH, FH), FH)

    barrier = pltpu.get_barrier_semaphore()
    over_y = ring("mlp", y)

    def signal(semaphore, **where):
        pl.semaphore_signal(semaphore, inc=1, device_id=where, device_id_type=MESH)

    for o in (2, -2, 1, -1):
        signal(barrier, **over_z[1](o))
        signal(barrier, **over_y[1](o))
    for o in range(1, NX):
        signal(barrier, dp=lax.rem(x + o, NX))
    signal(barrier, width=sibling)

    loads = [
        pltpu.make_async_copy(tok_h, tok, ld.at[0]),
        pltpu.make_async_copy(gain_h, gain_v, ld.at[1]),
        pltpu.make_async_copy(wup_h.at[:, other], wup.at[:, other], ld.at[2]),
        pltpu.make_async_copy(cot_h, cotx.at[0], ld.at[3]),
        pltpu.make_async_copy(wdn_h.at[other], wdn.at[other], ld.at[4]),
        pltpu.make_async_copy(wup_h.at[:, mine], wup.at[:, mine], ld.at[5]),
        pltpu.make_async_copy(wdn_h.at[mine], wdn.at[mine], ld.at[6]),
    ]
    for load in loads:
        load.start()

    loads[0].wait()
    loads[1].wait()
    values = tok[...].astype(F32)
    total = jnp.sum(values, axis=1, keepdims=True)
    shifted = values - total * (1.0 / DS)
    g_all = gain_v[...].reshape(1, DS)
    leaning[0:T] = (shifted * g_all).astype(BF16)
    row = lax.broadcasted_iota(jnp.int32, (TB, DS), 0)
    g_one = g_all.astype(BF16).astype(F32)
    g_two = (g_all - g_one).astype(BF16).astype(F32)
    g_rows = jnp.where(row == 0, g_one, jnp.where(row == 1, g_two, jnp.where(row == 2, g_all - g_one - g_two, 0.0)))
    leaning[T:] = g_rows.astype(BF16)
    loads[2].wait()
    its_half = dot(leaning[...], wup[:, other], 1, 0)
    sib_s[0] = its_half[0:T].astype(BF16)

    loads[3].wait()
    loads[4].wait()
    sib_s[1] = dot(cotx[0], wdn[other, :], 1, 1).astype(BF16)
    pl.semaphore_wait(barrier, 8 + NX)
    for k in range(2):
        send(sib_s.at[k], sib_r.at[k], sib_ss.at[k], sib_rs.at[k], width=sibling)
    signal(known, width=sibling)
    for o in (2, -2):
        signal(known, **over_z[1](o))
        signal(known, **over_y[1](o))

    loads[5].wait()
    my_half = dot(leaning[...], wup[:, mine], 1, 0)
    own[0] = my_half[0:T].reshape(NZ, TB, FH)
    loads[6].wait()
    own[1] = dot(cotx[0], wdn[mine, :], 1, 1).reshape(NZ, TB, FH)

    shifted = tok[...].astype(F32) - total * (1.0 / DS)
    spread = jnp.sum(shifted * shifted, axis=1, keepdims=True)
    total_row = jnp.transpose(jnp.broadcast_to(total, (T, EXTRA)))[0:1]
    spread_row = jnp.transpose(jnp.broadcast_to(spread, (T, EXTRA)))[0:1]
    for h, half in ((c, my_half), (1 - c, its_half)):
        lean = jnp.sum(half[T:], axis=0, keepdims=True)
        stat_s[h, 0:1, 0:T] = total_row
        stat_s[h, 1:2, 0:T] = spread_row
        for j in range(FH // 128):
            stat_s[h, 2 + j : 3 + j, :] = lean[:, j * 128 : (j + 1) * 128]

    def merge(k):
        arrived(sib_r.at[k], sib_rs.at[k])
        both = own[k] + sib_r[k].astype(F32).reshape(NZ, TB, FH)
        own[k] = both
        zs[k] = both.astype(BF16)
        scatter(over_z, zs.at[k], zr.at[k], [zh.at[k, 0], zh.at[k, 1]], z_ss.at[k], z_rs.at[k])

    def merge_pass(k):
        scatter_pass(
            over_z, own.at[k], zr.at[k], [zh.at[k, 0], zh.at[k, 1]], zc.at[k], z_ss.at[k], z_rs.at[k]
        )

    def tell(k, carry):
        peer = lax.rem(w + k, NW)
        send(stat_s.at[lax.rem(peer, 2)], stat_r.at[k - 1], stat_ss, stat_rs, width=peer)
        return carry

    merge(0)
    merge(1)
    pl.semaphore_wait(known, 5)
    signal(all_known, width=sibling)

    right, left = lax.rem(x + 1, NX), lax.rem(x + NX - 1, NX)
    first_rows, last_rows = pl.ds(0, T // 2), pl.ds(T // 2, T // 2)

    def spread_x(k, buf):
        send(buf.at[0], buf.at[1], x_ss.at[k], x_rs.at[k, 0], dp=right)
        send(buf.at[0], buf.at[NX - 1], x_ss.at[k], x_rs.at[k, 1], dp=left)

    def pass_x(k, buf):
        arrived(buf.at[1], x_rs.at[k, 0])
        send(buf.at[1, first_rows], buf.at[2, first_rows], x_ss.at[k], x_rs.at[k, 2], dp=right)
        arrived(buf.at[NX - 1], x_rs.at[k, 1])
        send(buf.at[NX - 1, last_rows], buf.at[2, last_rows], x_ss.at[k], x_rs.at[k, 3], dp=left)

    def end_x(k, buf):
        arrived(buf.at[2, first_rows], x_rs.at[k, 2])
        arrived(buf.at[2, last_rows], x_rs.at[k, 3])

    spread_x(0, cotx)
    pl.semaphore_wait(all_known, 1)
    lax.fori_loop(1, NW, tell, 0)
    merge_pass(0)
    merge_pass(1)

    arrived(stat_r, stat_rs)
    its = stat_r[...]
    my_stat = stat_s[c]
    sums, spreads = its[:, 0, :], its[:, 1, :]
    mean = (jnp.sum(sums, axis=0, keepdims=True) + my_stat[0:1]) * (1.0 / D)
    away, my_away = sums * (1.0 / DS) - mean, my_stat[0:1] * (1.0 / DS) - mean
    variance = (
        jnp.sum(spreads + DS * away * away, axis=0, keepdims=True) + my_stat[1:2] + DS * my_away * my_away
    ) * (1.0 / D)
    inv_std = lax.rsqrt(variance + 1e-06)
    mean_col = jnp.transpose(jnp.broadcast_to(mean[:, 0:T], (EXTRA, T)))
    std_col = jnp.transpose(jnp.broadcast_to(inv_std[:, 0:T], (EXTRA, T)))
    inv_col[...] = std_col
    aways = jnp.concatenate([away[:, 0:T], my_away[:, 0:T], jnp.zeros((EXTRA - NW, T), F32)], axis=0)
    away_col[...] = jnp.transpose(aways)
    token_rows = pl.ds(pl.multiple_of(z * TB, TB), TB)
    my_aways = away_col[token_rows, :]
    leans, shift = [], []
    for j in range(FH // 128):
        piece = [its[s, 2 + j : 3 + j, :] for s in range(NW - 1)] + [my_stat[2 + j : 3 + j, :]]
        leans.append(functools.reduce(jnp.add, piece))
        shift.append(functools.reduce(jnp.add, [my_aways[:, s : s + 1] * piece[s] for s in range(NW)]))
    lean_row = jnp.concatenate(leans, axis=1)
    shift = jnp.concatenate(shift, axis=1)

    def hand_over(k):
        return lambda block: send(block, block, rel_ss.at[k], rel_rs.at[k], width=sibling)

    pre_act = (scatter_sum(over_z, own.at[0], zr.at[0], z_rs.at[0]) + shift) * inv_col[token_rows, 0:1]
    below = 0.5 * (1.0 + lax.erf(pre_act * inv_root_two))
    hid[c, z] = (pre_act * below).astype(BF16)
    units, grads = hid.at[c], gp.at[c]
    gather(over_z, units, ag_ss.at[0], ag_rs.at[0])
    hand_over(0)(hid.at[c, z])
    slope = below + pre_act * jnp.exp(-0.5 * pre_act * pre_act) * inv_root_two_pi
    grad_hidden = scatter_sum(over_z, own.at[1], zr.at[1], z_rs.at[1])
    grad_pre = (grad_hidden * slope).astype(BF16)
    wide = grad_pre.astype(F32)
    gp[c, z, :, 0:FH] = grad_pre
    gp[c, z, :, FH:] = pack(
        jnp.sum(wide * lean_row, axis=1, keepdims=True), jnp.sum(wide * pre_act, axis=1, keepdims=True)
    )
    gather(over_z, grads, ag_ss.at[1], ag_rs.at[1])
    hand_over(1)(gp.at[c, z])

    for j in range(DS // 128):
        cols = slice(j * 128, (j + 1) * 128)
        normal = (tok[:, cols].astype(F32) - mean_col) * std_col
        normed[:, cols] = normal
        scx[0, :, cols] = (normal * g_all[:, cols]).astype(BF16)
    spread_x(1, scx)

    gather_pass(over_z, units, ag_ss.at[0], [(over_z, ag_rs.at[0], 4)], hand_over(0))
    gather_near(over_z, units, ag_rs.at[0], hand_over(0))
    gather_pass(
        over_z, grads, ag_ss.at[1], [(over_z, ag_rs.at[1], 4), (across_z, far_rs, 0)], hand_over(1)
    )
    gather_near(over_z, grads, ag_rs.at[1], hand_over(1))

    block_of, _ = over_z
    near, far = (0, 1, -1, 2, -2), (3, -3, 4)

    half_ring = NY // 2
    slot = lax.rem(y, half_ring)

    def next_to(o):
        return lax.rem(y + o % NY, NY)

    def own_sums(k, part, got, result):
        arrived(got, y_rs.at[k])
        for side in range(2):
            block = lax.rem(y + side * half_ring, NY)
            summed = part[block] + jnp.sum(got[side].astype(F32), axis=0)
            result[lax.div(block, half_ring), lax.rem(block, half_ring)] = summed.astype(BF16)

    def from_owners(k, buf):
        both = buf.at[:, slot]
        for side, o in ((0, 1), (1, -1)):
            one = buf.at[side, slot]
            send(one, one, yag_ss.at[k], yag_rs.at[k, 2 + side], mlp=next_to(2 * o))
            send(both, both, yag_ss.at[k], yag_rs.at[k, side], mlp=next_to(o))

    def from_owners_end(k, buf):
        for side, o in ((0, -1), (1, 1)):
            arrived(buf.at[:, lax.rem(next_to(o), half_ring)], yag_rs.at[k, side])
            arrived(buf.at[side, lax.rem(next_to(2 * o), half_ring)], yag_rs.at[k, 2 + side])

    def rows_of(buf, h, blocks, lanes):
        return jnp.concatenate([buf[h, block_of(o), :, lanes] for o in blocks], axis=0)

    def to_owners(k, blocks, terms, part, sent, got):
        for i, o in enumerate(blocks):
            block = block_of(o)
            part[block] = terms[i * TB : (i + 1) * TB]
            sent[block] = terms[i * TB : (i + 1) * TB].astype(BF16)
            for side in range(2):
                owner = lax.rem(block + side * half_ring, NY)

                @pl.when(owner != y)
                def _():
                    place_there = got.at[side, lax.rem(owner - y + NY - 1, NY)]
                    send(sent.at[block], place_there, y_ss.at[k], y_rs.at[k], mlp=owner)

    def output_terms(blocks):
        units = slice(0, FH)
        term = dot(rows_of(hid, 0, blocks, units), wdn[0:FH, :], 1, 0)
        term = term + dot(rows_of(hid, 1, blocks, units), wdn[FH:, :], 1, 0)
        to_owners(0, blocks, term, part0, ys0, yr0)

    def gradient_terms(blocks):
        units, beside = slice(0, FH), slice(FH, FH + EXTRA)
        term = dot(rows_of(gp, 0, blocks, units), wup[:, 0:FH], 1, 1)
        term = term + dot(rows_of(gp, 1, blocks, units), wup[:, FH:], 1, 1)
        side = rows_of(gp, 0, blocks, beside).astype(F32) + rows_of(gp, 1, blocks, beside).astype(F32)
        first, second = unpack(side)
        tokens = [pl.ds(pl.multiple_of(block_of(o) * TB, TB), TB) for o in blocks]
        normal = jnp.concatenate([normed[rows, :] for rows in tokens], axis=0)
        scale = jnp.concatenate([inv_col[rows, 0:1] for rows in tokens], axis=0)
        corrected = scale * (
            term * gain_v[...].reshape(1, DS) - first * (1.0 / D) - normal * (second * (1.0 / D))
        )
        to_owners(1, blocks, corrected, part1, ys1, yr1)
        return jnp.sum((term * normal).reshape(len(blocks) * TB // 8, 8, DS), axis=0)

    my_blocks = pl.ds(pl.multiple_of(c * (NZ // 2), NZ // 2), NZ // 2)
    its_blocks = pl.ds(pl.multiple_of((1 - c) * (NZ // 2), NZ // 2), NZ // 2)

    def share(k, buf, dst):
        def one(o, carry):
            peer = lax.rem(x + o, NX)
            h, lanes = quarter(peer)
            send(buf.at[h, my_blocks, :, lanes], dst.at[o, my_blocks], q_ss.at[k], q_rs.at[k], dp=peer)
            return carry
        lax.fori_loop(1, NX, one, 0)
        h, lanes = quarter(x)
        dst[0] = buf[h, :, :, lanes]

    def join(k, dst):
        halves = dst.at[pl.ds(1, NX - 1), my_blocks]
        arrived(halves, q_rs.at[k])
        send(halves, halves, join_ss.at[k], join_rs.at[k], width=sibling)

    arrived(hid.at[1 - c, pl.ds(0, 5)], rel_rs.at[0])
    output_terms(near)
    gather_far(over_z, units, ag_rs.at[0], 4)
    for o in far:
        block = hid.at[c, block_of(o)]
        send(block, block, rel_ss.at[0], rel_rs.at[2], width=sibling)
    arrived(gp.at[1 - c, pl.ds(0, 5)], rel_rs.at[1])
    gg_sum[...] = gradient_terms(near)
    pass_x(0, cotx)
    pass_x(1, scx)
    arrived(hid.at[1 - c, pl.ds(0, 3)], rel_rs.at[2])
    output_terms(far)
    share(0, hid, hx)
    gather_far(over_z, grads, ag_rs.at[1], 4)
    gather_far(over_z, gp.at[1 - c], far_rs, 0)
    share(1, gp, gpx)
    gains = gg_sum[...] + gradient_terms(far)
    gains = jnp.sum(gains, axis=0, keepdims=True)
    rows = [gains[:, j * 128 : (j + 1) * 128] for j in range(DS // 128)]
    gg_s[...] = jnp.concatenate(rows + [jnp.zeros((8 - len(rows), 128), F32)], axis=0)

    def gain_x(o, carry):
        send(gg_s, ggx_r.at[o - 1], ggx_ss, ggx_rs, dp=lax.rem(x + o, NX))
        return carry
    lax.fori_loop(1, NX, gain_x, 0)
    join(0, hx)

    own_sums(0, part0, yr0, outv)
    from_owners(0, outv)

    arrived(ggx_r, ggx_rs)
    ggy_s[...] = gg_s[...] + jnp.sum(ggx_r[...], axis=0)

    def gain_y(o, carry):
        send(ggy_s, ggy_r.at[o - 1], ggy_ss, ggy_rs, mlp=lax.rem(y + o, NY))
        return carry
    lax.fori_loop(1, NY, gain_y, 0)

    join(1, gpx)

    end_x(0, cotx)
    arrived(hx.at[pl.ds(1, NX - 1), its_blocks], join_rs.at[0])
    gdn[...] = dot(hx[...].reshape(NX * T, FQ), cotx[...].reshape(NX * T, DS), 0, 0)
    own_sums(1, part1, yr1, gtv)
    from_owners(1, gtv)
    end_x(1, scx)
    arrived(gpx.at[pl.ds(1, NX - 1), its_blocks], join_rs.at[1])
    product = dot(scx[...].reshape(NX * T, DS), gpx[...].reshape(NX * T, FQ), 0, 0)
    pieces = FQ // 128
    for j in range(pieces):
        gup[pl.ds(j, DS, stride=pieces), :] = product[:, j * 128 : (j + 1) * 128]
    for k in range(2):
        arrived(sib_s.at[k], sib_ss.at[k])
        arrived(zs.at[k, pl.ds(0, NZ - 1)], z_ss.at[k])
    arrived(stat_r, stat_ss)
    arrived(hid.at[0, pl.ds(0, NZ - 1)], ag_ss.at[0])
    arrived(hid.at[0], rel_ss.at[0])
    arrived(gp.at[:, pl.ds(0, 5)], ag_ss.at[1])
    arrived(gp.at[0, pl.ds(0, 5)], rel_ss.at[1])
    for k, buf in enumerate((cotx, scx)):
        arrived(buf.at[pl.ds(0, NX - 1)], x_ss.at[k])
    for k, buf in enumerate((hx, gpx)):
        arrived(buf.at[pl.ds(1, NX - 1), my_blocks], q_ss.at[k])
        arrived(buf.at[pl.ds(1, NX - 1), my_blocks], join_ss.at[k])
    arrived(yr0, y_ss.at[0])
    arrived(yr1, y_ss.at[1])
    arrived(outv.at[:, pl.ds(0, 3)], yag_ss.at[0])
    arrived(ggx_r, ggx_ss)

    from_owners_end(0, outv)
    out[...] = outv[...].reshape(T, DS)
    from_owners_end(1, gtv)
    gt[...] = gtv[...].reshape(T, DS)
    arrived(ggy_r, ggy_rs)
    gains = ggy_s[...] + jnp.sum(ggy_r[...], axis=0)
    gg[...] = jnp.concatenate([gains[j : j + 1] for j in range(DS // 128)], axis=1).reshape(DS)
    arrived(gtv.at[:, pl.ds(0, 3)], yag_ss.at[1])
    arrived(ggy_r, ggy_ss)


def place(*refs):
    made, given, sems = refs[0:5], refs[5:10], refs[10]
    copies = [pltpu.make_async_copy(src, dst, sems.at[k]) for k, (src, dst) in enumerate(zip(made, given))]
    for copy in copies:
        copy.start()
    for copy in copies:
        copy.wait()


def solution(mesh):
    NX, NZ, NY = mesh.shape["dp"], mesh.shape["width"] // 2, mesh.shape["mlp"]

    def shards(tokens, gain, up_weight, down_weight, cotangent):
        T, DS = tokens.shape
        FS = up_weight.shape[1]
        FH, FQ = FS // 2, FS // NX
        vmem, dma = pltpu.VMEM, pltpu.SemaphoreType.DMA
        results = (
            jax.ShapeDtypeStruct((T, DS), BF16),
            jax.ShapeDtypeStruct((T, DS), BF16),
            jax.ShapeDtypeStruct((DS,), F32),
            jax.ShapeDtypeStruct((DS * FQ // 128, 128), F32),
            jax.ShapeDtypeStruct((FQ, DS), F32),
        )
        call = pl.pallas_call(
            functools.partial(kernel, (NX, NZ, NY, DS * 2 * NZ)),
            out_shape=results,
            in_specs=[pl.BlockSpec(memory_space=pltpu.HBM)] * 5,
            out_specs=[pl.BlockSpec(memory_space=pltpu.VMEM)] * 5,
            scratch_shapes=[
                vmem((T, DS), BF16), vmem((DS,), F32), vmem((DS, FS), BF16), vmem((FS, DS), BF16),
                vmem((NX, T, DS), BF16), vmem((NX, T, DS), BF16), vmem((T, DS), F32), vmem((T, EXTRA), F32),
                vmem((2, 8, 128), F32), vmem((2 * NZ - 1, 8, 128), F32),
                vmem((2, T, FH), BF16), vmem((2, T, FH), BF16), vmem((2, NZ, TB, FH), F32),
                vmem((2, NZ, TB, FH), BF16), vmem((2, 6, TB, FH), BF16),
                vmem((2, 2, TB, FH // 2), BF16), vmem((2, 2, TB, FH), BF16),
                vmem((T + TB, DS), BF16), vmem((T, EXTRA), F32),
                vmem((2, NZ, TB, FH), BF16), vmem((2, NZ, TB, FH + EXTRA), BF16),
                vmem((NX, NZ, TB, FQ), BF16), vmem((NX, NZ, TB, FQ), BF16),
                *(
                    shape
                    for _ in range(2)
                    for shape in (
                        vmem((NY, TB, DS), BF16), vmem((2, NY - 1, TB, DS), BF16), vmem((NY, TB, DS), F32),
                    )
                ),
                vmem((2, NY // 2, TB, DS), BF16), vmem((2, NY // 2, TB, DS), BF16),
                vmem((8, DS), F32), vmem((8, 128), F32), vmem((NX - 1, 8, 128), F32),
                vmem((8, 128), F32), vmem((NY - 1, 8, 128), F32),
                dma((7,)), dma((2,)), dma((2,)), dma, dma, dma((2,)), dma((2, 8)),
                dma((2,)), dma((2, 8)), dma((4,)), dma((2,)), dma((3,)),
                dma((2,)), dma((2, 4)), dma((2,)), dma((2,)), dma((2,)), dma((2,)),
                dma((2,)), dma((2,)), dma((2,)), dma((2, 4)), dma, dma, dma, dma,
                pltpu.SemaphoreType.REGULAR, pltpu.SemaphoreType.REGULAR,
            ],
            compiler_params=pltpu.CompilerParams(
                collective_id=0, has_side_effects=True, vmem_limit_bytes=48 * 1024 * 1024
            ),
            cost_estimate=pl.CostEstimate(
                flops=12 * T * DS * FS, bytes_accessed=4 * DS * FS + 8 * DS * FQ, transcendentals=2 * TB * FH
            ),
        )
        put = pl.pallas_call(
            place,
            out_shape=results,
            in_specs=[pl.BlockSpec(memory_space=pltpu.VMEM)] * 5,
            out_specs=[pl.BlockSpec(memory_space=pltpu.HBM)] * 5,
            scratch_shapes=[dma((5,))],
            compiler_params=pltpu.CompilerParams(vmem_limit_bytes=4 * 1024 * 1024),
        )
        output, grad_tokens, grad_gain, grad_up, grad_down = put(
            *call(*(pltpu.with_memory_space_constraint(a, pltpu.HBM) for a in (tokens, gain, up_weight, down_weight, cotangent)))
        )
        return output, grad_tokens, grad_gain, grad_up.reshape(DS, 1, FQ), grad_down[None, :, :]

    placed = (P("dp", "width"), P("width"), P("width", "mlp"), P("mlp", "width"), P("dp", "width"))
    return jax.shard_map(
        shards,
        mesh=mesh,
        in_specs=placed,
        out_specs=(
            P("dp", "width"),
            P("dp", "width"),
            P("width"),
            P("width", "mlp", "dp"),
            P("mlp", "dp", "width"),
        ),
        check_vma=False,
    )
```
